128 devices in a mesh: dp: 4 (over y), expert: 8 (over x, z_lo), tensor: 4 (over z_hi, core).
Axes of the slice: x: 4, y: 4, z: 4 (z_hi: 2, z_lo: 2; z = z_hi * 2 + z_lo), core: 2. Of those that a mesh axis runs over, the one named last changes fastest.
Arguments:
- tokens: bfloat16 [4, 1024, 2048], P('dp', 'expert'), may hold values from -6 to 6
- cotangent: bfloat16 [4, 1024, 2048], P('dp', 'expert'), may hold values from -6 to 6
- doc_lengths: int32 [4, 8], P('dp'), may hold values from 1 to 897, as said below
- att_routes: int32 [4, 1024, 2], P('dp', 'expert'), may hold values from 0 to 7, all different within a row; in each aligned block of 128 rows (0 to 127, 128 to 255, ..., all dimensions but the last counted through in order) at most 40 rows name the same one
- att_gates: float32 [4, 1024, 2], P('dp', 'expert'), may hold values from 0.25 to 0.75
- ffn_routes: int32 [4, 1024, 2], P('dp', 'expert'), may hold values from 0 to 7, all different within a row; in each aligned block of 128 rows (0 to 127, 128 to 255, ..., all dimensions but the last counted through in order) at most 40 rows name the same one
- ffn_gates: float32 [4, 1024, 2], P('dp', 'expert'), may hold values from 0.25 to 0.75
- kv_weight: bfloat16 [2048, 2, 2048], P(('dp', 'expert'), None, 'tensor'), may hold values from -0.125 to 0.125
- query_weight: bfloat16 [8, 2048, 2048], P(None, ('dp', 'expert'), 'tensor'), may hold values from -0.125 to 0.125
- out_weight: bfloat16 [8, 2048, 2048], P(None, 'tensor', ('dp', 'expert')), may hold values from -0.75 to 0.75
- attn_gain: bfloat16 [2048], P(('dp', 'expert')), may hold values from 0.5 to 1.5
- ffn_gain: bfloat16 [2048], P(('dp', 'expert')), may hold values from 0.5 to 1.5
- gate_weight: bfloat16 [8, 2048, 5632], P('expert', 'dp', 'tensor'), may hold values from -0.125 to 0.125
- up_weight: bfloat16 [8, 2048, 5632], P('expert', 'dp', 'tensor'), may hold values from -0.125 to 0.125
- down_weight: bfloat16 [8, 5632, 2048], P('expert', 'tensor', 'dp'), may hold values from -0.078125 to 0.078125
Outputs:
- output: bfloat16 [4, 1024, 2048], P('dp', 'expert')
- input_grad: float32 [4, 1024, 2048], P('dp', 'expert')
- kv_weight_grad: float32 [2048, 2, 2048], P(('dp', 'expert'), None, 'tensor')
- query_weight_grad: float32 [8, 2048, 2048], P(None, ('dp', 'expert'), 'tensor')
- out_weight_grad: float32 [8, 2048, 2048], P(None, 'tensor', ('dp', 'expert'))
- attn_gain_grad: float32 [2048], P(('dp', 'expert'))
- ffn_gain_grad: float32 [2048], P(('dp', 'expert'))
- gate_weight_grad: float32 [8, 2048, 5632], P('expert', 'dp', 'tensor')
- up_weight_grad: float32 [8, 2048, 5632], P('expert', 'dp', 'tensor')
- down_weight_grad: float32 [8, 5632, 2048], P('expert', 'tensor', 'dp')
The draws below stay inside these ranges and needn't reach their ends.
Inputs may be any that keep to these rules, and one draw needn't show every extreme that they name: `doc_lengths`: the 8 document lengths of a sequence are positive and sum to 1024; one of them is exactly 1024 - 1024 // 8 + 1. `att_routes`: each token names 2 different maps; in each aligned block of 128 positions of a sequence no map is named by more than 40 tokens, a bound that some block reaches. `ffn_routes`: each token names 2 different experts; in each aligned block of 128 positions of a sequence no expert is named by more than 40 tokens, a bound that some block reaches.
All inputs are finite; a program needn't handle non-finite values.
Results may differ from the reference program's by a relative error of at most 0.028.
Values may be sent and summed in bfloat16 or wider, within the bound.
A program may use at most 256 MiB of HBM per device.

```python
import math
import jax
import jax.numpy as jnp
import numpy as np
from jax import lax

D = 2048
HD = 128
KV = 16
ATT_EXP = 8
TOPK = 2
FF = 5632
NDOCS = 8
SEQ_LEN = 1024
SEQS = 1
EXPERTS = 8
GROUP = 128
CAP = 40
ACAP = 40
SEQS_ALL = 4
N_DP = 4
N_EXPERT = 8


def draw_doc_lengths(key, part):
    key = jax.random.fold_in(key, 7)
    first_key, second_key = jax.random.split(key)
    seq_total = SEQS * N_DP
    group_len = SEQ_LEN // N_EXPERT
    short_total = group_len - 1
    spare = short_total - (NDOCS - 1)
    raw_draw = jax.random.randint(first_key, (seq_total, NDOCS - 1), 1, 16)
    raw_draw = raw_draw * raw_draw
    raw_sum = jnp.sum(raw_draw, axis=1, keepdims=True)
    short_docs = 1 + raw_draw * spare // raw_sum
    leftover = short_total - jnp.sum(short_docs, axis=1, keepdims=True)
    first_col = (jnp.arange(NDOCS - 1, dtype=jnp.int32) == 0).astype(jnp.int32)[None, :]
    short_docs = short_docs + leftover * first_col
    longest = jnp.full((seq_total, 1), SEQ_LEN - short_total, jnp.int32)
    long_slot = jax.random.randint(second_key, (seq_total, 1), 0, NDOCS)
    column = jnp.arange(NDOCS, dtype=jnp.int32)[None, :]
    blank = jnp.zeros((seq_total, 1), jnp.int32)
    before_long = jnp.concatenate([short_docs, blank], 1)
    after_long = jnp.concatenate([blank, short_docs], 1)
    result = jnp.where(column < long_slot, before_long, jnp.where(column == long_slot, longest, after_long))
    return result.astype(jnp.int32)


def steps_of(key, dims, cuts, low, top_value):
    def one(axis_at, shards_of):
        heights = jax.random.uniform(jax.random.fold_in(jax.random.fold_in(key, 6), axis_at), (shards_of,), jnp.float32, low / len(cuts), top_value / len(cuts))
        return jnp.repeat(jnp.exp(heights), dims[axis_at] // shards_of).reshape((-1,) + (1,) * (len(dims) - axis_at - 1))

    loudness = one(*cuts[0])
    for cut in cuts[1:]:
        loudness = loudness * one(*cut)
    return loudness


def routed_block(rng, own, number, rows, amount, top, reach, lean):
    ranking = jax.random.permutation(rng, amount)
    heavy_load, common = portions_of(amount, rows * top, reach, lean, True), portions_of(amount, rows * top, reach, lean, False)
    places = jnp.arange(amount)

    def named(sizes, rotation):
        used = int((sizes > 0).sum())
        fixed = max(1, used // 4)
        shifted = fixed + (places - fixed + rotation * (used - fixed)) % max(1, amount - fixed)
        return jnp.zeros((amount,), jnp.int32).at[ranking[jnp.where(places < fixed, places, shifted)]].set(jnp.asarray(sizes, jnp.int32))

    sizes = jnp.where(number % 4 == 0, named(heavy_load, number // 4), named(common, number - number // 4 - 1))
    mixed = jax.random.permutation(jax.random.fold_in(own, 3), amount)
    source_of, taker = mixed[0:amount // 2 * 2:2], mixed[1:amount // 2 * 2:2]
    slack = jnp.minimum(sizes[source_of] - 1, reach - sizes[taker]) // 2
    slack = jnp.where((source_of == ranking[0]) | (taker == ranking[0]) | (sizes[taker] == 0), 0, jnp.maximum(slack, 0))
    shifted = jax.random.randint(jax.random.fold_in(own, 4), (amount // 2,), 0, 1 << 20) % (slack + 1)
    sizes = sizes.at[source_of].add(-shifted).at[taker].add(shifted)
    members = jnp.searchsorted(jnp.cumsum(sizes), jnp.arange(rows * top), side="right").astype(jnp.int32)
    grid = members.reshape(top, rows).T
    grid = grid[jax.random.permutation(jax.random.fold_in(own, 1), rows)]
    rotation = jax.random.randint(jax.random.fold_in(own, 2), (rows, 1), 0, top)
    return jnp.take_along_axis(grid, (jnp.arange(top)[None, :] + rotation) % top, axis=1)


def portions_of(count, total, bound, skew, full):
    weights = [(1 << 20) // math.isqrt(grade ** skew) + 1 for grade in range(1, count + 1)]
    largest = bound if full else min(bound, max(-(-total // count), total * weights[0] // sum(weights)))
    least = 1 if total - largest >= count - 1 else 0
    holding, surplus = [largest] + [least] * (count - 1), total - largest - least * (count - 1)
    while surplus > 0:
        movable = [i for i in range(1, count) if holding[i] < largest] or [i for i in range(1, count) if holding[i] < bound]
        pool, left = sum([weights[i] for i in movable]), surplus
        for i in movable:
            more = min(bound - holding[i], max(1, left * weights[i] // pool), surplus)
            holding[i] = holding[i] + more
            surplus = surplus - more
    return np.array(holding)


def scatter_about(stream_key, shape, width, most, cuts=(), held_as=jnp.bfloat16):
    gain = steps_of(stream_key, shape, cuts, -0.22, 0.18) if cuts else 1.0
    drawn = jax.random.normal(stream_key, shape, jnp.float32) * width * gain
    return jnp.minimum(jnp.maximum(drawn, -most), most).astype(held_as)


def setup_inputs(seed: int = 0) -> dict:
    streams_of = jax.random.split(jax.random.key(seed), 16)
    tokens = scatter_about(streams_of[0], (SEQS_ALL, SEQ_LEN, D), 1.0, 6.0, ((0, 4), (1, 8)))
    cotangent = scatter_about(streams_of[1], (SEQS_ALL, SEQ_LEN, D), 1.0, 6.0, ((0, 4), (1, 8)))
    doc_lengths = draw_doc_lengths(jax.random.fold_in(streams_of[15], 71), 0)
    att_routes_keys = jax.random.split(jax.random.fold_in(streams_of[3], 1), SEQS_ALL * SEQ_LEN // GROUP)
    att_routes_turns = jax.random.permutation(jax.random.fold_in(streams_of[3], 3), SEQS_ALL * SEQ_LEN // GROUP)
    att_routes = jax.vmap(lambda own, number: routed_block(jax.random.fold_in(streams_of[3], 2), own, number, GROUP, ATT_EXP, TOPK, ACAP, 1))(att_routes_keys, att_routes_turns).reshape((SEQS_ALL, SEQ_LEN, TOPK))
    att_gates = jnp.clip(0.25 + 0.5 * jax.random.uniform(streams_of[4], (SEQS_ALL, SEQ_LEN, TOPK), jnp.float32) ** steps_of(streams_of[4], (SEQS_ALL, SEQ_LEN, TOPK), ((0, 4), (1, 8)), -0.2, 0.2), 0.25, 0.75)
    ffn_routes_keys = jax.random.split(jax.random.fold_in(streams_of[5], 1), SEQS_ALL * SEQ_LEN // GROUP)
    ffn_routes_turns = jax.random.permutation(jax.random.fold_in(streams_of[5], 3), SEQS_ALL * SEQ_LEN // GROUP)
    ffn_routes = jax.vmap(lambda own, number: routed_block(jax.random.fold_in(streams_of[5], 2), own, number, GROUP, EXPERTS, TOPK, CAP, 2))(ffn_routes_keys, ffn_routes_turns).reshape((SEQS_ALL, SEQ_LEN, TOPK))
    ffn_gates = jnp.clip(0.25 + 0.5 * jax.random.uniform(streams_of[6], (SEQS_ALL, SEQ_LEN, TOPK), jnp.float32) ** steps_of(streams_of[6], (SEQS_ALL, SEQ_LEN, TOPK), ((0, 4), (1, 8)), -0.2, 0.2), 0.25, 0.75)
    kv_weight = scatter_about(streams_of[7], (D, 2, KV * HD), D ** -0.5, 0.125, ((0, 32), (2, 4)))
    query_weight = scatter_about(streams_of[8], (ATT_EXP, D, KV * HD), D ** -0.5, 0.125, ((1, 32), (2, 4)))
    out_weight = scatter_about(streams_of[9], (ATT_EXP, KV * HD, D), 64 ** -0.5, 0.75, ((1, 4), (2, 32)))
    attn_gain = jnp.clip(1.0 + 0.1 * jax.random.normal(streams_of[10], (D,), jnp.float32), 0.5, 1.5).astype(jnp.bfloat16)
    ffn_gain = jnp.clip(1.0 + 0.1 * jax.random.normal(streams_of[11], (D,), jnp.float32), 0.5, 1.5).astype(jnp.bfloat16)
    gate_weight = scatter_about(streams_of[12], (EXPERTS, D, FF), D ** -0.5, 0.125, ((0, 8), (1, 4), (2, 4)))
    up_weight = scatter_about(streams_of[13], (EXPERTS, D, FF), D ** -0.5, 0.125, ((0, 8), (1, 4), (2, 4)))
    down_weight = scatter_about(streams_of[14], (EXPERTS, FF, D), FF ** -0.5, 0.078125, ((0, 8), (1, 4), (2, 4)))
    return {"tokens": tokens, "cotangent": cotangent, "doc_lengths": doc_lengths, "att_routes": att_routes, "att_gates": att_gates, "ffn_routes": ffn_routes, "ffn_gates": ffn_gates, "kv_weight": kv_weight, "query_weight": query_weight, "out_weight": out_weight, "attn_gain": attn_gain, "ffn_gain": ffn_gain, "gate_weight": gate_weight, "up_weight": up_weight, "down_weight": down_weight}


HIGHEST = lax.Precision.HIGHEST
EPSILON = 1e-06

@jax.custom_vjp
def low(v):
    return lax.optimization_barrier(v.astype(jnp.bfloat16)).astype(jnp.float32)

@jax.custom_vjp
def low_back(v):
    return v

def low_keep(v):
    return (low(v), None)

def low_pass(kept, grad):
    return (grad,)

def back_keep(v):
    return (v, None)

def back_low(kept, grad):
    return (low(grad),)
low.defvjp(low_keep, low_pass)
low_back.defvjp(back_keep, back_low)

def rope_tables(positions):
    half_dim = HD // 2
    freqs = 10000.0 ** (-(jnp.arange(half_dim).astype(jnp.float32) * 2.0 / HD))
    angles = positions[:, None] * freqs[None, :]
    return (jnp.cos(angles), jnp.sin(angles))

def rotate(values, cos_tab, sin_tab):
    half_dim = values.shape[-1] // 2
    first_half = values[..., :half_dim]
    second_half = values[..., half_dim:]
    return jnp.concatenate([first_half * cos_tab - second_half * sin_tab, second_half * cos_tab + first_half * sin_tab], -1)

def segment_ids(lengths, length_all):
    ends = jnp.cumsum(lengths, -1, dtype=jnp.int32)
    places = jnp.arange(length_all, dtype=jnp.int32)
    return lax.optimization_barrier(jnp.sum((ends[..., None, :] <= places[:, None]).astype(jnp.int32), -1)).astype(jnp.int32)

def slot_maps(routes, expert_count, capacity):
    blocks, block_len, choices = routes.shape
    row_len = block_len * choices
    flat_routes = routes.reshape(blocks, row_len)
    onehot = (flat_routes[:, :, None] == jnp.arange(expert_count, dtype=jnp.int32)[None, None, :]).astype(jnp.int32)
    position = lax.optimization_barrier(jnp.sum((jnp.cumsum(onehot, axis=1, dtype=jnp.int32) - 1) * onehot, -1)).astype(jnp.int32)
    block_base = (jnp.arange(blocks, dtype=jnp.int32) * capacity)[:, None]
    flat_slot = (flat_routes * (blocks * capacity) + block_base + position).reshape(-1).astype(jnp.int32)
    source = jnp.full((expert_count * blocks * capacity,), blocks * row_len, jnp.int32)
    source = source.at[flat_slot].set(jnp.arange(blocks * row_len, dtype=jnp.int32))
    return (flat_slot, source)

def take_rows(rows, source):
    padded = jnp.concatenate([rows, jnp.zeros((1,) + rows.shape[1:], rows.dtype)], 0)
    return padded[source]

def layer(params, inputs, lengths, att_route, att_gate, ffn_route, ffn_gate):
    kv_full, query_full, out_full, gain_one, gain_two, gate_full, up_full, down_full = params
    length = inputs.shape[0]
    row_count = length * TOPK
    inv_one = lax.rsqrt(lax.optimization_barrier(jnp.mean(inputs * inputs, -1, keepdims=True)) + EPSILON)
    normed = low(inputs * inv_one * gain_one)
    projected = jnp.einsum('td,dcf->tcf', normed, kv_full, precision=HIGHEST)
    cos_tab, sin_tab = rope_tables(jnp.arange(length).astype(jnp.float32))
    key_rows = low_back(projected[:, 0]).reshape(length, KV, HD)
    key_rows = low(rotate(key_rows, cos_tab[:, None], sin_tab[:, None]))
    value_rows = low(low_back(projected[:, 1])).reshape(length, KV, HD)
    att_slot, att_source = slot_maps(att_route[None], ATT_EXP, N_EXPERT * ACAP)
    att_token = jnp.where(att_source < row_count, att_source // TOPK, length)
    x_buffer = take_rows(normed, att_token).reshape(ATT_EXP, -1, D)
    q_buffer = jnp.einsum('acd,adh->ach', x_buffer, query_full, precision=HIGHEST)
    queries = low_back(q_buffer.reshape(-1, KV * HD)[att_slot]).reshape(length, TOPK, KV, HD)
    queries = low(rotate(queries, cos_tab[:, None, None], sin_tab[:, None, None]))
    scores = low_back(jnp.einsum('tjhd,khd->hjtk', queries, key_rows, precision=HIGHEST) * HD ** (-0.5))
    segments = segment_ids(lengths, length)
    places = jnp.arange(length, dtype=jnp.int32)
    visible = (segments[:, None] == segments[None, :]) & (places[None, :] <= places[:, None])
    scores = jnp.where(visible, scores, -1e+30)
    weights = low(jax.nn.softmax(scores, axis=-1))
    mixed = jnp.einsum('hjtk,khd->tjhd', weights, value_rows, precision=HIGHEST)
    mixed = low_back(low(mixed)).reshape(row_count, KV * HD)
    o_buffer = take_rows(mixed, att_source).reshape(ATT_EXP, -1, KV * HD)
    z_buffer = jnp.einsum('ach,ahd->acd', o_buffer, out_full, precision=HIGHEST)
    branch = low_back(z_buffer.reshape(-1, D)[att_slot]).reshape(length, TOPK, D)
    state = inputs + lax.optimization_barrier(jnp.sum(branch * att_gate[:, :, None], 1))
    inv_two = lax.rsqrt(lax.optimization_barrier(jnp.mean(state * state, -1, keepdims=True)) + EPSILON)
    normed_two = low(state * inv_two * gain_two)
    ffn_slot, ffn_source = slot_maps(ffn_route[None], EXPERTS, N_EXPERT * CAP)
    ffn_token = jnp.where(ffn_source < row_count, ffn_source // TOPK, length)
    expert_in = take_rows(normed_two, ffn_token).reshape(EXPERTS, -1, D)
    gate_act = low_back(jnp.einsum('ecd,edf->ecf', expert_in, gate_full, precision=HIGHEST))
    up_act = low_back(jnp.einsum('ecd,edf->ecf', expert_in, up_full, precision=HIGHEST))
    hidden = low(jax.nn.silu(gate_act) * up_act)
    expert_out = jnp.einsum('ecf,efd->ecd', hidden, down_full, precision=HIGHEST)
    ffn_rows = low_back(expert_out.reshape(-1, D)[ffn_slot]).reshape(length, TOPK, D)
    return state + lax.optimization_barrier(jnp.sum(ffn_rows * ffn_gate[:, :, None], 1))

def reference(tokens, cotangent, doc_lengths, att_routes, att_gates, ffn_routes, ffn_gates, kv_weight, query_weight, out_weight, attn_gain, ffn_gain, gate_weight, up_weight, down_weight):
    params = tuple((weight.astype(jnp.float32) for weight in (kv_weight, query_weight, out_weight, attn_gain, ffn_gain, gate_weight, up_weight, down_weight)))

    def one_sequence(totals, sequence):
        inputs, upstream, lengths, att_route, att_gate, ffn_route, ffn_gate = sequence

        def forward(weights, state_in):
            return layer(weights, state_in, lengths, att_route, att_gate, ffn_route, ffn_gate)
        result, pull = jax.vjp(forward, params, inputs)
        d_params, d_inputs = pull(upstream)
        return (jax.tree.map(jnp.add, totals, d_params), (result.astype(jnp.bfloat16), d_inputs))
    zeros_init = jax.tree.map(jnp.zeros_like, params)
    totals, (output, input_grad) = lax.scan(one_sequence, zeros_init, (tokens.astype(jnp.float32), cotangent.astype(jnp.float32), doc_lengths, att_routes, att_gates, ffn_routes, ffn_gates))
    return (output, input_grad, totals[0], totals[1], totals[2], totals[3], totals[4], totals[5], totals[6], totals[7])
```

```python
import jax
import jax.numpy as jnp
from jax import lax
from jax.sharding import PartitionSpec as P

HD = 128
ATT_EXP = 8
TOPK = 2
EPSILON = 1e-06
BF = jnp.bfloat16
F32 = jnp.float32


def dot(spec, left, right):
    return jnp.einsum(spec, left, right, preferred_element_type=F32)


def swap(blocks, axes):
    return lax.all_to_all(blocks, axes, split_axis=0, concat_axis=0, tiled=True)


def spread(block, axis):
    count = lax.axis_size(axis)
    return swap(jnp.broadcast_to(block[None], (count,) + block.shape), axis)


def rope_tables(positions):
    half_dim = HD // 2
    freqs = 10000.0 ** (-(jnp.arange(half_dim).astype(F32) * 2.0 / HD))
    angles = positions[..., None].astype(F32) * freqs
    return (jnp.cos(angles), jnp.sin(angles))


def rotate(values, cos_tab, sin_tab):
    half_dim = values.shape[-1] // 2
    first_half = values[..., :half_dim]
    second_half = values[..., half_dim:]
    return jnp.concatenate(
        [
            first_half * cos_tab - second_half * sin_tab,
            second_half * cos_tab + first_half * sin_tab,
        ],
        -1,
    )


def slot_places(routes, expert_count, capacity):
    length = routes.shape[-2]
    names = jnp.arange(expert_count, dtype=jnp.int32)[:, None]
    member = jnp.any(jnp.swapaxes(routes, -1, -2)[..., None, :] == names, -3)
    order = jnp.arange(length)
    before = (order[:, None] < order[None, :]).astype(BF)
    rank = dot("...et,tu->...eu", member.astype(BF), before)
    slots = jnp.arange(capacity, dtype=F32)[:, None]
    return (member[..., None, :] & (rank[..., None, :] == slots)).astype(BF)


def per_device(
    tokens,
    cotangent,
    doc_lengths,
    att_routes,
    att_gates,
    ffn_routes,
    ffn_gates,
    kv_weight,
    query_weight,
    out_weight,
    attn_gain,
    ffn_gain,
    gate_weight,
    up_weight,
    down_weight,
):
    _, group, width = tokens.shape
    owners = lax.axis_size("expert")
    shares = lax.axis_size("tensor")
    dps = lax.axis_size("dp")
    own = lax.axis_index("expert")
    share = lax.axis_index("tensor")
    columns = owners // 2
    column_half = own % 2
    att_cap = min(group, group * TOPK * 5 // (4 * ATT_EXP))
    ffn_cap = min(group, group * TOPK * 5 // (4 * owners))
    rows = owners * att_cap
    seq_len = owners * group
    piece = width // shares
    local = kv_weight.shape[0]
    head_width = kv_weight.shape[2]

    kv_parts = jnp.transpose(kv_weight.reshape(local, 2, columns, HD), (2, 0, 1, 3))
    kv_parts = jnp.repeat(kv_parts.reshape(columns, local, 2 * HD), 2, axis=0)
    gains = jnp.pad(jnp.stack([attn_gain, ffn_gain], 1), ((0, 0), (0, HD - 2)))
    gains = jnp.broadcast_to(gains[None], (owners, local, HD))
    first_pack = swap(jnp.concatenate([kv_parts, gains, query_weight], 2), "expert")
    second_pack = swap(jnp.swapaxes(out_weight, 1, 2), "expert")
    first_full = lax.all_gather(first_pack.reshape(owners * local, -1), "dp", axis=0, tiled=True)
    out_full = lax.all_gather(second_pack.reshape(owners * local, -1), "dp", axis=0, tiled=True)
    key_value = first_full[:, : 2 * HD]
    gain_one = first_full[:, 2 * HD].astype(F32)
    gain_two = first_full[:, 2 * HD + 1].astype(F32)
    query_full = first_full[:, 3 * HD :]
    gate_full = lax.all_gather(gate_weight[0], "dp", axis=0, tiled=True)
    up_full = lax.all_gather(up_weight[0], "dp", axis=0, tiled=True)
    down_full = lax.all_gather(down_weight[0], "dp", axis=0, tiled=False)

    marks = jnp.pad(att_routes[0].astype(BF), ((0, 0), (0, HD - TOPK)))
    gathered = spread(jnp.concatenate([tokens[0], marks], 1), "expert")
    routes_all = gathered[:, :, width : width + TOPK].astype(jnp.int32)
    inputs_all = gathered[:, :, :width].astype(F32)
    inv_all = lax.rsqrt(jnp.mean(inputs_all * inputs_all, -1, keepdims=True) + EPSILON)
    normed = (inputs_all * inv_all * gain_one).astype(BF)
    places = slot_places(routes_all, ATT_EXP, att_cap)
    token_names = jnp.arange(group, dtype=F32)
    block_starts = (jnp.arange(owners) * group).astype(F32)
    slot_pos = jnp.sum(places.astype(F32) * token_names, -1) + block_starts[:, None, None]
    place_owned = lax.dynamic_index_in_dim(places, own, 1, False)
    pos_owned = lax.dynamic_index_in_dim(slot_pos, own, 1, False)
    pos_half = lax.dynamic_slice_in_dim(slot_pos, column_half * columns, columns, 0)
    row_pos = jnp.swapaxes(pos_half, 0, 1).reshape(rows * columns)
    ends = jnp.cumsum(doc_lengths[0], dtype=jnp.int32).astype(F32)
    key_pos = jnp.arange(seq_len).astype(F32)
    row_seg = jnp.sum((ends[None, :] <= row_pos[:, None]).astype(jnp.int32), -1)
    key_seg = jnp.sum((ends[None, :] <= key_pos[:, None]).astype(jnp.int32), -1)
    visible = (row_seg[:, None] == key_seg[None, :]) & (key_pos[None, :] <= row_pos[:, None])

    def to_heads(values):
        values = values.astype(BF).reshape(2, columns, att_cap, columns, HD)
        values = jnp.transpose(values, (3, 0, 1, 2, 4)).reshape(owners, columns * att_cap, HD)
        return swap(values, "expert").reshape(rows * columns, HD)

    def to_maps(values):
        values = swap(values.astype(BF).reshape(owners, columns * att_cap, HD), "expert")
        values = values.reshape(columns, 2, columns, att_cap, HD)
        return jnp.transpose(values, (1, 2, 3, 0, 4)).reshape(rows, head_width)

    chosen = dot("bst,btd->bsd", place_owned, normed).astype(BF).reshape(rows, width)
    cos_slot, sin_slot = rope_tables(pos_owned)
    query_rows = dot("cd,dh->ch", chosen, query_full).reshape(owners, att_cap, -1, HD)
    query_rows = rotate(query_rows, cos_slot[:, :, None], sin_slot[:, :, None])
    queries = to_heads(query_rows)
    normed = normed.reshape(seq_len, width)
    projected = dot("td,df->tf", normed, key_value)
    cos_key, sin_key = rope_tables(key_pos)
    keys = rotate(projected[:, :HD], cos_key, sin_key).astype(BF)
    values = projected[:, HD:].astype(BF)

    scale = HD ** (-0.5)
    scores = jnp.where(visible, dot("qd,kd->qk", queries, keys) * scale, -1e30)
    row_top = jnp.max(scores, -1, keepdims=True)
    shifted = jnp.exp(scores - row_top)
    row_total = jnp.sum(shifted, -1, keepdims=True)
    probs = shifted / row_total
    log_sum = row_top + jnp.log(row_total)
    mixed = to_maps(dot("qk,kd->qd", probs.astype(BF), values))

    def to_blocks(parts):
        parts = parts.astype(BF).reshape(shares, owners, -1, piece)
        parts = jnp.swapaxes(parts, 0, 1).reshape(owners * shares, -1, piece)
        return swap(parts, ("expert", "tensor"))

    def choice_places(places_here, routes):
        names = jnp.arange(places_here.shape[0], dtype=jnp.int32)
        picks = (routes[:, :, None] == names).astype(BF)
        return jnp.einsum("mst,tjm->jtms", places_here, picks)

    def from_slots(selection, parts):
        selection = jnp.broadcast_to(
            selection[..., None, :], selection.shape[:-1] + (shares, selection.shape[-1])
        )
        selection = selection.reshape(selection.shape[:-3] + (-1,))
        return dot("...tk,kd->...td", selection, parts.reshape(-1, piece))

    def join(part):
        return jnp.swapaxes(spread(part, "tensor"), 0, 1).reshape(group, -1)

    place_att = slot_places(att_routes[0], ATT_EXP, att_cap)
    pick_att = choice_places(place_att, att_routes[0])
    att_gate = att_gates[0]
    out_rows = jnp.einsum(
        "ch,kdh->kcd", mixed, out_full.reshape(shares, piece, head_width), preferred_element_type=F32
    )
    branch = from_slots(pick_att, to_blocks(out_rows))
    attention = jnp.einsum("jtd,tj->td", branch, att_gate, precision=lax.Precision.HIGHEST)
    inputs = tokens[0].astype(F32)
    state = inputs + join(attention.astype(BF)).astype(F32)
    inv_two = lax.rsqrt(jnp.mean(state * state, -1, keepdims=True) + EPSILON)
    normed_two = (state * inv_two * gain_two).astype(BF)

    place_ffn = slot_places(ffn_routes[0], owners, ffn_cap)
    pick_ffn = choice_places(place_ffn, ffn_routes[0])
    ffn_gate = ffn_gates[0]
    gate_slot = jnp.einsum("jtms,tj->ms", pick_ffn, ffn_gate, precision=lax.Precision.HIGHEST)
    upstream = cotangent[0]
    grad_rows = (dot("mst,td->msd", place_ffn, upstream) * gate_slot[:, :, None]).astype(BF)
    expert_grad = swap(grad_rows, "expert").reshape(-1, width)
    send_rows = dot("mst,td->msd", place_ffn, normed_two).astype(BF)
    expert_in = swap(send_rows, "expert").reshape(-1, width)
    gate_act = dot("cd,df->cf", expert_in, gate_full)
    up_act = dot("cd,df->cf", expert_in, up_full)
    sigma = jax.nn.sigmoid(gate_act)
    hidden = (gate_act * sigma * up_act).astype(BF)
    expert_out = dot("cf,kfd->kcd", hidden, down_full)
    ffn_rows = from_slots(pick_ffn, to_blocks(expert_out))
    ffn_part = jnp.einsum("jtd,tj->td", ffn_rows, ffn_gate, precision=lax.Precision.HIGHEST)
    state_part = lax.dynamic_slice_in_dim(state, share * piece, piece, 1)
    output_part = (state_part + ffn_part).astype(BF)

    split_grad = expert_grad.reshape(-1, shares, piece)
    d_hidden = dot("ckd,kfd->cf", split_grad, down_full)
    d_gate = (d_hidden * up_act * sigma * (1.0 + gate_act * (1.0 - sigma))).astype(BF)
    d_up = (d_hidden * gate_act * sigma).astype(BF)
    d_expert_in = dot("cf,df->cd", d_gate, gate_full) + dot("cf,df->cd", d_up, up_full)
    d_expert_in = jnp.swapaxes(d_expert_in.reshape(-1, shares, piece), 0, 1)
    d_norm_rows = to_blocks(d_expert_in)
    d_normed_two = join(
        from_slots(jnp.transpose(place_ffn, (2, 0, 1)), d_norm_rows).astype(BF)
    ).astype(F32)

    def scatter(grad):
        return lax.psum_scatter(grad.astype(BF), "dp", scatter_dimension=0, tiled=True)

    down_grad = scatter(dot("cf,ckd->kfd", hidden, split_grad)).astype(F32)
    gate_grad = scatter(dot("cd,cf->df", expert_in, d_gate)).astype(F32)[None]
    up_grad = scatter(dot("cd,cf->df", expert_in, d_up)).astype(F32)[None]

    upstream = upstream.astype(F32)
    scaled_two = gain_two * d_normed_two
    d_gain_two = jnp.sum(d_normed_two * state * inv_two, 0)
    d_state = (
        upstream
        + inv_two * scaled_two
        - state * inv_two**3 * jnp.mean(state * scaled_two, -1, keepdims=True)
    )
    d_branch = (att_gate.T[:, :, None] * d_state[None]).astype(BF)
    branch_rows = dot("jtms,jtd->msd", pick_att, d_branch).astype(BF)
    d_rows = swap(branch_rows, "expert").reshape(rows, width)
    d_mixed = to_heads(dot("cd,dh->ch", d_rows, out_full))
    out_grad = scatter(dot("cd,ch->dh", d_rows, mixed)).reshape(owners, local, head_width)
    out_grad = jnp.swapaxes(swap(out_grad, "expert"), 1, 2).astype(F32)

    scores = dot("qd,kd->qk", queries, keys) * scale
    probs = jnp.where(visible, jnp.exp(scores - log_sum), 0.0)
    d_probs = dot("qd,kd->qk", d_mixed, values)
    delta = jnp.sum(probs * d_probs, -1, keepdims=True)
    d_scores = (probs * (d_probs - delta)).astype(BF)
    d_queries = dot("qk,kd->qd", d_scores, keys) * scale
    d_keys = dot("qk,qd->kd", d_scores, queries) * scale
    d_values = dot("qk,qd->kd", probs.astype(BF), d_mixed)
    cos_row, sin_row = rope_tables(row_pos)
    d_query_rows = to_maps(rotate(d_queries, cos_row, -sin_row))
    first = column_half == 0
    pairs = [(i, i + 1 - 2 * (i % 2)) for i in range(owners)]
    d_other = lax.ppermute(jnp.where(first, d_values, d_keys).astype(BF), "expert", pairs)
    d_own = jnp.where(first, d_keys, d_values) + d_other.astype(F32)
    d_own = jnp.where(first, rotate(d_own, cos_key, -sin_key), d_own).astype(BF)
    own_weight = jnp.where(first, key_value[:, :HD], key_value[:, HD:])

    d_query_tokens = dot(
        "bst,bsh->bth", place_owned, d_query_rows.reshape(owners, att_cap, head_width)
    )
    d_proj = jnp.concatenate([d_query_tokens.astype(BF).reshape(seq_len, -1), d_own], 1)
    weight_cat = jnp.concatenate([query_full, own_weight], 1).reshape(shares, piece, -1)
    d_normed = dot("th,kdh->ktd", d_proj, weight_cat)
    d_parts = to_blocks(d_normed)
    d_normed_one = jnp.sum(d_parts.astype(F32), 0).astype(BF)
    both = spread(jnp.concatenate([d_normed_one, output_part], 1), "tensor")
    d_normed_one = jnp.swapaxes(both[:, :, :piece], 0, 1).reshape(group, width).astype(F32)
    output = jnp.swapaxes(both[:, :, piece:], 0, 1).reshape(1, group, width)
    scaled_one = gain_one * d_normed_one
    inv_one = lax.rsqrt(jnp.mean(inputs * inputs, -1, keepdims=True) + EPSILON)
    d_gain_one = jnp.sum(d_normed_one * inputs * inv_one, 0)
    input_grad = (
        d_state
        + inv_one * scaled_one
        - inputs * inv_one**3 * jnp.mean(inputs * scaled_one, -1, keepdims=True)
    )[None]

    map_grad = scatter(dot("td,th->dh", normed, d_proj)).reshape(owners, local, -1)
    map_grad = swap(map_grad, "expert").astype(F32)
    query_grad = map_grad[:, :, :head_width]
    kv_grad = jnp.transpose(
        map_grad[:, :, head_width:].reshape(columns, 2, local, HD), (2, 1, 0, 3)
    ).reshape(local, 2, head_width)
    gain_grads = jnp.stack([d_gain_one, d_gain_two]).reshape(2, dps * owners, local)
    gain_grads = jnp.sum(swap(jnp.swapaxes(gain_grads, 0, 1), ("dp", "expert")), 0)
    return (
        output,
        input_grad,
        kv_grad,
        query_grad,
        out_grad,
        gain_grads[0],
        gain_grads[1],
        gate_grad,
        up_grad,
        down_grad,
    )


def solution(mesh):
    in_specs = (
        P("dp", "expert", None),
        P("dp", "expert", None),
        P("dp", None),
        P("dp", "expert", None),
        P("dp", "expert", None),
        P("dp", "expert", None),
        P("dp", "expert", None),
        P(("dp", "expert"), None, "tensor"),
        P(None, ("dp", "expert"), "tensor"),
        P(None, "tensor", ("dp", "expert")),
        P(("dp", "expert")),
        P(("dp", "expert")),
        P("expert", "dp", "tensor"),
        P("expert", "dp", "tensor"),
        P("expert", "tensor", "dp"),
    )
    out_specs = (
        P("dp", "expert", None),
        P("dp", "expert", None),
        P(("dp", "expert"), None, "tensor"),
        P(None, ("dp", "expert"), "tensor"),
        P(None, "tensor", ("dp", "expert")),
        P(("dp", "expert")),
        P(("dp", "expert")),
        P("expert", "dp", "tensor"),
        P("expert", "dp", "tensor"),
        P("expert", "tensor", "dp"),
    )
    return jax.shard_map(
        per_device, mesh=mesh, in_specs=in_specs, out_specs=out_specs, check_vma=False
    )
```

```python
import jax
import jax.numpy as jnp
from jax import lax
from jax.experimental import pallas as pl
from jax.experimental.pallas import tpu as pltpu
from jax.sharding import PartitionSpec as P

HD = 128
ATT_EXP = 8
TOPK = 2
EPSILON = 1e-06
BF = jnp.bfloat16
F32 = jnp.float32


def dot(spec, left, right):
    return jnp.einsum(spec, left, right, preferred_element_type=F32)


def swap(blocks, axes):
    return lax.all_to_all(blocks, axes, split_axis=0, concat_axis=0, tiled=True)


def spread(block, axis):
    count = lax.axis_size(axis)
    return swap(jnp.broadcast_to(block[None], (count,) + block.shape), axis)


def rope_tables(positions):
    half_dim = HD // 2
    freqs = 10000.0 ** (-(jnp.arange(half_dim).astype(F32) * 2.0 / HD))
    angles = positions[..., None].astype(F32) * freqs
    return (jnp.cos(angles), jnp.sin(angles))


def rotate(values, cos_tab, sin_tab):
    half_dim = values.shape[-1] // 2
    first_half = values[..., :half_dim]
    second_half = values[..., half_dim:]
    return jnp.concatenate(
        [
            first_half * cos_tab - second_half * sin_tab,
            second_half * cos_tab + first_half * sin_tab,
        ],
        -1,
    )


def slot_places(routes, expert_count, capacity):
    length = routes.shape[-2]
    names = jnp.arange(expert_count, dtype=jnp.int32)[:, None]
    member = jnp.any(jnp.swapaxes(routes, -1, -2)[..., None, :] == names, -3)
    order = jnp.arange(length)
    before = (order[:, None] < order[None, :]).astype(BF)
    rank = dot("...et,tu->...eu", member.astype(BF), before)
    slots = jnp.arange(capacity, dtype=F32)[:, None]
    return (member[..., None, :] & (rank[..., None, :] == slots)).astype(BF)


def remote(src, dst, send, recv, device):
    return pltpu.make_async_remote_copy(
        src_ref=src,
        dst_ref=dst,
        send_sem=send,
        recv_sem=recv,
        device_id=device,
        device_id_type=pl.DeviceIdType.MESH,
    )


def each(count, body, start=1):
    def step(index, carry):
        body(index)
        return carry

    lax.fori_loop(start, count, step, 0)


def mm(left, right, left_dim=1, right_dim=0):
    return lax.dot_general(
        left, right, (((left_dim,), (right_dim,)), ((), ())), preferred_element_type=F32
    )


def enter(own, half, core, owners):
    semaphore = pltpu.get_barrier_semaphore()

    def hello(expert, tensor):
        pl.semaphore_signal(
            semaphore,
            inc=1,
            device_id={"expert": expert, "tensor": tensor},
            device_id_type=pl.DeviceIdType.MESH,
        )

    def column(step):
        hello(
            lax.rem(own + lax.div(step, 2), owners),
            2 * lax.rem(half + lax.rem(step, 2), 2) + core,
        )

    each(2 * owners, column)
    hello(own, 2 * half + 1 - core)
    hello(own, 2 * (1 - half) + 1 - core)
    pl.semaphore_wait(semaphore, 2 * owners + 1)


def send_home(merged, landing, sends, recvs, own, half, core, owners):
    def outgoing(step):
        to, side = lax.rem(own + lax.div(step, 2), owners), lax.rem(half + lax.rem(step, 2), 2)
        return remote(
            merged.at[side, to],
            landing.at[half, own],
            sends.at[step],
            recvs.at[step],
            {"expert": to, "tensor": 2 * side + core},
        )

    each(2 * owners, lambda step: outgoing(step).start())
    landing[half, own] = merged[half, own]
    return outgoing


def wait_home(outgoing, owners):
    each(2 * owners, lambda step: outgoing(step).wait())


def share_slices(slices, sends, recvs, own, share, shares):
    def copy(step):
        return remote(
            slices.at[share],
            slices.at[share],
            sends.at[step],
            recvs.at[step],
            {"expert": own, "tensor": lax.rem(share + step, shares)},
        )

    each(shares, lambda step: copy(step).start())
    each(shares, lambda step: copy(step).wait())


def middle_kernel(
    parts,
    sel_ffn,
    state,
    inv_two,
    upstream,
    gain_two,
    sel_att,
    att_gate,
    out_full,
    queries,
    keys,
    values,
    log_sum,
    row_pos,
    row_seg,
    key_pos,
    key_seg,
    cos_row,
    sin_row,
    cos_key,
    sin_key,
    place_back,
    d_state,
    gain_grad,
    d_rows,
    d_proj,
    sibling,
    merged,
    landing,
    slices,
    rows_out,
    heads_out,
    heads_in,
    queries_out,
    queries_in,
    pair_out,
    pair_in,
    d_keys,
    d_values,
    one_send,
    one_recv,
    home_send,
    home_recv,
    slice_send,
    slice_recv,
    row_send,
    row_recv,
    head_send,
    head_recv,
    back_send,
    back_recv,
):
    own, share = lax.axis_index("expert"), lax.axis_index("tensor")
    owners, shares = heads_out.shape[0], slices.shape[0]
    half, core = lax.div(share, 2), lax.rem(share, 2)
    piece, width = slices.shape[2], state.shape[1]
    slots = merged.shape[2]
    rows = owners * slots
    wide = width // 2
    head_rows = heads_out.shape[1]
    columns = owners // 2
    other = {"expert": own, "tensor": 2 * half + 1 - core}
    enter(own, half, core, owners)

    across = remote(parts.at[1 - core], sibling, one_send.at[0], one_recv.at[0], other)
    across.start()
    across.wait()
    for side in range(2):
        merged[side] = (parts[core, side].astype(F32) + sibling[side].astype(F32)).astype(BF)
    outgoing = send_home(merged, landing, home_send, home_recv, own, half, core, owners)
    wait_home(outgoing, owners)
    total = mm(sel_ffn[...], landing[0].reshape(rows, piece))
    total = total + mm(sel_ffn[...], landing[1].reshape(rows, piece))
    slices[share] = total.astype(BF)
    share_slices(slices, slice_send, slice_recv, own, share, shares)

    inv = inv_two[...]
    mean = jnp.zeros_like(inv)
    for index in range(shares):
        cut = slice(index * piece, (index + 1) * piece)
        grad, value = slices[index].astype(F32), state[:, cut]
        mean = mean + jnp.sum(value * gain_two[:, cut] * grad, 1, keepdims=True)
        gain_grad[:, cut] = jnp.sum(grad * value * inv, 0, keepdims=True)
    mean = mean * (inv * inv * inv / width)
    for index in range(shares):
        cut = slice(index * piece, (index + 1) * piece)
        grad = gain_two[:, cut] * slices[index].astype(F32)
        d_state[:, cut] = upstream[:, cut].astype(F32) + inv * grad - state[:, cut] * mean

    for index in range(2):
        start = pl.multiple_of(core * wide + index * piece, piece)
        grad = d_state[:, pl.ds(start, piece)]
        both = jnp.concatenate(
            [(att_gate[0] * grad).astype(BF), (att_gate[1] * grad).astype(BF)], 0
        )
        picked = mm(sel_att[...], both).astype(BF).reshape(owners, slots, piece)
        rows_out[:, :, index * piece : (index + 1) * piece] = picked

    def row_copy(step):
        to = lax.rem(own + step, owners)
        return remote(
            rows_out.at[to],
            d_rows.at[core, own],
            row_send.at[step],
            row_recv.at[step],
            {"expert": to, "tensor": share},
        )

    each(owners, lambda step: row_copy(step).start())
    d_rows[core, own] = rows_out[own]
    each(owners, lambda step: row_copy(step).wait())
    across = remote(d_rows.at[core], d_rows.at[core], one_send.at[1], one_recv.at[1], other)
    across.start()
    start = pl.multiple_of(core * wide, wide)
    d_mixed = mm(d_rows[core].reshape(rows, wide), out_full[pl.ds(start, wide), :])
    across.wait()
    start = pl.multiple_of((1 - core) * wide, wide)
    d_mixed = d_mixed + mm(d_rows[1 - core].reshape(rows, wide), out_full[pl.ds(start, wide), :])
    d_mixed = d_mixed.astype(BF)
    for column in range(columns):
        for part in range(2):
            heads_out[2 * column + part] = d_mixed[
                part * head_rows : (part + 1) * head_rows, column * HD : (column + 1) * HD
            ]

    def head_copy(step):
        to = lax.rem(own + step, owners)
        return remote(
            heads_out.at[to],
            heads_in.at[own],
            head_send.at[step],
            head_recv.at[step],
            {"expert": to, "tensor": share},
        )

    each(owners, lambda step: head_copy(step).start())
    heads_in[own] = heads_out[own]

    scale = HD ** (-0.5)
    d_keys[...] = jnp.zeros_like(d_keys)
    d_values[...] = jnp.zeros_like(d_values)

    def attend(index):
        span = pl.ds(pl.multiple_of(index * head_rows, head_rows), head_rows)
        query, key, value, grad = queries[span, :], keys[...], values[...], heads_in[index]
        scores = mm(query, key, 1, 1) * scale
        visible = (row_seg[span, :] == key_seg[...]) & (key_pos[...] <= row_pos[span, :])
        probs = jnp.where(visible, jnp.exp(scores - log_sum[span, :]), 0.0)
        d_probs = mm(grad, value, 1, 1)
        delta = jnp.sum(probs * d_probs, 1, keepdims=True)
        d_scores = (probs * (d_probs - delta)).astype(BF)
        d_query = mm(d_scores, key) * scale
        d_query = d_query * cos_row[span, :] + pltpu.roll(d_query, HD // 2, 1) * sin_row[span, :]
        queries_out[index] = d_query.astype(BF)
        d_keys[...] += mm(d_scores, query, 0, 0)
        d_values[...] += mm(probs.astype(BF), grad, 0, 0)

    def query_copy(step):
        to = lax.rem(own + owners - step, owners)
        return remote(
            queries_out.at[to],
            queries_in.at[own],
            back_send.at[step],
            back_recv.at[step],
            {"expert": to, "tensor": share},
        )

    def attend_other(step):
        head_copy(step).wait()
        attend(lax.rem(own + owners - step, owners))
        query_copy(step).start()

    attend(own)
    queries_in[own] = queries_out[own]
    each(owners, attend_other)

    first = lax.rem(own, 2) == 0
    pair_out[...] = jnp.where(first, d_values[...], d_keys[...] * scale).astype(BF)
    pair = {"expert": own + 1 - 2 * lax.rem(own, 2), "tensor": share}
    across = remote(pair_out, pair_in, one_send.at[2], one_recv.at[2], pair)
    across.start()
    each(owners, lambda step: query_copy(step).wait())
    group = place_back.shape[1]
    for part in range(2):
        for index in range(columns):
            block = part * columns + index
            cut = slice(index * slots, (index + 1) * slots)
            picked = jnp.concatenate(
                [queries_in[2 * column + part, cut, :] for column in range(columns)], 1
            )
            d_proj[block * group : (block + 1) * group, : columns * HD] = mm(
                place_back[block], picked
            ).astype(BF)
    across.wait()
    mine = jnp.where(first, d_keys[...] * scale, d_values[...]) + pair_in[...].astype(F32)
    turned = mine * cos_key[...] + pltpu.roll(mine, HD // 2, 1) * sin_key[...]
    d_proj[:, columns * HD :] = jnp.where(first, turned, mine).astype(BF)


def last_kernel(
    d_proj,
    weights,
    output_part,
    tokens,
    inv_one,
    gain_one,
    d_state,
    output,
    input_grad,
    gain_grad,
    far,
    near,
    sibling,
    landing,
    slices,
    one_send,
    one_recv,
    home_send,
    home_recv,
    slice_send,
    slice_recv,
):
    own, share = lax.axis_index("expert"), lax.axis_index("tensor")
    owners, shares = near.shape[1], slices.shape[0]
    half, core = lax.div(share, 2), lax.rem(share, 2)
    group, piece = near.shape[2], near.shape[3]
    width = shares * piece
    head_width = d_proj.shape[1] - HD
    other = {"expert": own, "tensor": 2 * half + 1 - core}
    enter(own, half, core, owners)
    part = lax.rem(own, 2)

    def product(index):
        span = pl.ds(pl.multiple_of(index * piece, piece), piece)
        queries = mm(d_proj[:, :head_width], weights[span, 3 * HD :], 1, 1)
        side = weights[span, pl.ds(pl.multiple_of(part * HD, HD), HD)]
        return (queries + mm(d_proj[:, head_width:], side, 1, 1)).reshape(owners, group, piece)

    def across(side):
        return remote(far.at[side], sibling.at[side], one_send.at[side], one_recv.at[side], other)

    for side in range(2):
        far[side] = product(2 * side + 1 - core).astype(BF)
        across(side).start()
    for side in range(2):
        near[side] = product(2 * side + core).astype(BF)
    for side in range(2):
        across(side).wait()
        near[side] = (near[side].astype(F32) + sibling[side].astype(F32)).astype(BF)
    outgoing = send_home(near, landing, home_send, home_recv, own, half, core, owners)
    wait_home(outgoing, owners)
    total = jnp.zeros((group, piece), F32)
    for side in range(2):
        for index in range(owners):
            total = total + landing[side, index].astype(F32)
    slices[share, 0] = total.astype(BF)
    slices[share, 1] = output_part[...]
    share_slices(slices, slice_send, slice_recv, own, share, shares)
    inv = inv_one[...]
    mean = jnp.zeros_like(inv)
    for index in range(shares):
        cut = slice(index * piece, (index + 1) * piece)
        grad, value = slices[index, 0].astype(F32), tokens[:, cut].astype(F32)
        output[:, cut] = slices[index, 1]
        mean = mean + jnp.sum(value * gain_one[:, cut] * grad, 1, keepdims=True)
        gain_grad[:, cut] = jnp.sum(grad * value * inv, 0, keepdims=True)
    mean = mean * (inv * inv * inv / width)
    for index in range(shares):
        cut = slice(index * piece, (index + 1) * piece)
        grad = gain_one[:, cut] * slices[index, 0].astype(F32)
        value = tokens[:, cut].astype(F32)
        input_grad[:, cut] = d_state[:, cut] + inv * grad - value * mean


def call_kernel(kernel, collective_id, outs, scratch, semaphores, args):
    vmem = pl.BlockSpec(memory_space=pltpu.VMEM)
    return pl.pallas_call(
        kernel,
        out_shape=[jax.ShapeDtypeStruct(shape, dtype) for shape, dtype in outs],
        in_specs=[vmem] * len(args),
        out_specs=[vmem] * len(outs),
        scratch_shapes=[pltpu.VMEM(shape, dtype) for shape, dtype in scratch]
        + [pltpu.SemaphoreType.DMA((count,)) for count in semaphores],
        compiler_params=pltpu.CompilerParams(
            collective_id=collective_id, has_side_effects=True, vmem_limit_bytes=56 * 2**20
        ),
    )(*args)


def per_device(
    tokens,
    cotangent,
    doc_lengths,
    att_routes,
    att_gates,
    ffn_routes,
    ffn_gates,
    kv_weight,
    query_weight,
    out_weight,
    attn_gain,
    ffn_gain,
    gate_weight,
    up_weight,
    down_weight,
):
    _, group, width = tokens.shape
    owners = lax.axis_size("expert")
    shares = lax.axis_size("tensor")
    dps = lax.axis_size("dp")
    own = lax.axis_index("expert")
    share = lax.axis_index("tensor")
    columns = owners // 2
    column_half = own % 2
    att_cap = -(-min(group, group * TOPK * 5 // (4 * ATT_EXP)) // 16) * 16
    ffn_cap = -(-min(group, group * TOPK * 5 // (4 * owners)) // 16) * 16
    rows = owners * att_cap
    seq_len = owners * group
    piece = width // shares
    local = kv_weight.shape[0]
    head_width = kv_weight.shape[2]

    def choice_places(places_here, routes):
        names = jnp.arange(places_here.shape[0], dtype=jnp.int32)
        picks = (routes[:, :, None] == names).astype(BF)
        return jnp.einsum("mst,tjm->jtms", places_here, picks)

    place_ffn = slot_places(ffn_routes[0], owners, ffn_cap)
    pick_ffn = choice_places(place_ffn, ffn_routes[0])
    ffn_gate = ffn_gates[0]
    gate_slot = jnp.einsum("jtms,tj->ms", pick_ffn, ffn_gate, precision=lax.Precision.HIGHEST)
    upstream = cotangent[0]
    grad_rows = (dot("mst,td->msd", place_ffn, upstream) * gate_slot[:, :, None]).astype(BF)

    kv_parts = jnp.transpose(kv_weight.reshape(local, 2, columns, HD), (2, 0, 1, 3))
    kv_parts = jnp.repeat(kv_parts.reshape(columns, local, 2 * HD), 2, axis=0)
    gains = jnp.pad(jnp.stack([attn_gain, ffn_gain], 1), ((0, 0), (0, HD - 2)))
    gains = jnp.broadcast_to(gains[None], (owners, local, HD))
    first_pack = swap(jnp.concatenate([kv_parts, gains, query_weight], 2), "expert")
    down_full = lax.all_gather(down_weight[0], "dp", axis=0, tiled=False)
    marks = jnp.pad(att_routes[0].astype(BF), ((0, 0), (0, HD - TOPK)))
    early = width * 5 // 8
    token_pack = jnp.concatenate([tokens[0, :, early:], marks], 1)
    early_tokens, first_pack = lax.optimization_barrier((tokens[0, :, :early], first_pack))
    early_tokens = spread(early_tokens, "expert")
    first_pack, down_full, early_tokens, token_pack, out_parts = lax.optimization_barrier(
        (first_pack, down_full, early_tokens, token_pack, jnp.swapaxes(out_weight, 1, 2))
    )
    first_full = lax.all_gather(first_pack.reshape(owners * local, -1), "dp", axis=0, tiled=True)
    second_pack = swap(out_parts, "expert")
    token_pack, second_pack, grad_rows = lax.optimization_barrier(
        (token_pack, second_pack, grad_rows)
    )
    out_full = lax.all_gather(second_pack.reshape(owners * local, -1), "dp", axis=0, tiled=True)
    late_tokens = spread(token_pack, "expert")
    late_tokens, grad_rows = lax.optimization_barrier((late_tokens, grad_rows))
    expert_grad = swap(grad_rows, "expert").reshape(-1, width)
    first_full, expert_grad = lax.optimization_barrier((first_full, expert_grad))
    gate_up = jnp.concatenate([gate_weight[0], up_weight[0]], 1)
    gate_up_full = lax.all_gather(gate_up, "dp", axis=0, tiled=True)
    units = gate_weight.shape[2]
    key_value = first_full[:, : 2 * HD]
    gain_one = first_full[:, 2 * HD].astype(F32)
    gain_two = first_full[:, 2 * HD + 1].astype(F32)
    query_full = first_full[:, 3 * HD :]
    gate_up = jnp.concatenate([gate_weight[0], up_weight[0]], 1)
    out_full, gate_up = lax.optimization_barrier((out_full, gate_up))
    gate_up_full = lax.all_gather(gate_up, "dp", axis=0, tiled=True)
    units = gate_weight.shape[2]

    routes_all = late_tokens[:, :, width - early : width - early + TOPK].astype(jnp.int32)
    inputs_all = jnp.concatenate([early_tokens, late_tokens[:, :, : width - early]], 2).astype(F32)
    inv_all = lax.rsqrt(jnp.mean(inputs_all * inputs_all, -1, keepdims=True) + EPSILON)
    normed = (inputs_all * inv_all * gain_one).astype(BF)
    places = slot_places(routes_all, ATT_EXP, att_cap)
    token_names = jnp.arange(group, dtype=F32)
    block_starts = (jnp.arange(owners) * group).astype(F32)
    slot_pos = jnp.sum(places.astype(F32) * token_names, -1) + block_starts[:, None, None]
    place_owned = lax.dynamic_index_in_dim(places, own, 1, False)
    pos_owned = lax.dynamic_index_in_dim(slot_pos, own, 1, False)
    pos_half = lax.dynamic_slice_in_dim(slot_pos, column_half * columns, columns, 0)
    row_pos = jnp.swapaxes(pos_half, 0, 1).reshape(rows * columns)
    ends = jnp.cumsum(doc_lengths[0], dtype=jnp.int32).astype(F32)
    key_pos = jnp.arange(seq_len).astype(F32)
    row_seg = jnp.sum((ends[None, :] <= row_pos[:, None]).astype(jnp.int32), -1)
    key_seg = jnp.sum((ends[None, :] <= key_pos[:, None]).astype(jnp.int32), -1)
    visible = (row_seg[:, None] == key_seg[None, :]) & (key_pos[None, :] <= row_pos[:, None])

    def to_heads(values):
        values = values.astype(BF).reshape(2, columns, att_cap, columns, HD)
        values = jnp.transpose(values, (3, 0, 1, 2, 4)).reshape(owners, columns * att_cap, HD)
        return swap(values, "expert").reshape(rows * columns, HD)

    def to_maps(values):
        values = swap(values.astype(BF).reshape(owners, columns * att_cap, HD), "expert")
        values = values.reshape(columns, 2, columns, att_cap, HD)
        return jnp.transpose(values, (1, 2, 3, 0, 4)).reshape(rows, head_width)

    chosen = dot("bst,btd->bsd", place_owned, normed).astype(BF).reshape(rows, width)
    cos_slot, sin_slot = rope_tables(pos_owned)
    query_rows = dot("cd,dh->ch", chosen, query_full).reshape(owners, att_cap, -1, HD)
    query_rows = rotate(query_rows, cos_slot[:, :, None], sin_slot[:, :, None])
    queries = to_heads(query_rows)
    normed = normed.reshape(seq_len, width)
    projected = dot("td,df->tf", normed, key_value)
    cos_key, sin_key = rope_tables(key_pos)
    keys = rotate(projected[:, :HD], cos_key, sin_key).astype(BF)
    values = projected[:, HD:].astype(BF)

    scale = HD ** (-0.5)
    scores = jnp.where(visible, dot("qd,kd->qk", queries, keys) * scale, -1e30)
    row_top = jnp.max(scores, -1, keepdims=True)
    shifted = jnp.exp(scores - row_top)
    row_total = jnp.sum(shifted, -1, keepdims=True)
    probs = shifted / row_total
    log_sum = row_top + jnp.log(row_total)
    mixed = to_maps(dot("qk,kd->qd", probs.astype(BF), values))

    def to_blocks(parts):
        parts = parts.astype(BF).reshape(shares, owners, -1, piece)
        parts = jnp.swapaxes(parts, 0, 1).reshape(owners * shares, -1, piece)
        return swap(parts, ("expert", "tensor"))

    def from_slots(selection, parts):
        selection = jnp.broadcast_to(
            selection[..., None, :], selection.shape[:-1] + (shares, selection.shape[-1])
        )
        selection = selection.reshape(selection.shape[:-3] + (-1,))
        return dot("...tk,kd->...td", selection, parts.reshape(-1, piece))

    def join(part):
        return jnp.swapaxes(spread(part, "tensor"), 0, 1).reshape(group, -1)

    place_att = slot_places(att_routes[0], ATT_EXP, att_cap)
    pick_att = choice_places(place_att, att_routes[0])
    att_gate = att_gates[0]
    out_rows = jnp.einsum(
        "ch,kdh->kcd", mixed, out_full.reshape(shares, piece, head_width), preferred_element_type=F32
    )
    branch = from_slots(pick_att, to_blocks(out_rows))
    attention = jnp.einsum("jtd,tj->td", branch, att_gate, precision=lax.Precision.HIGHEST)
    inputs = tokens[0].astype(F32)
    state = inputs + join(attention.astype(BF)).astype(F32)
    inv_two = lax.rsqrt(jnp.mean(state * state, -1, keepdims=True) + EPSILON)
    normed_two = (state * inv_two * gain_two).astype(BF)

    send_rows = dot("mst,td->msd", place_ffn, normed_two).astype(BF)
    expert_in = swap(send_rows, "expert").reshape(-1, width)
    both_act = dot("cd,df->cf", expert_in, gate_up_full)
    gate_act, up_act = both_act[:, :units], both_act[:, units:]
    sigma = jax.nn.sigmoid(gate_act)
    hidden = (gate_act * sigma * up_act).astype(BF)
    expert_out = dot("cf,kfd->kcd", hidden, down_full)
    ffn_rows = from_slots(pick_ffn, to_blocks(expert_out))
    ffn_part = jnp.einsum("jtd,tj->td", ffn_rows, ffn_gate, precision=lax.Precision.HIGHEST)
    state_part = lax.dynamic_slice_in_dim(state, share * piece, piece, 1)
    output_part = (state_part + ffn_part).astype(BF)

    split_grad = expert_grad.reshape(-1, shares, piece)
    d_hidden = dot("ckd,kfd->cf", split_grad, down_full)
    d_gate = (d_hidden * up_act * sigma * (1.0 + gate_act * (1.0 - sigma))).astype(BF)
    d_up = (d_hidden * gate_act * sigma).astype(BF)
    d_both = jnp.concatenate([d_gate, d_up], 1)
    d_expert_in = dot("cf,df->cd", d_both, gate_up_full)
    used = min(group, group * TOPK * 5 // (4 * owners))

    def tight(array):
        array = array.reshape((owners, ffn_cap) + array.shape[1:])[:, :used]
        return array.reshape((-1,) + array.shape[2:])

    hidden_all = lax.all_gather(tight(hidden), "dp", axis=0, tiled=True)
    d_both_all = lax.all_gather(tight(d_both), "dp", axis=0, tiled=True)
    slices = jnp.concatenate([expert_in.reshape(-1, dps, piece), expert_grad.reshape(-1, dps, piece)], 2)
    slices = swap(jnp.swapaxes(tight(slices), 0, 1), "dp").reshape(-1, 2 * piece)
    d_parts = jnp.transpose(d_expert_in.astype(BF).reshape(owners, ffn_cap, 2, 2, piece), (3, 2, 0, 1, 4))

    def scatter(grad):
        return lax.psum_scatter(grad.astype(BF), "dp", scatter_dimension=0, tiled=True)

    cos_row, sin_row = rope_tables(row_pos)
    slots = att_cap
    d_state, d_gain_two, d_rows, d_proj = call_kernel(
        middle_kernel,
        1,
        [
            ((group, width), F32),
            ((1, width), F32),
            ((2, owners, slots, width // 2), BF),
            ((seq_len, head_width + HD), BF),
        ],
        [
            ((2, owners, ffn_cap, piece), BF),
            ((2, owners, ffn_cap, piece), BF),
            ((2, owners, ffn_cap, piece), BF),
            ((shares, group, piece), BF),
            ((owners, slots, width // 2), BF),
            ((owners, columns * slots, HD), BF),
            ((owners, columns * slots, HD), BF),
            ((owners, columns * slots, HD), BF),
            ((owners, columns * slots, HD), BF),
            ((seq_len, HD), BF),
            ((seq_len, HD), BF),
            ((seq_len, HD), F32),
            ((seq_len, HD), F32),
        ],
        [3, 3, 2 * owners, 2 * owners, shares, shares, owners, owners, owners, owners, owners, owners],
        [
            d_parts,
            jnp.transpose(place_ffn, (2, 0, 1)).reshape(group, -1),
            state,
            inv_two,
            upstream,
            gain_two[None],
            jnp.transpose(pick_att, (2, 3, 0, 1)).reshape(rows, -1),
            att_gate.T[:, :, None],
            out_full,
            queries,
            keys,
            values,
            log_sum,
            row_pos[:, None],
            row_seg[:, None],
            key_pos[None],
            key_seg[None],
            jnp.concatenate([cos_row, cos_row], 1),
            jnp.concatenate([sin_row, -sin_row], 1),
            jnp.concatenate([cos_key, cos_key], 1),
            jnp.concatenate([sin_key, -sin_key], 1),
            jnp.swapaxes(place_owned, 1, 2),
        ],
    )
    inv_one = lax.rsqrt(jnp.mean(inputs * inputs, -1, keepdims=True) + EPSILON)
    output, input_grad, d_gain_one = call_kernel(
        last_kernel,
        2,
        [((group, width), BF), ((group, width), F32), ((1, width), F32)],
        [
            ((2, owners, group, piece), BF),
            ((2, owners, group, piece), BF),
            ((2, owners, group, piece), BF),
            ((2, owners, group, piece), BF),
            ((shares, 2, group, piece), BF),
        ],
        [2, 2, 2 * owners, 2 * owners, shares, shares],
        [d_proj, first_full, output_part, tokens[0], inv_one, gain_one[None], d_state],
    )
    out_grad = scatter(dot("kcd,ch->kdh", d_rows.reshape(2, rows, -1), mixed).reshape(width, -1))
    out_grad = swap(out_grad.reshape(owners, local, head_width), "expert")
    out_grad = jnp.swapaxes(out_grad, 1, 2).astype(F32)

    down_grad = dot("cf,cd->fd", hidden_all, slices[:, piece:])[None]
    gate_up_grad = dot("cd,cf->df", slices[:, :piece], d_both_all)
    gate_grad, up_grad = gate_up_grad[None, :, :units], gate_up_grad[None, :, units:]
    map_grad = scatter(dot("td,th->dh", normed, d_proj)).reshape(owners, local, -1)
    map_grad = swap(map_grad, "expert").astype(F32)
    query_grad = map_grad[:, :, :head_width]
    kv_grad = jnp.transpose(
        map_grad[:, :, head_width:].reshape(columns, 2, local, HD), (2, 1, 0, 3)
    ).reshape(local, 2, head_width)
    gain_grads = jnp.stack([d_gain_one[0], d_gain_two[0]]).reshape(2, dps * owners, local)
    gain_grads = jnp.sum(swap(jnp.swapaxes(gain_grads, 0, 1), ("dp", "expert")), 0)
    return (
        output[None],
        input_grad[None],
        kv_grad,
        query_grad,
        out_grad,
        gain_grads[0],
        gain_grads[1],
        gate_grad,
        up_grad,
        down_grad,
    )


def solution(mesh):
    in_specs = (
        P("dp", "expert", None),
        P("dp", "expert", None),
        P("dp", None),
        P("dp", "expert", None),
        P("dp", "expert", None),
        P("dp", "expert", None),
        P("dp", "expert", None),
        P(("dp", "expert"), None, "tensor"),
        P(None, ("dp", "expert"), "tensor"),
        P(None, "tensor", ("dp", "expert")),
        P(("dp", "expert")),
        P(("dp", "expert")),
        P("expert", "dp", "tensor"),
        P("expert", "dp", "tensor"),
        P("expert", "tensor", "dp"),
    )
    out_specs = (
        P("dp", "expert", None),
        P("dp", "expert", None),
        P(("dp", "expert"), None, "tensor"),
        P(None, ("dp", "expert"), "tensor"),
        P(None, "tensor", ("dp", "expert")),
        P(("dp", "expert")),
        P(("dp", "expert")),
        P("expert", "dp", "tensor"),
        P("expert", "dp", "tensor"),
        P("expert", "tensor", "dp"),
    )
    return jax.shard_map(
        per_device, mesh=mesh, in_specs=in_specs, out_specs=out_specs, check_vma=False
    )
```

```python
import jax
import jax.numpy as jnp
import numpy as np
from jax import lax
from jax.experimental import pallas as pl
from jax.experimental.pallas import tpu as pltpu
from jax.sharding import PartitionSpec as P

HD = 128
ATT_EXP = 8
TOPK = 2
EPSILON = 1e-06
BF = jnp.bfloat16
F32 = jnp.float32


def dot(spec, left, right):
    return jnp.einsum(spec, left, right, preferred_element_type=F32)


def swap(blocks, axes):
    return lax.all_to_all(blocks, axes, split_axis=0, concat_axis=0, tiled=True)


def slot_places(routes, expert_count, capacity):
    length = routes.shape[-2]
    names = jnp.arange(expert_count, dtype=jnp.int32)[:, None]
    member = jnp.any(jnp.swapaxes(routes, -1, -2)[..., None, :] == names, -3)
    order = jnp.arange(length)
    before = (order[:, None] < order[None, :]).astype(BF)
    rank = dot("...et,tu->...eu", member.astype(BF), before)
    slots = jnp.arange(capacity, dtype=F32)[:, None]
    return (member[..., None, :] & (rank[..., None, :] == slots)).astype(BF)


def remote(src, dst, send, recv, device):
    return pltpu.make_async_remote_copy(
        src_ref=src,
        dst_ref=dst,
        send_sem=send,
        recv_sem=recv,
        device_id=device,
        device_id_type=pl.DeviceIdType.MESH,
    )


def each(count, body, start=1):
    def step(index, carry):
        body(index)
        return carry

    lax.fori_loop(start, count, step, 0)


def mm(left, right, left_dim=1, right_dim=0, precision=None):
    return lax.dot_general(
        left,
        right,
        (((left_dim,), (right_dim,)), ((), ())),
        precision=precision,
        preferred_element_type=F32,
    )


def enter(own, half, core, owners, around=()):
    semaphore = pltpu.get_barrier_semaphore()
    for index in around:
        pl.semaphore_signal(
            semaphore, inc=1, device_id={"dp": index}, device_id_type=pl.DeviceIdType.MESH
        )

    def hello(expert, tensor):
        pl.semaphore_signal(
            semaphore,
            inc=1,
            device_id={"expert": expert, "tensor": tensor},
            device_id_type=pl.DeviceIdType.MESH,
        )

    def column(step):
        hello(
            lax.rem(own + lax.div(step, 2), owners),
            2 * lax.rem(half + lax.rem(step, 2), 2) + core,
        )

    each(2 * owners, column)
    hello(own, 2 * half + 1 - core)
    hello(own, 2 * (1 - half) + 1 - core)
    pl.semaphore_wait(semaphore, 2 * owners + 1 + len(around))


def send_home(merged, landing, sends, recvs, own, half, core, owners):
    def outgoing(step):
        to, side = lax.rem(own + lax.div(step, 2), owners), lax.rem(half + lax.rem(step, 2), 2)
        return remote(
            merged.at[side, to],
            landing.at[half, own],
            sends.at[step],
            recvs.at[step],
            {"expert": to, "tensor": 2 * side + core},
        )

    each(2 * owners, lambda step: outgoing(step).start())
    landing[half, own] = merged[half, own]
    return outgoing


def wait_home(outgoing, owners):
    each(2 * owners, lambda step: outgoing(step).wait())


def share_slices(slices, sends, recvs, own, share, shares):
    def copy(step):
        return remote(
            slices.at[share],
            slices.at[share],
            sends.at[step],
            recvs.at[step],
            {"expert": own, "tensor": lax.rem(share + step, shares)},
        )

    each(shares, lambda step: copy(step).start())
    each(shares, lambda step: copy(step).wait())


class Ring:
    def __init__(self, buffer, sends, recvs, base, index, count):
        self.buffer, self.sends, self.recvs, self.base = buffer, sends, recvs, base
        self.index = index
        self.after, self.before = lax.rem(index + 1, count), lax.rem(index + count - 1, count)
        self.cut = buffer.shape[1] // 2

    def copy(self, kind, source=None):
        buffer, cut = self.buffer, self.cut
        if kind < 2:
            src = buffer.at[self.index] if source is None else source
            dst = buffer.at[self.index]
        elif kind == 2:
            src = dst = buffer.at[self.before, pl.ds(0, cut)]
        else:
            src = dst = buffer.at[self.after, pl.ds(cut, cut)]
        place = self.base + kind
        device = {"dp": self.after if kind % 2 == 0 else self.before}
        return remote(src, dst, self.sends.at[place], self.recvs.at[place], device)

    def start(self, source=None):
        self.copy(0, source).start()
        self.copy(1, source).start()

    def forward(self):
        self.copy(0).wait_recv()
        self.copy(2).start()
        self.copy(1).wait_recv()
        self.copy(3).start()

    def finish(self):
        self.copy(2).wait_recv()
        self.copy(3).wait_recv()

    def drain(self, source=None):
        self.copy(0, source).wait_send()
        self.copy(1, source).wait_send()
        self.copy(2).wait_send()
        self.copy(3).wait_send()


def first_kernel(
    tokens,
    marks,
    pack_one,
    pack_two,
    gate_weight,
    up_weight,
    down_weight,
    upstream,
    sel_ffn,
    gate_slot,
    pick_att,
    att_gate,
    pick_ffn,
    ffn_gate,
    ends,
    cos_key,
    sin_key,
    first_full,
    out_full,
    normed,
    gains,
    inv_one,
    queries,
    keys,
    values,
    row_info,
    cos_slot,
    sin_slot,
    place,
    mixed,
    state,
    inv_two,
    features_all,
    hidden,
    d_both,
    d_parts,
    output_part,
    features,
    expert_in,
    expert_grad,
    routes,
    slot_keys,
    inv_all,
    heads_out,
    mixed_out,
    mixed_in,
    far,
    near,
    sibling,
    landing,
    landing_two,
    slices,
    rows_out,
    grads_out,
    gate_up,
    down,
    act,
    ring_send,
    ring_recv,
    local,
    pack_send,
    pack_recv,
    token_send,
    token_recv,
    mark_send,
    mark_recv,
    one_send,
    one_recv,
    head_send,
    head_recv,
    back_send,
    back_recv,
    home_send,
    home_recv,
    home_two_send,
    home_two_recv,
    slice_send,
    slice_recv,
    row_send,
    row_recv,
    grad_send,
    grad_recv,
    feature_send,
    feature_recv,
):
    own, share, dp = lax.axis_index("expert"), lax.axis_index("tensor"), lax.axis_index("dp")
    owners, shares, dps = heads_out.shape[0], slices.shape[0], first_full.shape[0]
    half, core = lax.div(share, 2), lax.rem(share, 2)
    group, piece = slices.shape[1], slices.shape[2]
    width = shares * piece
    wide = width // 2
    slots = rows_out.shape[1]
    rows = owners * slots
    head_rows = heads_out.shape[1]
    columns = owners // 2
    part = lax.rem(own, 2)
    local_rows = pack_one.shape[1]
    units = gate_weight.shape[1]
    other = {"expert": own, "tensor": 2 * half + 1 - core}
    enter(own, half, core, owners, [lax.rem(dp + step, dps) for step in range(1, dps)])

    down_ring = Ring(down, ring_send, ring_recv, 0, dp, dps)
    one_ring = Ring(first_full, ring_send, ring_recv, 4, dp, dps)
    two_ring = Ring(out_full, ring_send, ring_recv, 8, dp, dps)
    gate_ring = Ring(gate_up.at[0], ring_send, ring_recv, 12, dp, dps)
    up_ring = Ring(gate_up.at[1], ring_send, ring_recv, 16, dp, dps)
    own_rows = pl.ds(pl.multiple_of(own * local_rows, local_rows), local_rows)

    def to_owner(src, dst, sends, recvs, step):
        to = lax.rem(own + step, owners)
        device = {"expert": to, "tensor": share}
        return remote(src(to), dst, sends.at[step], recvs.at[step], device)

    def pack_copy(step):
        return to_owner(pack_one.at.__getitem__, first_full.at[dp, own_rows], pack_send, pack_recv, step)

    def second_copy(step):
        to = lax.rem(own + step, owners)
        return remote(
            pack_two.at[to],
            out_full.at[dp, own_rows],
            pack_send.at[owners + step],
            pack_recv.at[owners + step],
            {"expert": to, "tensor": share},
        )

    def token_copy(step):
        start = pl.multiple_of(core * wide, wide)
        return to_owner(
            lambda to: tokens.at[:, pl.ds(start, wide)],
            normed.at[core, own],
            token_send,
            token_recv,
            step,
        )

    def mark_copy(step):
        return to_owner(lambda to: marks, routes.at[own], mark_send, mark_recv, step)

    down_ring.start(down_weight)
    each(owners, lambda step: pack_copy(step).start())
    each(owners, lambda step: mark_copy(step).start())
    each(owners, lambda step: token_copy(step).start())
    each(owners, lambda step: second_copy(step).start())
    own_copies = [
        pltpu.make_async_copy(pack_one.at[own], first_full.at[dp, own_rows], local.at[0]),
        pltpu.make_async_copy(pack_two.at[own], out_full.at[dp, own_rows], local.at[1]),
        pltpu.make_async_copy(gate_weight, gate_up.at[0, dp], local.at[2]),
        pltpu.make_async_copy(up_weight, gate_up.at[1, dp], local.at[3]),
        pltpu.make_async_copy(down_weight, down.at[dp], local.at[4]),
    ]
    for copy in own_copies:
        copy.start()
    routes[own] = marks[...]
    normed[core, own] = tokens[:, pl.ds(pl.multiple_of(core * wide, wide), wide)]

    own_copies[0].wait()
    each(owners, lambda step: pack_copy(step).wait())
    one_ring.start()
    each(owners, lambda step: mark_copy(step).wait())

    def picked_rows(source, out, scale):
        for index in range(2):
            cut = pl.ds(pl.multiple_of(core * wide + index * piece, piece), piece)
            taken = mm(sel_ffn[...], source[:, cut], 0, 0)
            if scale is not None:
                taken = taken * scale
            taken = taken.astype(BF).reshape(owners, slots, piece)
            out[:, :, index * piece : (index + 1) * piece] = taken

    picked_rows(upstream, grads_out, gate_slot[...])

    def grad_copy(step):
        return to_owner(grads_out.at.__getitem__, expert_grad.at[core, own], grad_send, grad_recv, step)

    token_rows = lax.broadcasted_iota(jnp.int32, (group, group), 0)
    token_columns = lax.broadcasted_iota(jnp.int32, (group, group), 1)
    before = (token_rows < token_columns).astype(F32).astype(BF)
    token_names = token_rows.astype(F32).astype(BF)
    slot_names = lax.broadcasted_iota(jnp.int32, (slots, group), 0).astype(F32)
    first_routes = jnp.concatenate([routes[index, 0:1, :] for index in range(owners)], 0)
    second_routes = jnp.concatenate([routes[index, 1:2, :] for index in range(owners)], 0)

    def map_keys(name):
        member = (first_routes == name) | (second_routes == name)
        rank = mm(jnp.where(member, 1.0, 0.0).astype(BF), before)
        return jnp.where(member, rank, -1.0)

    for name in range(owners):
        slot_keys[name] = map_keys(float(name))

    def one_hot(name, block):
        key = slot_keys[name, pl.ds(block, 1), :]
        return jnp.where(key == slot_names, 1.0, 0.0)

    def table(hot, array, block):
        span = pl.ds(pl.multiple_of(block * group, group), group)
        return mm(hot, array[span, :], precision=lax.Precision.HIGHEST)

    def row_block(index, carry):
        name, block = lax.div(index, columns), part * columns + lax.rem(index, columns)
        hot = one_hot(name, block)
        pos = mm(hot.astype(BF), token_names) + (block * group).astype(F32)
        start = jnp.zeros_like(pos)
        for end in range(ends.shape[0]):
            bound = ends[end : end + 1, :]
            start = jnp.maximum(start, jnp.where(bound <= pos, bound, 0.0))
        span = pl.ds(pl.multiple_of(index * slots, slots), slots)
        row_info[span, 0:1] = pos[:, 0:1]
        row_info[span, 1:2] = start[:, 0:1]
        return carry

    lax.fori_loop(0, owners * columns, row_block, 0)

    each(owners, lambda step: token_copy(step).wait())
    across = remote(normed.at[core], normed.at[core], one_send.at[0], one_recv.at[0], other)
    across.start()
    each(owners, lambda step: grad_copy(step).start())
    expert_grad[core, own] = grads_out[own]
    own_copies[1].wait()
    each(owners, lambda step: second_copy(step).wait())
    two_ring.start()
    gate_ring.start(gate_weight)
    up_ring.start(up_weight)
    across.wait()

    def squares(index, carry):
        low, high = normed[0, index].astype(F32), normed[1, index].astype(F32)
        total = jnp.sum(low * low, 1, keepdims=True) + jnp.sum(high * high, 1, keepdims=True)
        inv_all[index] = lax.rsqrt(total / width + EPSILON)
        return carry

    lax.fori_loop(0, owners, squares, 0)
    inv_one[...] = inv_all[own]
    one_ring.forward()
    down_ring.forward()
    one_ring.finish()

    for index in range(dps):
        turned = jnp.transpose(first_full[index, :, 2 * HD : 3 * HD].astype(F32))
        gains[:, index * piece : (index + 1) * piece] = turned[0:2, :]

    chosen = expert_in
    def norm_block(index, carry):
        hot = one_hot(own, index)
        place[index] = hot.astype(BF)
        span = pl.ds(pl.multiple_of(index * slots, slots), slots)
        cos_slot[span, :] = table(hot, cos_key, index)
        sin_slot[span, :] = table(hot, sin_key, index)
        for side in range(2):
            cut = slice(side * wide, (side + 1) * wide)
            rounded = normed[side, index].astype(F32) * inv_all[index] * gains[0:1, cut]
            rounded = rounded.astype(BF)
            normed[side, index] = rounded
            chosen[side, index] = mm(hot.astype(BF), rounded).astype(BF)
        return carry

    lax.fori_loop(0, owners, norm_block, 0)
    query = jnp.zeros((rows, columns * HD), F32)
    for index in range(dps):
        cut = slice((index % 2) * piece, (index % 2 + 1) * piece)
        taken = chosen[index // 2, :, :, cut].reshape(rows, piece)
        query = query + mm(taken, first_full[index, :, 3 * HD :])
    for column in range(columns):
        head = query[:, column * HD : (column + 1) * HD]
        head = (head * cos_slot[...] + pltpu.roll(head, HD // 2, 1) * sin_slot[...]).astype(BF)
        for side in range(2):
            heads_out[2 * column + side] = head[side * head_rows : (side + 1) * head_rows]

    def head_copy(step):
        return to_owner(heads_out.at.__getitem__, queries.at[own], head_send, head_recv, step)

    each(owners, lambda step: head_copy(step).start())
    queries[own] = heads_out[own]

    def key_block(index, carry):
        both = jnp.zeros((group, 2 * HD), F32)
        for step in range(dps):
            cut = slice((step % 2) * piece, (step % 2 + 1) * piece)
            both = both + mm(normed[step // 2, index, :, cut], first_full[step, :, : 2 * HD])
        span = pl.ds(pl.multiple_of(index * group, group), group)
        key = both[:, :HD]
        key = key * cos_key[span, :] + pltpu.roll(key, HD // 2, 1) * sin_key[span, :]
        keys[span, :] = key.astype(BF)
        values[span, :] = both[:, HD:].astype(BF)
        return carry

    lax.fori_loop(0, owners, key_block, 0)
    two_ring.forward()

    scale = HD ** (-0.5)
    key_pos = lax.broadcasted_iota(jnp.int32, (1, owners * group), 1).astype(F32)

    def attend(index):
        span = pl.ds(pl.multiple_of(index * head_rows, head_rows), head_rows)
        scores = mm(queries[index], keys[...], 1, 1) * scale
        visible = (key_pos <= row_info[span, 0:1]) & (key_pos >= row_info[span, 1:2])
        scores = jnp.where(visible, scores, -1e30)
        top = jnp.max(scores, 1, keepdims=True)
        shifted = jnp.exp(scores - top)
        total = jnp.sum(shifted, 1, keepdims=True)
        row_info[span, 2:3] = top + jnp.log(total)
        probs = (shifted / total).astype(BF)
        mixed_out[index] = mm(probs, values[...]).astype(BF)

    def back_copy(step):
        to = lax.rem(own + owners - step, owners)
        return remote(
            mixed_out.at[to],
            mixed_in.at[own],
            back_send.at[step],
            back_recv.at[step],
            {"expert": to, "tensor": share},
        )

    def attend_other(step):
        head_copy(step).wait()
        attend(lax.rem(own + owners - step, owners))
        back_copy(step).start()

    attend(own)
    mixed_in[own] = mixed_out[own]
    each(owners, attend_other)
    gate_ring.forward()
    two_ring.finish()
    each(owners, lambda step: back_copy(step).wait())
    for column in range(columns):
        for side in range(2):
            mixed[
                side * head_rows : (side + 1) * head_rows, column * HD : (column + 1) * HD
            ] = mixed_in[2 * column + side]

    def chip_sum(product, far, near, sibling, base):
        def across(side):
            place = base + side
            return remote(far.at[side], sibling.at[side], one_send.at[place], one_recv.at[place], other)

        for side in range(2):
            far[side] = product(2 * side + 1 - core)
            across(side).start()
        for side in range(2):
            near[side] = product(2 * side + core)
        for side in range(2):
            across(side).wait()
            near[side] = (near[side].astype(F32) + sibling[side].astype(F32)).astype(BF)

    def at_tokens(pick, gate, landing):
        total = jnp.zeros((group, piece), F32)
        for choice in range(TOPK):
            taken = mm(pick[choice], landing[0].reshape(rows, piece))
            taken = taken + mm(pick[choice], landing[1].reshape(rows, piece))
            total = total + gate[choice] * taken
        return total

    def map_product(index):
        return mm(mixed[...], out_full[index], 1, 1).astype(BF).reshape(owners, slots, piece)

    chip_sum(map_product, far, near, sibling, 1)
    outgoing = send_home(near, landing, home_send, home_recv, own, half, core, owners)
    up_ring.forward()
    wait_home(outgoing, owners)
    slices[share] = at_tokens(pick_att, att_gate, landing).astype(BF)
    share_slices(slices, slice_send, slice_recv, own, share, shares)

    total = jnp.zeros((group, 1), F32)
    for index in range(shares):
        cut = slice(index * piece, (index + 1) * piece)
        value = tokens[:, cut].astype(F32) + slices[index].astype(F32)
        state[:, cut] = value
        total = total + jnp.sum(value * value, 1, keepdims=True)
    inv = lax.rsqrt(total / width + EPSILON)
    inv_two[...] = inv
    for index in range(2):
        cut = pl.ds(pl.multiple_of(core * wide + index * piece, piece), piece)
        rounded = (state[:, cut] * inv * gains[1:2, cut]).astype(BF)
        taken = mm(sel_ffn[...], rounded, 0, 0).astype(BF).reshape(owners, slots, piece)
        rows_out[:, :, index * piece : (index + 1) * piece] = taken

    def row_copy(step):
        return to_owner(rows_out.at.__getitem__, expert_in.at[core, own], row_send, row_recv, step)

    each(owners, lambda step: row_copy(step).start())
    expert_in[core, own] = rows_out[own]
    each(owners, lambda step: grad_copy(step).wait())
    across = remote(expert_grad.at[core], expert_grad.at[core], one_send.at[5], one_recv.at[5], other)
    across.start()
    each(owners, lambda step: row_copy(step).wait())
    across_rows = remote(expert_in.at[core], expert_in.at[core], one_send.at[6], one_recv.at[6], other)
    across_rows.start()
    across.wait()
    across_rows.wait()

    used = hidden.shape[0] // owners

    def tight(array):
        pieces = [array[index * slots : index * slots + used] for index in range(owners)]
        return jnp.concatenate(pieces, 0)

    def loose(array):
        blank = jnp.zeros((slots - used, array.shape[1]), F32)
        pieces = []
        for index in range(owners):
            pieces += [array[index * used : (index + 1) * used], blank]
        return jnp.concatenate(pieces, 0).astype(BF).reshape(owners, slots, piece)

    for index in range(dps):
        cut = slice((index % 2) * piece, (index % 2 + 1) * piece)
        for side, source in enumerate((expert_in, expert_grad)):
            taken = source[index // 2, :, :, cut].reshape(rows, piece).astype(F32)
            features[index, :, side * piece : (side + 1) * piece] = tight(taken).astype(BF)
    def feature_copy(step):
        to = lax.rem(dp + step, dps)
        return remote(
            features.at[to],
            features_all.at[dp],
            feature_send.at[step],
            feature_recv.at[step],
            {"dp": to},
        )

    each(dps, lambda step: feature_copy(step).start())
    keep = pltpu.make_async_copy(features.at[dp], features_all.at[dp], feature_send.at[0])
    keep.start()
    for copy in own_copies[2:]:
        copy.wait()
    tile = 2 * HD

    def unit_tiles(body):
        def step(index, carry):
            body(pl.ds(pl.multiple_of(index * tile, tile), tile))
            return carry

        lax.fori_loop(0, units // tile, step, 0)
        if units % tile:
            body(pl.ds(units - units % tile, units % tile))

    gate_ring.finish()

    def gate_tile(cut):
        total = mm(features[0, :, :piece], gate_up[0, 0, :, cut])
        for index in range(1, dps):
            total = total + mm(features[index, :, :piece], gate_up[0, index, :, cut])
        act[0, :, cut] = total

    unit_tiles(gate_tile)
    up_ring.finish()

    def up_tile(cut):
        up = mm(features[0, :, :piece], gate_up[1, 0, :, cut])
        for index in range(1, dps):
            up = up + mm(features[index, :, :piece], gate_up[1, index, :, cut])
        act[1, :, cut] = up
        gate = act[0, :, cut]
        hidden[:, cut] = (gate / (1.0 + jnp.exp(-gate)) * up).astype(BF)

    unit_tiles(up_tile)
    down_ring.finish()
    chip_sum(lambda index: loose(mm(hidden[...], down[index])), far, near, sibling, 7)
    outgoing_two = send_home(
        near, landing_two, home_two_send, home_two_recv, own, half, core, owners
    )

    def grad_tile(cut):
        grad = mm(features[0, :, piece:], down[0, cut, :], 1, 1)
        for index in range(1, dps):
            grad = grad + mm(features[index, :, piece:], down[index, cut, :], 1, 1)
        gate, up = act[0, :, cut], act[1, :, cut]
        sigma = 1.0 / (1.0 + jnp.exp(-gate))
        d_both[0, :, cut] = (grad * up * sigma * (1.0 + gate * (1.0 - sigma))).astype(BF)
        d_both[1, :, cut] = (grad * gate * sigma).astype(BF)

    unit_tiles(grad_tile)
    for index in range(dps):
        total = mm(d_both[0], gate_up[0, index], 1, 1) + mm(d_both[1], gate_up[1, index], 1, 1)
        d_parts[index % 2, index // 2] = loose(total)
    wait_home(outgoing_two, owners)
    rest = at_tokens(pick_ffn, ffn_gate, landing_two)
    span = pl.ds(pl.multiple_of(share * piece, piece), piece)
    output_part[...] = (state[:, span] + rest).astype(BF)
    keep.wait()
    each(dps, lambda step: feature_copy(step).wait())
    one_ring.drain()
    two_ring.drain()
    gate_ring.drain(gate_weight)
    up_ring.drain(up_weight)
    down_ring.drain(down_weight)


def middle_kernel(
    parts,
    sel_ffn,
    state,
    inv_two,
    upstream,
    gains,
    sel_att,
    att_gate,
    out_full,
    queries,
    keys,
    values,
    row_info,
    cos_slot,
    sin_slot,
    cos_key,
    sin_key,
    place,
    hidden,
    d_both,
    d_state,
    gain_grad,
    d_rows,
    d_proj,
    hidden_all,
    d_both_all,
    sibling,
    merged,
    landing,
    slices,
    rows_out,
    heads_out,
    heads_in,
    queries_out,
    queries_in,
    pair_out,
    pair_in,
    d_keys,
    d_values,
    one_send,
    one_recv,
    home_send,
    home_recv,
    slice_send,
    slice_recv,
    row_send,
    row_recv,
    head_send,
    head_recv,
    back_send,
    back_recv,
    ring_send,
    ring_recv,
):
    own, share = lax.axis_index("expert"), lax.axis_index("tensor")
    owners, shares = heads_out.shape[0], slices.shape[0]
    half, core = lax.div(share, 2), lax.rem(share, 2)
    piece, width = slices.shape[2], state.shape[1]
    slots = merged.shape[2]
    rows = owners * slots
    wide = width // 2
    head_rows = heads_out.shape[1]
    columns = owners // 2
    other = {"expert": own, "tensor": 2 * half + 1 - core}
    dp, dps = lax.axis_index("dp"), hidden_all.shape[0]
    enter(own, half, core, owners, (lax.rem(dp + 1, dps), lax.rem(dp + dps - 1, dps)))

    both_ring = Ring(d_both_all, ring_send, ring_recv, 0, dp, dps)
    hidden_ring = Ring(hidden_all, ring_send, ring_recv, 4, dp, dps)
    both_ring.start(d_both)
    hidden_ring.start(hidden)
    keeps = [
        pltpu.make_async_copy(d_both, d_both_all.at[dp], ring_send.at[8]),
        pltpu.make_async_copy(hidden, hidden_all.at[dp], ring_send.at[9]),
    ]
    for keep in keeps:
        keep.start()

    across = remote(parts.at[1 - core], sibling, one_send.at[0], one_recv.at[0], other)
    across.start()
    across.wait()
    for side in range(2):
        merged[side] = (parts[core, side].astype(F32) + sibling[side].astype(F32)).astype(BF)
    outgoing = send_home(merged, landing, home_send, home_recv, own, half, core, owners)
    wait_home(outgoing, owners)
    total = mm(sel_ffn[...], landing[0].reshape(rows, piece))
    total = total + mm(sel_ffn[...], landing[1].reshape(rows, piece))
    slices[share] = total.astype(BF)
    share_slices(slices, slice_send, slice_recv, own, share, shares)

    inv = inv_two[...]
    mean = jnp.zeros_like(inv)
    for index in range(shares):
        cut = slice(index * piece, (index + 1) * piece)
        grad, value = slices[index].astype(F32), state[:, cut]
        mean = mean + jnp.sum(value * gains[1:2, cut] * grad, 1, keepdims=True)
        gain_grad[:, cut] = jnp.sum(grad * value * inv, 0, keepdims=True)
    mean = mean * (inv * inv * inv / width)
    for index in range(shares):
        cut = slice(index * piece, (index + 1) * piece)
        grad = gains[1:2, cut] * slices[index].astype(F32)
        d_state[:, cut] = upstream[:, cut].astype(F32) + inv * grad - state[:, cut] * mean

    for index in range(2):
        start = pl.multiple_of(core * wide + index * piece, piece)
        grad = d_state[:, pl.ds(start, piece)]
        both = jnp.concatenate(
            [(att_gate[0] * grad).astype(BF), (att_gate[1] * grad).astype(BF)], 0
        )
        picked = mm(sel_att[...], both).astype(BF).reshape(owners, slots, piece)
        rows_out[:, :, index * piece : (index + 1) * piece] = picked

    def row_copy(step):
        to = lax.rem(own + step, owners)
        return remote(
            rows_out.at[to],
            d_rows.at[core, own],
            row_send.at[step],
            row_recv.at[step],
            {"expert": to, "tensor": share},
        )

    each(owners, lambda step: row_copy(step).start())
    d_rows[core, own] = rows_out[own]
    each(owners, lambda step: row_copy(step).wait())
    across = remote(d_rows.at[core], d_rows.at[core], one_send.at[1], one_recv.at[1], other)
    across.start()

    def half_product(side):
        taken = d_rows[side].reshape(rows, wide)
        return mm(taken[:, :piece], out_full[2 * side]) + mm(taken[:, piece:], out_full[2 * side + 1])

    d_mixed = half_product(core)
    across.wait()
    d_mixed = (d_mixed + half_product(1 - core)).astype(BF)
    for column in range(columns):
        for part in range(2):
            heads_out[2 * column + part] = d_mixed[
                part * head_rows : (part + 1) * head_rows, column * HD : (column + 1) * HD
            ]

    def head_copy(step):
        to = lax.rem(own + step, owners)
        return remote(
            heads_out.at[to],
            heads_in.at[own],
            head_send.at[step],
            head_recv.at[step],
            {"expert": to, "tensor": share},
        )

    each(owners, lambda step: head_copy(step).start())
    heads_in[own] = heads_out[own]

    scale = HD ** (-0.5)
    key_pos = lax.broadcasted_iota(jnp.int32, (1, keys.shape[0]), 1).astype(F32)
    d_keys[...] = jnp.zeros_like(d_keys)
    d_values[...] = jnp.zeros_like(d_values)

    def attend(index):
        span = pl.ds(pl.multiple_of(index * head_rows, head_rows), head_rows)
        query, key, value, grad = queries[index], keys[...], values[...], heads_in[index]
        scores = mm(query, key, 1, 1) * scale
        visible = (key_pos <= row_info[span, 0:1]) & (key_pos >= row_info[span, 1:2])
        probs = jnp.where(visible, jnp.exp(scores - row_info[span, 2:3]), 0.0)
        d_probs = mm(grad, value, 1, 1)
        delta = jnp.sum(probs * d_probs, 1, keepdims=True)
        d_scores = (probs * (d_probs - delta)).astype(BF)
        queries_out[index] = (mm(d_scores, key) * scale).astype(BF)
        d_keys[...] += mm(d_scores, query, 0, 0)
        d_values[...] += mm(probs.astype(BF), grad, 0, 0)

    def query_copy(step):
        to = lax.rem(own + owners - step, owners)
        return remote(
            queries_out.at[to],
            queries_in.at[own],
            back_send.at[step],
            back_recv.at[step],
            {"expert": to, "tensor": share},
        )

    def attend_other(step):
        head_copy(step).wait()
        attend(lax.rem(own + owners - step, owners))
        query_copy(step).start()

    both_ring.forward()
    attend(own)
    queries_in[own] = queries_out[own]
    each(owners, attend_other)

    first = lax.rem(own, 2) == 0
    pair_out[...] = jnp.where(first, d_values[...], d_keys[...] * scale).astype(BF)
    pair = {"expert": own + 1 - 2 * lax.rem(own, 2), "tensor": share}
    across = remote(pair_out, pair_in, one_send.at[2], one_recv.at[2], pair)
    across.start()
    each(owners, lambda step: query_copy(step).wait())
    group = place.shape[2]
    for part in range(2):
        for index in range(columns):
            block = part * columns + index
            cut = slice(index * slots, (index + 1) * slots)
            span = slice(block * slots, (block + 1) * slots)
            turned = []
            for column in range(columns):
                grad = queries_in[2 * column + part, cut, :].astype(F32)
                back = pltpu.roll(grad, HD // 2, 1) * sin_slot[span, :]
                turned.append((grad * cos_slot[span, :] - back).astype(BF))
            picked = jnp.concatenate(turned, 1)
            d_proj[block * group : (block + 1) * group, : columns * HD] = mm(
                place[block], picked, 0, 0
            ).astype(BF)
    hidden_ring.forward()
    across.wait()
    mine = jnp.where(first, d_keys[...] * scale, d_values[...]) + pair_in[...].astype(F32)
    turned = mine * cos_key[...] + pltpu.roll(mine, HD // 2, 1) * sin_key[...]
    d_proj[:, columns * HD :] = jnp.where(first, turned, mine).astype(BF)
    both_ring.finish()
    hidden_ring.finish()
    both_ring.drain(d_both)
    hidden_ring.drain(hidden)
    for keep in keeps:
        keep.wait()


def last_kernel(
    d_proj,
    weights,
    output_part,
    tokens,
    inv_one,
    gains,
    d_state,
    output,
    input_grad,
    gain_grad,
    far,
    near,
    sibling,
    landing,
    slices,
    one_send,
    one_recv,
    home_send,
    home_recv,
    slice_send,
    slice_recv,
):
    own, share = lax.axis_index("expert"), lax.axis_index("tensor")
    owners, shares = near.shape[1], slices.shape[0]
    half, core = lax.div(share, 2), lax.rem(share, 2)
    group, piece = near.shape[2], near.shape[3]
    width = shares * piece
    head_width = d_proj.shape[1] - HD
    other = {"expert": own, "tensor": 2 * half + 1 - core}
    enter(own, half, core, owners)
    part = lax.rem(own, 2)

    def product(index):
        queries = mm(d_proj[:, :head_width], weights[index, :, 3 * HD :], 1, 1)
        side = weights[index, :, pl.ds(pl.multiple_of(part * HD, HD), HD)]
        return (queries + mm(d_proj[:, head_width:], side, 1, 1)).reshape(owners, group, piece)

    def across(side):
        return remote(far.at[side], sibling.at[side], one_send.at[side], one_recv.at[side], other)

    for side in range(2):
        far[side] = product(2 * side + 1 - core).astype(BF)
        across(side).start()
    for side in range(2):
        near[side] = product(2 * side + core).astype(BF)
    for side in range(2):
        across(side).wait()
        near[side] = (near[side].astype(F32) + sibling[side].astype(F32)).astype(BF)
    outgoing = send_home(near, landing, home_send, home_recv, own, half, core, owners)
    wait_home(outgoing, owners)
    total = jnp.zeros((group, piece), F32)
    for side in range(2):
        for index in range(owners):
            total = total + landing[side, index].astype(F32)
    slices[share, 0] = total.astype(BF)
    slices[share, 1] = output_part[...]
    share_slices(slices, slice_send, slice_recv, own, share, shares)
    inv = inv_one[...]
    mean = jnp.zeros_like(inv)
    for index in range(shares):
        cut = slice(index * piece, (index + 1) * piece)
        grad, value = slices[index, 0].astype(F32), tokens[:, cut].astype(F32)
        output[:, cut] = slices[index, 1]
        mean = mean + jnp.sum(value * gains[0:1, cut] * grad, 1, keepdims=True)
        gain_grad[:, cut] = jnp.sum(grad * value * inv, 0, keepdims=True)
    mean = mean * (inv * inv * inv / width)
    for index in range(shares):
        cut = slice(index * piece, (index + 1) * piece)
        grad = gains[0:1, cut] * slices[index, 0].astype(F32)
        value = tokens[:, cut].astype(F32)
        input_grad[:, cut] = d_state[:, cut] + inv * grad - value * mean


def call_kernel(kernel, collective_id, outs, scratch, semaphores, args, far_args=(), far_outs=()):
    def specs(count, far):
        spaces = [pl.ANY if index in far else pltpu.VMEM for index in range(count)]
        return [pl.BlockSpec(memory_space=space) for space in spaces]

    return pl.pallas_call(
        kernel,
        out_shape=[jax.ShapeDtypeStruct(shape, dtype) for shape, dtype in outs],
        in_specs=specs(len(args), far_args),
        out_specs=specs(len(outs), far_outs),
        scratch_shapes=[pltpu.VMEM(shape, dtype) for shape, dtype in scratch]
        + [pltpu.SemaphoreType.DMA((count,)) for count in semaphores],
        compiler_params=pltpu.CompilerParams(
            collective_id=collective_id, has_side_effects=True, vmem_limit_bytes=60 * 2**20
        ),
    )(*args)


def per_device(
    tokens,
    cotangent,
    doc_lengths,
    att_routes,
    att_gates,
    ffn_routes,
    ffn_gates,
    kv_weight,
    query_weight,
    out_weight,
    attn_gain,
    ffn_gain,
    gate_weight,
    up_weight,
    down_weight,
):
    _, group, width = tokens.shape
    owners = lax.axis_size("expert")
    shares = lax.axis_size("tensor")
    dps = lax.axis_size("dp")
    own = lax.axis_index("expert")
    share = lax.axis_index("tensor")
    columns = owners // 2
    column_half = own % 2
    att_cap = -(-min(group, group * TOPK * 5 // (4 * ATT_EXP)) // 16) * 16
    ffn_cap = -(-min(group, group * TOPK * 5 // (4 * owners)) // 16) * 16
    rows = owners * att_cap
    seq_len = owners * group
    piece = width // shares
    local = kv_weight.shape[0]
    head_width = kv_weight.shape[2]

    def choice_places(places_here, routes):
        names = jnp.arange(places_here.shape[0], dtype=jnp.int32)
        picks = (routes[:, :, None] == names).astype(BF)
        return jnp.einsum("mst,tjm->jtms", places_here, picks)

    place_ffn = slot_places(ffn_routes[0], owners, ffn_cap)
    pick_ffn = choice_places(place_ffn, ffn_routes[0])
    ffn_gate = ffn_gates[0]
    gate_slot = jnp.einsum("jtms,tj->ms", pick_ffn, ffn_gate, precision=lax.Precision.HIGHEST)

    kv_parts = jnp.transpose(kv_weight.reshape(local, 2, columns, HD), (2, 0, 1, 3))
    kv_parts = jnp.repeat(kv_parts.reshape(columns, local, 2 * HD), 2, axis=0)
    both_gains = jnp.pad(jnp.stack([attn_gain, ffn_gain], 1), ((0, 0), (0, HD - 2)))
    both_gains = jnp.broadcast_to(both_gains[None], (owners, local, HD))
    pack_one = jnp.concatenate([kv_parts, both_gains, query_weight], 2)
    pack_two = jnp.swapaxes(out_weight, 1, 2)
    marks = jnp.pad(att_routes[0].T.astype(F32), ((0, 8 - TOPK), (0, 0)), constant_values=-1.0)
    place_att = slot_places(att_routes[0], ATT_EXP, att_cap)
    pick_att = choice_places(place_att, att_routes[0])
    att_gate = att_gates[0]
    ends = jnp.cumsum(doc_lengths[0], dtype=jnp.int32).astype(F32)
    ends = jnp.broadcast_to(ends[:, None], (ends.shape[0], HD))
    angles = np.arange(seq_len)[:, None] * 10000.0 ** (-np.arange(HD // 2) * 2.0 / HD)
    cos_key = jnp.asarray(np.concatenate([np.cos(angles)] * 2, 1), F32)
    sin_key = jnp.asarray(np.concatenate([-np.sin(angles), np.sin(angles)], 1), F32)
    used = min(group, group * TOPK * 5 // (4 * owners))
    units = gate_weight.shape[2]
    slots = att_cap
    head_rows = columns * slots
    block = (2, owners, slots, piece)
    (
        first_full,
        out_full,
        normed,
        gains,
        inv_one,
        queries,
        keys,
        values,
        row_info,
        cos_slot,
        sin_slot,
        place,
        mixed,
        state,
        inv_two,
        features_all,
        hidden,
        d_both,
        d_parts,
        output_part,
    ) = call_kernel(
        first_kernel,
        3,
        [
            ((dps, owners * local, 3 * HD + head_width), BF),
            ((dps, owners * local, head_width), BF),
            ((2, owners, group, width // 2), BF),
            ((2, width), F32),
            ((group, 1), F32),
            ((owners, head_rows, HD), BF),
            ((seq_len, HD), BF),
            ((seq_len, HD), BF),
            ((owners * head_rows, HD), F32),
            ((rows, HD), F32),
            ((rows, HD), F32),
            ((owners, slots, group), BF),
            ((rows, head_width), BF),
            ((group, width), F32),
            ((group, 1), F32),
            ((dps, owners * used, 2 * piece), BF),
            ((owners * used, units), BF),
            ((2, owners * used, units), BF),
            ((2,) + block, BF),
            ((group, piece), BF),
        ],
        [
            ((dps, owners * used, 2 * piece), BF),
            ((2, owners, slots, width // 2), BF),
            ((2, owners, slots, width // 2), BF),
            ((owners, 8, group), F32),
            ((owners, owners, group), F32),
            ((owners, group, 1), F32),
            ((owners, head_rows, HD), BF),
            ((owners, head_rows, HD), BF),
            ((owners, head_rows, HD), BF),
        ]
        + [(block, BF)] * 5
        + [
            ((shares, group, piece), BF),
            ((owners, slots, width // 2), BF),
            ((owners, slots, width // 2), BF),
            ((2, dps, width // dps, units), BF),
            ((dps, units, piece), BF),
            ((2, owners * used, units), F32),
        ],
        [20, 20, 5, 2 * owners, 2 * owners]
        + [owners] * 4
        + [9, 9]
        + [owners] * 4
        + [2 * owners] * 4
        + [shares, shares]
        + [owners] * 4
        + [dps, dps],
        [
            tokens[0],
            marks,
            pack_one,
            pack_two,
            gate_weight[0],
            up_weight[0],
            down_weight[0],
            cotangent[0],
            jnp.transpose(place_ffn, (2, 0, 1)).reshape(group, -1),
            gate_slot.reshape(-1, 1),
            pick_att.reshape(TOPK, group, rows),
            att_gate.T[:, :, None],
            pick_ffn.reshape(TOPK, group, rows),
            ffn_gate.T[:, :, None],
            ends,
            cos_key,
            sin_key,
        ],
        far_args=(2, 3, 4, 5, 6),
        far_outs=(15,),
    )

    def scatter(grad):
        return lax.psum_scatter(grad.astype(BF), "dp", scatter_dimension=0, tiled=True)

    d_state, d_gain_two, d_rows, d_proj, hidden_all, d_both_all = call_kernel(
        middle_kernel,
        1,
        [
            ((group, width), F32),
            ((1, width), F32),
            ((2, owners, slots, width // 2), BF),
            ((seq_len, head_width + HD), BF),
            ((dps, owners * used, units), BF),
            ((dps, 2 * owners * used, units), BF),
        ],
        [
            (block, BF),
            (block, BF),
            (block, BF),
            ((shares, group, piece), BF),
            ((owners, slots, width // 2), BF),
            ((owners, columns * slots, HD), BF),
            ((owners, columns * slots, HD), BF),
            ((owners, columns * slots, HD), BF),
            ((owners, columns * slots, HD), BF),
            ((seq_len, HD), BF),
            ((seq_len, HD), BF),
            ((seq_len, HD), F32),
            ((seq_len, HD), F32),
        ],
        [3, 3, 2 * owners, 2 * owners, shares, shares] + [owners] * 6 + [10, 8],
        [
            d_parts,
            jnp.transpose(place_ffn, (2, 0, 1)).reshape(group, -1),
            state,
            inv_two,
            cotangent[0],
            gains,
            jnp.transpose(pick_att, (2, 3, 0, 1)).reshape(rows, -1),
            att_gate.T[:, :, None],
            out_full,
            queries,
            keys,
            values,
            row_info,
            cos_slot,
            sin_slot,
            cos_key,
            -sin_key,
            place,
            hidden,
            d_both.reshape(2 * owners * used, units),
        ],
        far_args=(18, 19),
        far_outs=(4, 5),
    )
    output, input_grad, d_gain_one = call_kernel(
        last_kernel,
        2,
        [((group, width), BF), ((group, width), F32), ((1, width), F32)],
        [((2, owners, group, piece), BF)] * 4 + [((shares, 2, group, piece), BF)],
        [2, 2, 2 * owners, 2 * owners, shares, shares],
        [d_proj, first_full, output_part, tokens[0], inv_one, gains, d_state],
    )
    normed = normed.reshape(2, seq_len, width // 2)
    out_grad = scatter(dot("kcd,ch->kdh", d_rows.reshape(2, rows, -1), mixed).reshape(width, -1))
    out_grad = swap(out_grad.reshape(owners, local, head_width), "expert")
    out_grad = jnp.swapaxes(out_grad, 1, 2).astype(F32)

    slices = features_all.reshape(-1, 2 * piece)
    d_both_all = d_both_all.reshape(dps, 2, -1, units)
    down_grad = dot("cf,cd->fd", hidden_all.reshape(-1, units), slices[:, piece:])[None]
    inputs_all = features_all[:, :, :piece]
    gate_grad = dot("scd,scf->df", inputs_all, d_both_all[:, 0])[None]
    up_grad = dot("scd,scf->df", inputs_all, d_both_all[:, 1])[None]
    map_grad = scatter(dot("std,th->sdh", normed, d_proj).reshape(width, -1))
    map_grad = map_grad.reshape(owners, local, -1)
    map_grad = swap(map_grad, "expert").astype(F32)
    query_grad = map_grad[:, :, :head_width]
    kv_grad = jnp.transpose(
        map_grad[:, :, head_width:].reshape(columns, 2, local, HD), (2, 1, 0, 3)
    ).reshape(local, 2, head_width)
    gain_grads = jnp.stack([d_gain_one[0], d_gain_two[0]]).reshape(2, dps * owners, local)
    gain_grads = jnp.sum(swap(jnp.swapaxes(gain_grads, 0, 1), ("dp", "expert")), 0)
    return (
        output[None],
        input_grad[None],
        kv_grad,
        query_grad,
        out_grad,
        gain_grads[0],
        gain_grads[1],
        gate_grad,
        up_grad,
        down_grad,
    )


def solution(mesh):
    in_specs = (
        P("dp", "expert", None),
        P("dp", "expert", None),
        P("dp", None),
        P("dp", "expert", None),
        P("dp", "expert", None),
        P("dp", "expert", None),
        P("dp", "expert", None),
        P(("dp", "expert"), None, "tensor"),
        P(None, ("dp", "expert"), "tensor"),
        P(None, "tensor", ("dp", "expert")),
        P(("dp", "expert")),
        P(("dp", "expert")),
        P("expert", "dp", "tensor"),
        P("expert", "dp", "tensor"),
        P("expert", "tensor", "dp"),
    )
    out_specs = (
        P("dp", "expert", None),
        P("dp", "expert", None),
        P(("dp", "expert"), None, "tensor"),
        P(None, ("dp", "expert"), "tensor"),
        P(None, "tensor", ("dp", "expert")),
        P(("dp", "expert")),
        P(("dp", "expert")),
        P("expert", "dp", "tensor"),
        P("expert", "dp", "tensor"),
        P("expert", "tensor", "dp"),
    )
    return jax.shard_map(
        per_device, mesh=mesh, in_specs=in_specs, out_specs=out_specs, check_vma=False
    )
```

```python
import jax
import jax.numpy as jnp
import numpy as np
from jax import lax
from jax.experimental import pallas as pl
from jax.experimental.pallas import tpu as pltpu
from jax.sharding import PartitionSpec as P

HD = 128
ATT_EXP = 8
TOPK = 2
EPSILON = 1e-06
BF = jnp.bfloat16
F32 = jnp.float32


def dot(spec, left, right):
    return jnp.einsum(spec, left, right, preferred_element_type=F32)


def swap(blocks, axes):
    return lax.all_to_all(blocks, axes, split_axis=0, concat_axis=0, tiled=True)


def slot_places(routes, expert_count, capacity):
    length = routes.shape[-2]
    names = jnp.arange(expert_count, dtype=jnp.int32)[:, None]
    member = jnp.any(jnp.swapaxes(routes, -1, -2)[..., None, :] == names, -3)
    order = jnp.arange(length)
    before = (order[:, None] < order[None, :]).astype(BF)
    rank = dot("...et,tu->...eu", member.astype(BF), before)
    slots = jnp.arange(capacity, dtype=F32)[:, None]
    return (member[..., None, :] & (rank[..., None, :] == slots)).astype(BF)


def remote(src, dst, send, recv, device):
    return pltpu.make_async_remote_copy(
        src_ref=src,
        dst_ref=dst,
        send_sem=send,
        recv_sem=recv,
        device_id=device,
        device_id_type=pl.DeviceIdType.MESH,
    )


def each(count, body, start=1):
    def step(index, carry):
        body(index)
        return carry

    lax.fori_loop(start, count, step, 0)


def mm(left, right, left_dim=1, right_dim=0, precision=None):
    return lax.dot_general(
        left,
        right,
        (((left_dim,), (right_dim,)), ((), ())),
        precision=precision,
        preferred_element_type=F32,
    )


def enter(own, half, core, owners, around=(), greeted=0):
    semaphore = pltpu.get_barrier_semaphore()
    for index in around:
        pl.semaphore_signal(
            semaphore, inc=1, device_id={"dp": index}, device_id_type=pl.DeviceIdType.MESH
        )

    def hello(expert, tensor):
        pl.semaphore_signal(
            semaphore,
            inc=1,
            device_id={"expert": expert, "tensor": tensor},
            device_id_type=pl.DeviceIdType.MESH,
        )

    def column(step):
        hello(
            lax.rem(own + lax.div(step, 2), owners),
            2 * lax.rem(half + lax.rem(step, 2), 2) + core,
        )

    each(2 * owners, column)
    hello(own, 2 * half + 1 - core)
    hello(own, 2 * (1 - half) + 1 - core)
    pl.semaphore_wait(semaphore, 2 * owners + 1 + len(around) + greeted)


def send_home(merged, landing, sends, recvs, own, half, core, owners):
    def outgoing(step):
        to, side = lax.rem(own + lax.div(step, 2), owners), lax.rem(half + lax.rem(step, 2), 2)
        return remote(
            merged.at[side, to],
            landing.at[half, own],
            sends.at[step],
            recvs.at[step],
            {"expert": to, "tensor": 2 * side + core},
        )

    each(2 * owners, lambda step: outgoing(step).start())
    landing[half, own] = merged[half, own]
    return outgoing


def wait_home(outgoing, owners):
    each(2 * owners, lambda step: outgoing(step).wait())


def share_slices(slices, sends, recvs, own, share, shares):
    def copy(step):
        return remote(
            slices.at[share],
            slices.at[share],
            sends.at[step],
            recvs.at[step],
            {"expert": own, "tensor": lax.rem(share + step, shares)},
        )

    each(shares, lambda step: copy(step).start())
    each(shares, lambda step: copy(step).wait())


class Ring:
    def __init__(self, buffer, sends, recvs, base, index, count):
        self.buffer, self.sends, self.recvs, self.base = buffer, sends, recvs, base
        self.index = index
        self.after, self.before = lax.rem(index + 1, count), lax.rem(index + count - 1, count)
        self.cut = buffer.shape[1] // 2

    def copy(self, kind, source=None):
        buffer, cut = self.buffer, self.cut
        if kind < 2:
            src = buffer.at[self.index] if source is None else source
            dst = buffer.at[self.index]
        elif kind == 2:
            src = dst = buffer.at[self.before, pl.ds(0, cut)]
        else:
            src = dst = buffer.at[self.after, pl.ds(cut, cut)]
        place = self.base + kind
        device = {"dp": self.after if kind % 2 == 0 else self.before}
        return remote(src, dst, self.sends.at[place], self.recvs.at[place], device)

    def start(self, source=None):
        self.copy(0, source).start()
        self.copy(1, source).start()

    def forward(self):
        self.copy(0).wait_recv()
        self.copy(2).start()
        self.copy(1).wait_recv()
        self.copy(3).start()

    def finish(self):
        self.copy(2).wait_recv()
        self.copy(3).wait_recv()

    def drain(self, source=None):
        self.copy(0, source).wait_send()
        self.copy(1, source).wait_send()
        self.copy(2).wait_send()
        self.copy(3).wait_send()


def first_kernel(
    tokens,
    marks,
    own_gains,
    pack_one,
    pack_two,
    gate_weight,
    up_weight,
    down_weight,
    upstream,
    sel_ffn,
    gate_slot,
    pick_att,
    att_gate,
    pick_ffn,
    ffn_gate,
    ends,
    cos_key,
    sin_key,
    first_full,
    out_full,
    normed,
    gains,
    inv_one,
    queries,
    pairs,
    row_info,
    cos_slot,
    sin_slot,
    place,
    mixed,
    state,
    inv_two,
    features_all,
    hidden,
    d_both,
    d_parts,
    output_part,
    features,
    expert_in,
    expert_grad,
    routes,
    gain_parts,
    slot_keys,
    inv_all,
    heads_out,
    mixed_out,
    mixed_in,
    far,
    near,
    sibling,
    landing,
    landing_two,
    slices,
    rows_out,
    grads_out,
    gate_up,
    down,
    act,
    ring_send,
    ring_recv,
    local,
    pack_send,
    pack_recv,
    token_send,
    token_recv,
    mark_send,
    mark_recv,
    one_send,
    one_recv,
    head_send,
    head_recv,
    back_send,
    back_recv,
    home_send,
    home_recv,
    home_two_send,
    home_two_recv,
    slice_send,
    slice_recv,
    row_send,
    row_recv,
    grad_send,
    grad_recv,
    feature_send,
    feature_recv,
    gain_send,
    gain_recv,
):
    own, share, dp = lax.axis_index("expert"), lax.axis_index("tensor"), lax.axis_index("dp")
    owners, shares, dps = heads_out.shape[0], slices.shape[0], first_full.shape[0]
    half, core = lax.div(share, 2), lax.rem(share, 2)
    group, piece = slices.shape[1], slices.shape[2]
    width = shares * piece
    wide = width // 2
    slots = rows_out.shape[1]
    rows = owners * slots
    head_rows = heads_out.shape[1]
    columns = owners // 2
    part = lax.rem(own, 2)
    local_rows = pack_one.shape[1]
    units = gate_weight.shape[1]
    other = {"expert": own, "tensor": 2 * half + 1 - core}
    enter(own, half, core, owners, [lax.rem(dp + step, dps) for step in range(1, dps)])

    down_ring = Ring(down, ring_send, ring_recv, 0, dp, dps)
    one_ring = Ring(first_full, ring_send, ring_recv, 4, dp, dps)
    two_ring = Ring(out_full, ring_send, ring_recv, 8, dp, dps)
    up_ring = Ring(gate_up.at[1], ring_send, ring_recv, 12, dp, dps)
    low, high = pl.ds(0, piece // 2), pl.ds(piece // 2, piece // 2)
    low_ring = Ring(gate_up.at[0, :, low], ring_send, ring_recv, 16, dp, dps)
    high_ring = Ring(gate_up.at[0, :, high], ring_send, ring_recv, 20, dp, dps)
    own_rows = pl.ds(pl.multiple_of(own * local_rows, local_rows), local_rows)

    def to_owner(src, dst, sends, recvs, step):
        to = lax.rem(own + step, owners)
        device = {"expert": to, "tensor": share}
        return remote(src(to), dst, sends.at[step], recvs.at[step], device)

    def pack_copy(step):
        return to_owner(pack_one.at.__getitem__, first_full.at[dp, own_rows], pack_send, pack_recv, step)

    def second_copy(step):
        to = lax.rem(own + step, owners)
        return remote(
            pack_two.at[to],
            out_full.at[dp, own_rows],
            pack_send.at[owners + step],
            pack_recv.at[owners + step],
            {"expert": to, "tensor": share},
        )

    def token_copy(step):
        start = pl.multiple_of(core * wide, wide)
        return to_owner(
            lambda to: tokens.at[:, pl.ds(start, wide)],
            normed.at[core, own],
            token_send,
            token_recv,
            step,
        )

    def mark_copy(step):
        return to_owner(lambda to: marks, routes.at[own], mark_send, mark_recv, step)

    each(owners, lambda step: pack_copy(step).start())
    each(owners, lambda step: mark_copy(step).start())

    def gain_copy(step):
        return to_owner(lambda to: own_gains, gain_parts.at[dp, own], gain_send, gain_recv, step)

    def far_gain_copy(step):
        to = lax.rem(dp + step, dps)
        place = owners + step
        return remote(
            gain_parts.at[dp],
            gain_parts.at[dp],
            gain_send.at[place],
            gain_recv.at[place],
            {"dp": to},
        )

    gain_parts[dp, own] = own_gains[...]
    each(owners, lambda step: gain_copy(step).start())
    low_ring.start(gate_weight.at[low])
    own_copies = [
        pltpu.make_async_copy(pack_one.at[own], first_full.at[dp, own_rows], local.at[0]),
        pltpu.make_async_copy(pack_two.at[own], out_full.at[dp, own_rows], local.at[1]),
        pltpu.make_async_copy(gate_weight, gate_up.at[0, dp], local.at[2]),
        pltpu.make_async_copy(up_weight, gate_up.at[1, dp], local.at[3]),
        pltpu.make_async_copy(down_weight, down.at[dp], local.at[4]),
    ]
    for copy in own_copies:
        copy.start()
    routes[own] = marks[...]
    normed[core, own] = tokens[:, pl.ds(pl.multiple_of(core * wide, wide), wide)]

    own_copies[0].wait()
    each(owners, lambda step: pack_copy(step).wait())
    one_ring.start()
    high_ring.start(gate_weight.at[high])
    each(owners, lambda step: token_copy(step).start())
    each(owners, lambda step: second_copy(step).start())
    each(owners, lambda step: mark_copy(step).wait())
    each(owners, lambda step: gain_copy(step).wait())
    each(dps, lambda step: far_gain_copy(step).start())

    def picked_rows(source, out, scale):
        for index in range(2):
            cut = pl.ds(pl.multiple_of(core * wide + index * piece, piece), piece)
            taken = mm(sel_ffn[...], source[:, cut], 0, 0)
            if scale is not None:
                taken = taken * scale
            taken = taken.astype(BF).reshape(owners, slots, piece)
            out[:, :, index * piece : (index + 1) * piece] = taken

    picked_rows(upstream, grads_out, gate_slot[...])

    def grad_copy(step):
        return to_owner(grads_out.at.__getitem__, expert_grad.at[core, own], grad_send, grad_recv, step)

    token_rows = lax.broadcasted_iota(jnp.int32, (group, group), 0)
    token_columns = lax.broadcasted_iota(jnp.int32, (group, group), 1)
    before = (token_rows < token_columns).astype(F32).astype(BF)
    token_names = token_rows.astype(F32).astype(BF)
    slot_names = lax.broadcasted_iota(jnp.int32, (slots, group), 0).astype(F32)
    first_routes = jnp.concatenate([routes[index, 0:1, :] for index in range(owners)], 0)
    second_routes = jnp.concatenate([routes[index, 1:2, :] for index in range(owners)], 0)

    def map_keys(name):
        member = (first_routes == name) | (second_routes == name)
        rank = mm(jnp.where(member, 1.0, 0.0).astype(BF), before)
        return jnp.where(member, rank, -1.0)

    for name in range(owners):
        slot_keys[name] = map_keys(float(name))

    def one_hot(name, block):
        key = slot_keys[name, pl.ds(block, 1), :]
        return jnp.where(key == slot_names, 1.0, 0.0)

    def table(hot, array, block):
        span = pl.ds(pl.multiple_of(block * group, group), group)
        return mm(hot, array[span, :], precision=lax.Precision.HIGHEST)

    def row_block(index, carry):
        name, block = lax.div(index, columns), part * columns + lax.rem(index, columns)
        hot = one_hot(name, block)
        pos = mm(hot.astype(BF), token_names) + (block * group).astype(F32)
        start = jnp.zeros_like(pos)
        for end in range(ends.shape[0]):
            bound = ends[end : end + 1, :]
            start = jnp.maximum(start, jnp.where(bound <= pos, bound, 0.0))
        span = pl.ds(pl.multiple_of(index * slots, slots), slots)
        row_info[span, 0:1] = pos[:, 0:1]
        row_info[span, 1:2] = start[:, 0:1]
        return carry

    lax.fori_loop(0, owners * columns, row_block, 0)

    each(owners, lambda step: token_copy(step).wait())
    across = remote(normed.at[core], normed.at[core], one_send.at[0], one_recv.at[0], other)
    across.start()
    each(owners, lambda step: grad_copy(step).start())
    expert_grad[core, own] = grads_out[own]
    own_copies[1].wait()
    each(owners, lambda step: second_copy(step).wait())
    one_ring.forward()
    two_ring.start()
    low_ring.forward()
    up_ring.start(up_weight)
    across.wait()

    def squares(index, carry):
        low, high = normed[0, index].astype(F32), normed[1, index].astype(F32)
        total = jnp.sum(low * low, 1, keepdims=True) + jnp.sum(high * high, 1, keepdims=True)
        inv_all[index] = lax.rsqrt(total / width + EPSILON)
        return carry

    lax.fori_loop(0, owners, squares, 0)
    inv_one[...] = inv_all[own]
    one_ring.finish()

    each(dps, lambda step: far_gain_copy(step).wait())
    left = lax.broadcasted_iota(jnp.int32, (8, HD), 1) < HD // 2
    for index in range(dps * owners // 2):
        name, side = index // columns, 2 * (index % columns)
        turned = pltpu.roll(gain_parts[name, side + 1], HD // 2, 1)
        joined = jnp.where(left, gain_parts[name, side], turned)
        gains[:, index * HD : (index + 1) * HD] = joined[0:2, :]

    chosen = expert_in
    def norm_block(index, carry):
        hot = one_hot(own, index)
        place[index] = hot.astype(BF)
        span = pl.ds(pl.multiple_of(index * slots, slots), slots)
        cos_slot[span, :] = table(hot, cos_key, index)
        sin_slot[span, :] = table(hot, sin_key, index)
        for side in range(2):
            cut = slice(side * wide, (side + 1) * wide)
            rounded = normed[side, index].astype(F32) * inv_all[index] * gains[0:1, cut]
            rounded = rounded.astype(BF)
            normed[side, index] = rounded
            chosen[side, index] = mm(hot.astype(BF), rounded).astype(BF)
        return carry

    lax.fori_loop(0, owners, norm_block, 0)
    query = jnp.zeros((rows, columns * HD), F32)
    for index in range(dps):
        cut = slice((index % 2) * piece, (index % 2 + 1) * piece)
        taken = chosen[index // 2, :, :, cut].reshape(rows, piece)
        query = query + mm(taken, first_full[index, :, HD:])
    for column in range(columns):
        head = query[:, column * HD : (column + 1) * HD]
        head = (head * cos_slot[...] + pltpu.roll(head, HD // 2, 1) * sin_slot[...]).astype(BF)
        for side in range(2):
            heads_out[2 * column + side] = head[side * head_rows : (side + 1) * head_rows]

    def head_copy(step):
        return to_owner(heads_out.at.__getitem__, queries.at[own], head_send, head_recv, step)

    each(owners, lambda step: head_copy(step).start())
    queries[own] = heads_out[own]

    first = part == 0

    def key_block(index, carry):
        taken = jnp.zeros((group, HD), F32)
        for step in range(dps):
            cut = slice((step % 2) * piece, (step % 2 + 1) * piece)
            taken = taken + mm(normed[step // 2, index, :, cut], first_full[step, :, :HD])
        span = pl.ds(pl.multiple_of(index * group, group), group)
        turned = taken * cos_key[span, :] + pltpu.roll(taken, HD // 2, 1) * sin_key[span, :]
        pairs[part, span, :] = jnp.where(first, turned, taken).astype(BF)
        return carry

    lax.fori_loop(0, owners, key_block, 0)
    pair = {"expert": own + 1 - 2 * part, "tensor": share}
    swapped = remote(pairs.at[part], pairs.at[part], one_send.at[10], one_recv.at[10], pair)
    swapped.start()

    scale = HD ** (-0.5)
    key_pos = lax.broadcasted_iota(jnp.int32, (1, owners * group), 1).astype(F32)

    def attend(index):
        span = pl.ds(pl.multiple_of(index * head_rows, head_rows), head_rows)
        scores = mm(queries[index], pairs[0], 1, 1) * scale
        visible = (key_pos <= row_info[span, 0:1]) & (key_pos >= row_info[span, 1:2])
        scores = jnp.where(visible, scores, -1e30)
        top = jnp.max(scores, 1, keepdims=True)
        shifted = jnp.exp(scores - top)
        total = jnp.sum(shifted, 1, keepdims=True)
        row_info[span, 2:3] = top + jnp.log(total)
        probs = (shifted / total).astype(BF)
        mixed_out[index] = mm(probs, pairs[1]).astype(BF)

    def back_copy(step):
        to = lax.rem(own + owners - step, owners)
        return remote(
            mixed_out.at[to],
            mixed_in.at[own],
            back_send.at[step],
            back_recv.at[step],
            {"expert": to, "tensor": share},
        )

    def attend_other(step):
        head_copy(step).wait()
        attend(lax.rem(own + owners - step, owners))
        back_copy(step).start()

    swapped.wait()
    attend(own)
    mixed_in[own] = mixed_out[own]
    each(owners, attend_other)
    two_ring.forward()
    high_ring.forward()
    down_ring.start(down_weight)
    two_ring.finish()
    each(owners, lambda step: back_copy(step).wait())
    for column in range(columns):
        for side in range(2):
            mixed[
                side * head_rows : (side + 1) * head_rows, column * HD : (column + 1) * HD
            ] = mixed_in[2 * column + side]

    def chip_sum(product, far, near, sibling, base):
        def across(side):
            place = base + side
            return remote(far.at[side], sibling.at[side], one_send.at[place], one_recv.at[place], other)

        for side in range(2):
            far[side] = product(2 * side + 1 - core)
            across(side).start()
        for side in range(2):
            near[side] = product(2 * side + core)
        for side in range(2):
            across(side).wait()
            near[side] = (near[side].astype(F32) + sibling[side].astype(F32)).astype(BF)

    def at_tokens(pick, gate, landing):
        total = jnp.zeros((group, piece), F32)
        for choice in range(TOPK):
            taken = mm(pick[choice], landing[0].reshape(rows, piece))
            taken = taken + mm(pick[choice], landing[1].reshape(rows, piece))
            total = total + gate[choice] * taken
        return total

    def map_product(index):
        return mm(mixed[...], out_full[index], 1, 1).astype(BF).reshape(owners, slots, piece)

    chip_sum(map_product, far, near, sibling, 1)
    outgoing = send_home(near, landing, home_send, home_recv, own, half, core, owners)
    up_ring.forward()
    wait_home(outgoing, owners)
    slices[share] = at_tokens(pick_att, att_gate, landing).astype(BF)
    share_slices(slices, slice_send, slice_recv, own, share, shares)

    total = jnp.zeros((group, 1), F32)
    for index in range(shares):
        cut = slice(index * piece, (index + 1) * piece)
        value = tokens[:, cut].astype(F32) + slices[index].astype(F32)
        state[:, cut] = value
        total = total + jnp.sum(value * value, 1, keepdims=True)
    inv = lax.rsqrt(total / width + EPSILON)
    inv_two[...] = inv
    for index in range(2):
        cut = pl.ds(pl.multiple_of(core * wide + index * piece, piece), piece)
        rounded = (state[:, cut] * inv * gains[1:2, cut]).astype(BF)
        taken = mm(sel_ffn[...], rounded, 0, 0).astype(BF).reshape(owners, slots, piece)
        rows_out[:, :, index * piece : (index + 1) * piece] = taken

    def row_copy(step):
        return to_owner(rows_out.at.__getitem__, expert_in.at[core, own], row_send, row_recv, step)

    each(owners, lambda step: row_copy(step).start())
    expert_in[core, own] = rows_out[own]
    each(owners, lambda step: grad_copy(step).wait())
    across = remote(expert_grad.at[core], expert_grad.at[core], one_send.at[5], one_recv.at[5], other)
    across.start()
    each(owners, lambda step: row_copy(step).wait())
    across_rows = remote(expert_in.at[core], expert_in.at[core], one_send.at[6], one_recv.at[6], other)
    across_rows.start()
    across.wait()
    across_rows.wait()

    used = hidden.shape[0] // owners

    def tight(array):
        pieces = [array[index * slots : index * slots + used] for index in range(owners)]
        return jnp.concatenate(pieces, 0)

    def loose(array):
        blank = jnp.zeros((slots - used, array.shape[1]), F32)
        pieces = []
        for index in range(owners):
            pieces += [array[index * used : (index + 1) * used], blank]
        return jnp.concatenate(pieces, 0).astype(BF).reshape(owners, slots, piece)

    for index in range(dps):
        cut = slice((index % 2) * piece, (index % 2 + 1) * piece)
        for side, source in enumerate((expert_in, expert_grad)):
            taken = source[index // 2, :, :, cut].reshape(rows, piece).astype(F32)
            features[side, index] = tight(taken).astype(BF)
    def feature_copy(step):
        to = lax.rem(dp + step, dps)
        return remote(
            features.at[core, to],
            features_all.at[core, dp],
            feature_send.at[step],
            feature_recv.at[step],
            {"dp": to},
        )

    keep = pltpu.make_async_copy(features.at[core, dp], features_all.at[core, dp], feature_send.at[0])
    keep.start()
    for copy in own_copies[2:]:
        copy.wait()
    tile = 2 * HD

    def unit_tiles(body):
        def step(index, carry):
            body(pl.ds(pl.multiple_of(index * tile, tile), tile))
            return carry

        lax.fori_loop(0, units // tile, step, 0)
        if units % tile:
            body(pl.ds(units - units % tile, units % tile))

    low_ring.finish()
    high_ring.finish()

    def gate_tile(cut):
        total = mm(features[0, 0], gate_up[0, 0, :, cut])
        for index in range(1, dps):
            total = total + mm(features[0, index], gate_up[0, index, :, cut])
        act[0, :, cut] = total

    unit_tiles(gate_tile)
    down_ring.forward()
    up_ring.finish()

    def up_tile(cut):
        up = mm(features[0, 0], gate_up[1, 0, :, cut])
        for index in range(1, dps):
            up = up + mm(features[0, index], gate_up[1, index, :, cut])
        act[1, :, cut] = up
        gate = act[0, :, cut]
        hidden[:, cut] = (gate / (1.0 + jnp.exp(-gate)) * up).astype(BF)

    unit_tiles(up_tile)
    down_ring.finish()
    each(dps, lambda step: feature_copy(step).start())
    chip_sum(lambda index: loose(mm(hidden[...], down[index])), far, near, sibling, 7)
    outgoing_two = send_home(
        near, landing_two, home_two_send, home_two_recv, own, half, core, owners
    )

    def grad_tile(cut):
        grad = mm(features[1, 0], down[0, cut, :], 1, 1)
        for index in range(1, dps):
            grad = grad + mm(features[1, index], down[index, cut, :], 1, 1)
        gate, up = act[0, :, cut], act[1, :, cut]
        sigma = 1.0 / (1.0 + jnp.exp(-gate))
        d_both[0, :, cut] = (grad * up * sigma * (1.0 + gate * (1.0 - sigma))).astype(BF)
        d_both[1, :, cut] = (grad * gate * sigma).astype(BF)

    unit_tiles(grad_tile)
    for index in range(dps):
        total = mm(d_both[0], gate_up[0, index], 1, 1) + mm(d_both[1], gate_up[1, index], 1, 1)
        d_parts[index % 2, index // 2] = loose(total)
    keep.wait()
    each(dps, lambda step: feature_copy(step).wait())
    across = remote(
        features_all.at[core], features_all.at[core], one_send.at[9], one_recv.at[9], other
    )
    across.start()
    wait_home(outgoing_two, owners)
    rest = at_tokens(pick_ffn, ffn_gate, landing_two)
    span = pl.ds(pl.multiple_of(share * piece, piece), piece)
    output_part[...] = (state[:, span] + rest).astype(BF)
    across.wait()
    one_ring.drain()
    two_ring.drain()
    low_ring.drain(gate_weight.at[low])
    high_ring.drain(gate_weight.at[high])
    up_ring.drain(up_weight)
    down_ring.drain(down_weight)


def back_kernel(
    parts,
    sel_ffn,
    state,
    inv_two,
    upstream,
    gains,
    sel_att,
    att_gate,
    out_full,
    queries,
    pairs,
    row_info,
    cos_slot,
    sin_slot,
    cos_key,
    sin_key,
    place,
    d_both,
    hidden,
    output_part,
    tokens,
    inv_one,
    mixed,
    far_weights,
    far_normed,
    far_features,
    output,
    input_grad,
    gain_grads,
    query_grad,
    out_grad,
    kv_grad,
    gate_grad,
    up_grad,
    down_grad,
    d_both_all,
    hidden_all,
    d_gain_two,
    d_rows,
    d_proj,
    return_in,
    parts_joined,
    rows_out,
    heads_out,
    heads_in,
    queries_out,
    queries_in,
    pair_out,
    pair_in,
    d_keys,
    d_values,
    far,
    near,
    sibling,
    landing,
    slices,
    map_grads,
    early,
    late,
    maps_in,
    gain_out,
    gain_in,
    weights,
    normed,
    features,
    acts,
    features_turned,
    wide_tiles,
    tall_tiles,
    first_send,
    first_recv,
    return_send,
    return_recv,
    join_send,
    join_recv,
    row_send,
    row_recv,
    head_send,
    head_recv,
    back_send,
    back_recv,
    ring_send,
    ring_recv,
    local,
    one_send,
    one_recv,
    home_send,
    home_recv,
    slice_send,
    slice_recv,
    step_send,
    step_recv,
    map_send,
    map_recv,
    gain_send,
    gain_recv,
    tile_sem,
):
    own, share = lax.axis_index("expert"), lax.axis_index("tensor")
    owners, shares = heads_out.shape[0], parts_joined.shape[0]
    half, core = lax.div(share, 2), lax.rem(share, 2)
    piece, width = parts_joined.shape[2], state.shape[1]
    slots = rows_out.shape[1]
    rows = owners * slots
    wide = width // 2
    head_rows = heads_out.shape[1]
    columns = owners // 2
    other = {"expert": own, "tensor": 2 * half + 1 - core}
    dp, dps = lax.axis_index("dp"), d_both_all.shape[0]

    def owner_at(step):
        return lax.rem(dp + lax.div(step, owners), dps), lax.rem(own + lax.rem(step, owners), owners)

    def hello(step):
        to_dp, to = owner_at(step)
        pl.semaphore_signal(
            pltpu.get_barrier_semaphore(),
            inc=1,
            device_id={"dp": to_dp, "expert": to},
            device_id_type=pl.DeviceIdType.MESH,
        )

    each(dps * owners, hello)
    enter(own, half, core, owners, greeted=dps * owners - 1)
    loads = [
        pltpu.make_async_copy(far_weights, weights, local.at[4]),
        pltpu.make_async_copy(far_normed, normed, local.at[5]),
        pltpu.make_async_copy(far_features.at[1], features, local.at[6]),
        pltpu.make_async_copy(far_features.at[0], acts.at[:, :, pl.ds(0, width // shares)], local.at[2]),
    ]
    for copy in loads:
        copy.start()

    both_ring = Ring(d_both_all, ring_send, ring_recv, 0, dp, dps)
    both_ring.start(d_both)
    hidden_ring = Ring(hidden_all, ring_send, ring_recv, 4, dp, dps)
    hidden_ring.start(hidden)
    keeps = [
        pltpu.make_async_copy(d_both, d_both_all.at[dp], local.at[0]),
        pltpu.make_async_copy(hidden, hidden_all.at[dp], local.at[7]),
    ]
    for copy in keeps:
        copy.start()

    used_slots = pl.ds(0, slots)
    return_near, return_out = sibling.at[:, :, used_slots], near.at[:, :, used_slots]
    across = remote(parts.at[1 - core], return_near, first_send.at[0], first_recv.at[0], other)
    across.start()
    across.wait()
    for side in range(2):
        return_out[side] = (parts[core, side].astype(F32) + return_near[side].astype(F32)).astype(BF)
    outgoing = send_home(return_out, return_in, return_send, return_recv, own, half, core, owners)
    wait_home(outgoing, owners)
    total = mm(sel_ffn[...], return_in[0].reshape(rows, piece))
    total = total + mm(sel_ffn[...], return_in[1].reshape(rows, piece))
    parts_joined[share] = total.astype(BF)
    share_slices(parts_joined, join_send, join_recv, own, share, shares)

    inv = inv_two[...]
    mean = jnp.zeros_like(inv)
    for index in range(shares):
        cut = slice(index * piece, (index + 1) * piece)
        grad, value = parts_joined[index].astype(F32), state[:, cut]
        mean = mean + jnp.sum(value * gains[1:2, cut] * grad, 1, keepdims=True)
        d_gain_two[:, cut] = jnp.sum(grad * value * inv, 0, keepdims=True)
    mean = mean * (inv * inv * inv / width)
    for index in range(shares):
        cut = slice(index * piece, (index + 1) * piece)
        grad = gains[1:2, cut] * parts_joined[index].astype(F32)
        input_grad[:, cut] = upstream[:, cut].astype(F32) + inv * grad - state[:, cut] * mean

    for index in range(2):
        start = pl.multiple_of(core * wide + index * piece, piece)
        grad = input_grad[:, pl.ds(start, piece)]
        both = jnp.concatenate(
            [(att_gate[0] * grad).astype(BF), (att_gate[1] * grad).astype(BF)], 0
        )
        picked = mm(sel_att[...], both).astype(BF).reshape(owners, slots, piece)
        rows_out[:, :, index * piece : (index + 1) * piece] = picked

    def row_copy(step):
        to = lax.rem(own + step, owners)
        return remote(
            rows_out.at[to],
            d_rows.at[core, own],
            row_send.at[step],
            row_recv.at[step],
            {"expert": to, "tensor": share},
        )

    each(owners, lambda step: row_copy(step).start())
    d_rows[core, own] = rows_out[own]
    each(owners, lambda step: row_copy(step).wait())
    across = remote(d_rows.at[core], d_rows.at[core], first_send.at[1], first_recv.at[1], other)
    across.start()

    def half_product(side):
        taken = d_rows[side].reshape(rows, wide)
        return mm(taken[:, :piece], out_full[2 * side]) + mm(taken[:, piece:], out_full[2 * side + 1])

    d_mixed = half_product(core)
    across.wait()
    d_mixed = (d_mixed + half_product(1 - core)).astype(BF)
    for column in range(columns):
        for part in range(2):
            heads_out[2 * column + part] = d_mixed[
                part * head_rows : (part + 1) * head_rows, column * HD : (column + 1) * HD
            ]

    def head_copy(step):
        to = lax.rem(own + step, owners)
        return remote(
            heads_out.at[to],
            heads_in.at[own],
            head_send.at[step],
            head_recv.at[step],
            {"expert": to, "tensor": share},
        )

    each(owners, lambda step: head_copy(step).start())
    heads_in[own] = heads_out[own]

    scale = HD ** (-0.5)
    key_pos = lax.broadcasted_iota(jnp.int32, (1, pairs.shape[1]), 1).astype(F32)
    d_keys[...] = jnp.zeros_like(d_keys)
    d_values[...] = jnp.zeros_like(d_values)

    def attend(index):
        span = pl.ds(pl.multiple_of(index * head_rows, head_rows), head_rows)
        query, key, value, grad = queries[index], pairs[0], pairs[1], heads_in[index]
        scores = mm(query, key, 1, 1) * scale
        visible = (key_pos <= row_info[span, 0:1]) & (key_pos >= row_info[span, 1:2])
        probs = jnp.where(visible, jnp.exp(scores - row_info[span, 2:3]), 0.0)
        d_probs = mm(grad, value, 1, 1)
        delta = jnp.sum(probs * d_probs, 1, keepdims=True)
        d_scores = (probs * (d_probs - delta)).astype(BF)
        queries_out[index] = (mm(d_scores, key) * scale).astype(BF)
        d_keys[...] += mm(d_scores, query, 0, 0)
        d_values[...] += mm(probs.astype(BF), grad, 0, 0)

    def query_copy(step):
        to = lax.rem(own + owners - step, owners)
        return remote(
            queries_out.at[to],
            queries_in.at[own],
            back_send.at[step],
            back_recv.at[step],
            {"expert": to, "tensor": share},
        )

    def attend_other(step):
        head_copy(step).wait()
        attend(lax.rem(own + owners - step, owners))
        query_copy(step).start()

    attend(own)
    queries_in[own] = queries_out[own]
    each(owners, attend_other)
    both_ring.forward()

    first = lax.rem(own, 2) == 0
    pair_out[...] = jnp.where(first, d_values[...], d_keys[...] * scale).astype(BF)
    pair = {"expert": own + 1 - 2 * lax.rem(own, 2), "tensor": share}
    across = remote(pair_out, pair_in, first_send.at[2], first_recv.at[2], pair)
    across.start()
    each(owners, lambda step: query_copy(step).wait())
    group = place.shape[2]
    for part in range(2):
        for index in range(columns):
            block = part * columns + index
            cut = slice(index * slots, (index + 1) * slots)
            span = slice(block * slots, (block + 1) * slots)
            turned = []
            for column in range(columns):
                grad = queries_in[2 * column + part, cut, :].astype(F32)
                back = pltpu.roll(grad, HD // 2, 1) * sin_slot[span, :]
                turned.append((grad * cos_slot[span, :] - back).astype(BF))
            picked = jnp.concatenate(turned, 1)
            d_proj[block * group : (block + 1) * group, : columns * HD] = mm(
                place[block], picked, 0, 0
            ).astype(BF)
    across.wait()
    mine = jnp.where(first, d_keys[...] * scale, d_values[...]) + pair_in[...].astype(F32)
    turned = mine * cos_key[...] + pltpu.roll(mine, HD // 2, 1) * sin_key[...]
    d_proj[:, columns * HD :] = jnp.where(first, turned, mine).astype(BF)

    group, piece = near.shape[2], near.shape[3]
    head_width = d_proj.shape[1] - HD
    local_rows = maps_in.shape[1]
    used, units = acts.shape[1], acts.shape[2]
    after, before = lax.rem(dp + 1, dps), lax.rem(dp + dps - 1, dps)
    facing = lax.rem(dp + 2, dps)
    for copy in loads:
        copy.wait()
    for index in range(dps):
        features_turned[index] = jnp.transpose(acts[index, :, :piece].astype(F32)).astype(BF)

    def load(side):
        source = hidden_all if side == 2 else d_both_all.at[:, pl.ds(side * used, used)]
        return pltpu.make_async_copy(source, acts, local.at[1])

    def map_grad(index):
        cut = pl.ds(pl.multiple_of(lax.rem(index, 2) * piece, piece), piece)
        inputs = normed[lax.div(index, 2), :, :, cut].reshape(owners * group, piece)
        outs = d_rows[lax.div(index, 2), :, :, cut].reshape(-1, piece)
        return mm(inputs, d_proj[...], 0, 0), mm(outs, mixed[...], 0, 0)

    middle = head_width + HD

    def keep_grad(index):
        ins, outs = map_grad(index)
        map_grads[index, :, :middle] = ins.astype(BF)
        map_grads[index, :, middle:] = outs.astype(BF)

    cut = piece // 2

    def step_copy(kind):
        to = {"dp": after if kind % 2 == 0 else before}
        sems = (step_send.at[kind], step_recv.at[kind])
        if kind < 2:
            span = pl.ds(kind * cut, cut)
            return remote(map_grads.at[facing, span], early.at[kind], *sems, to)
        return remote(map_grads.at[after if kind == 2 else before], late.at[kind - 2], *sems, to)

    keep_grad(facing)
    step_copy(0).start()
    step_copy(1).start()

    def product(index):
        queries = mm(d_proj[:, :head_width], weights[index, :, HD:], 1, 1)
        side = mm(d_proj[:, head_width:], weights[index, :, :HD], 1, 1)
        return (queries + side).reshape(owners, group, piece)

    def across(side):
        return remote(far.at[side], sibling.at[side], one_send.at[side], one_recv.at[side], other)

    for side in range(2):
        far[side] = product(2 * side + 1 - core).astype(BF)
        across(side).start()
    for side in range(2):
        near[side] = product(2 * side + core).astype(BF)
    for side in range(2):
        across(side).wait()
        near[side] = (near[side].astype(F32) + sibling[side].astype(F32)).astype(BF)
    outgoing = send_home(near, landing, home_send, home_recv, own, half, core, owners)

    keep_grad(after)
    keep_grad(before)
    step_copy(0).wait()
    step_copy(1).wait()
    top, bottom = slice(0, cut), slice(cut, 2 * cut)
    map_grads[after, top] = (map_grads[after, top].astype(F32) + early[0].astype(F32)).astype(BF)
    map_grads[before, bottom] = (
        map_grads[before, bottom].astype(F32) + early[1].astype(F32)
    ).astype(BF)
    step_copy(2).start()
    step_copy(3).start()
    both_ring.finish()
    keeps[0].wait()
    load(0).start()
    hidden_ring.forward()

    tile = 2 * HD
    whole, rest = units // tile, units % tile
    def unit_tiles(product, out, rows_first):
        def store(slot, span, size):
            if rows_first:
                return pltpu.make_async_copy(
                    tall_tiles.at[slot, pl.ds(0, size)], out.at[span], tile_sem.at[slot]
                )
            return pltpu.make_async_copy(
                wide_tiles.at[slot, :, pl.ds(0, size)], out.at[:, span], tile_sem.at[slot]
            )

        def put(slot, value, size):
            if rows_first:
                tall_tiles[slot, :size] = value
            else:
                wide_tiles[slot, :, :size] = value

        def pair(index, carry):
            for slot in range(2):
                span = pl.ds(pl.multiple_of((2 * index + slot) * tile, tile), tile)

                @pl.when(index > 0)
                def _(slot=slot, span=span):
                    store(slot, span, tile).wait()

                put(slot, product(span), tile)
                store(slot, span, tile).start()
            return carry

        lax.fori_loop(0, whole // 2, pair, 0)
        spans = [(0, pl.ds((whole - 2) * tile, tile), tile), (1, pl.ds((whole - 1) * tile, tile), tile)]
        for slot, span, size in spans:
            store(slot, span, size).wait()
        if whole % 2:
            span = pl.ds((whole - 1) * tile, tile)
            put(0, product(span), tile)
            store(0, span, tile).start()
        if rest:
            tail = pl.ds(whole * tile, rest)
            put(1, product(tail), rest)
            store(1, tail, rest).start()
            store(1, tail, rest).wait()
        if whole % 2:
            store(0, span, tile).wait()

    def wide_product(span):
        total = mm(features_turned[0], acts[0, :, span])
        for index in range(1, dps):
            total = total + mm(features_turned[index], acts[index, :, span])
        return total

    def tall_product(span):
        total = mm(acts[0, :, span], features[0], 0, 0)
        for index in range(1, dps):
            total = total + mm(acts[index, :, span], features[index], 0, 0)
        return total

    load(0).wait()
    unit_tiles(wide_product, gate_grad, False)
    load(1).start()
    keep_grad(dp)

    step_copy(2).wait()
    step_copy(3).wait()
    map_grads[dp] = (
        map_grads[dp].astype(F32) + late[0].astype(F32) + late[1].astype(F32)
    ).astype(BF)

    def home_rows(index):
        return pl.ds(pl.multiple_of(index * local_rows, local_rows), local_rows)

    def map_copy(step):
        to = lax.rem(own + step, owners)
        return remote(
            map_grads.at[dp, home_rows(to)],
            maps_in.at[own],
            map_send.at[step],
            map_recv.at[step],
            {"expert": to, "tensor": share},
        )

    each(owners, lambda step: map_copy(step).start())
    maps_in[own] = map_grads[dp, home_rows(own), :]
    wait_home(outgoing, owners)
    total = jnp.zeros((group, piece), F32)
    for side in range(2):
        for index in range(owners):
            total = total + landing[side, index].astype(F32)
    slices[share, 0] = total.astype(BF)
    slices[share, 1] = output_part[...]
    share_slices(slices, slice_send, slice_recv, own, share, shares)
    inv = inv_one[...]
    mean = jnp.zeros_like(inv)
    for index in range(shares):
        span = slice(index * piece, (index + 1) * piece)
        grad, value = slices[index, 0].astype(F32), tokens[:, span].astype(F32)
        output[:, span] = slices[index, 1]
        mean = mean + jnp.sum(value * gains[0:1, span] * grad, 1, keepdims=True)
        gain_one = jnp.sum(grad * value * inv, 0, keepdims=True)
        for chunk in range(piece // HD):
            lanes = slice(chunk * HD, (chunk + 1) * HD)
            place = index * (piece // HD) + chunk
            gain_out[place, 0:1] = gain_one[:, lanes]
            gain_out[place, 1:2] = d_gain_two[:, place * HD : (place + 1) * HD]

    def gain_copy(step):
        to_dp, to = owner_at(step)
        return remote(
            gain_out.at[lax.div(to_dp * owners + to, HD // local_rows)],
            gain_in.at[dp * owners + own],
            gain_send.at[step],
            gain_recv.at[step],
            {"dp": to_dp, "expert": to},
        )

    each(dps * owners, lambda step: gain_copy(step).start())
    gain_in[dp * owners + own] = gain_out[lax.div(dp * owners + own, HD // local_rows)]
    mean = mean * (inv * inv * inv / width)
    for index in range(shares):
        span = slice(index * piece, (index + 1) * piece)
        grad = gains[0:1, span] * slices[index, 0].astype(F32)
        value = tokens[:, span].astype(F32)
        input_grad[:, span] = input_grad[:, span] + inv * grad - value * mean

    load(1).wait()
    unit_tiles(wide_product, up_grad, False)
    hidden_ring.finish()
    keeps[1].wait()
    load(2).start()
    each(owners, lambda step: map_copy(step).wait())
    for index in range(owners):
        query_grad[index] = maps_in[index, :, :head_width].astype(F32)
        out_grad[index] = maps_in[index, :, middle:].astype(F32)
        column = index // 2
        kv_grad[index % 2, :, column * HD : (column + 1) * HD] = maps_in[
            index, :, head_width:middle
        ].astype(F32)
    load(2).wait()
    unit_tiles(tall_product, down_grad, True)
    each(dps * owners, lambda step: gain_copy(step).wait())
    total = gain_in[0, 0:2]
    for index in range(1, dps * owners):
        total = total + gain_in[index, 0:2]
    gain_grads[...] = total
    both_ring.drain(d_both)
    hidden_ring.drain(hidden)


def call_kernel(kernel, collective_id, outs, scratch, semaphores, args, far_args=(), far_outs=()):
    def specs(count, far):
        spaces = [pl.ANY if index in far else pltpu.VMEM for index in range(count)]
        return [pl.BlockSpec(memory_space=space) for space in spaces]

    return pl.pallas_call(
        kernel,
        out_shape=[jax.ShapeDtypeStruct(shape, dtype) for shape, dtype in outs],
        in_specs=specs(len(args), far_args),
        out_specs=specs(len(outs), far_outs),
        scratch_shapes=[pltpu.VMEM(shape, dtype) for shape, dtype in scratch]
        + [pltpu.SemaphoreType.DMA((count,)) for count in semaphores],
        compiler_params=pltpu.CompilerParams(
            collective_id=collective_id, has_side_effects=True, vmem_limit_bytes=60 * 2**20
        ),
    )(*args)


def per_device(
    tokens,
    cotangent,
    doc_lengths,
    att_routes,
    att_gates,
    ffn_routes,
    ffn_gates,
    kv_weight,
    query_weight,
    out_weight,
    attn_gain,
    ffn_gain,
    gate_weight,
    up_weight,
    down_weight,
):
    _, group, width = tokens.shape
    owners = lax.axis_size("expert")
    shares = lax.axis_size("tensor")
    dps = lax.axis_size("dp")
    own = lax.axis_index("expert")
    share = lax.axis_index("tensor")
    columns = owners // 2
    column_half = own % 2
    att_cap = -(-min(group, group * TOPK * 5 // (4 * ATT_EXP)) // 16) * 16
    ffn_cap = -(-min(group, group * TOPK * 5 // (4 * owners)) // 16) * 16
    rows = owners * att_cap
    seq_len = owners * group
    piece = width // shares
    local = kv_weight.shape[0]
    head_width = kv_weight.shape[2]

    def choice_places(places_here, routes):
        names = jnp.arange(places_here.shape[0], dtype=jnp.int32)
        picks = (routes[:, :, None] == names).astype(BF)
        return jnp.einsum("mst,tjm->jtms", places_here, picks)

    place_ffn = slot_places(ffn_routes[0], owners, ffn_cap)
    pick_ffn = choice_places(place_ffn, ffn_routes[0])
    ffn_gate = ffn_gates[0]
    gate_slot = jnp.einsum("jtms,tj->ms", pick_ffn, ffn_gate, precision=lax.Precision.HIGHEST)

    kv_parts = jnp.transpose(kv_weight.reshape(local, 2, columns, HD), (2, 1, 0, 3))
    pack_one = jnp.concatenate([kv_parts.reshape(owners, local, HD), query_weight], 2)
    own_gains = jnp.stack([attn_gain, ffn_gain]).astype(F32)
    own_gains = jnp.pad(own_gains, ((0, 8 - 2), (0, HD - local)))
    pack_two = jnp.swapaxes(out_weight, 1, 2)
    marks = jnp.pad(att_routes[0].T.astype(F32), ((0, 8 - TOPK), (0, 0)), constant_values=-1.0)
    place_att = slot_places(att_routes[0], ATT_EXP, att_cap)
    pick_att = choice_places(place_att, att_routes[0])
    att_gate = att_gates[0]
    ends = jnp.cumsum(doc_lengths[0], dtype=jnp.int32).astype(F32)
    ends = jnp.broadcast_to(ends[:, None], (ends.shape[0], HD))
    angles = np.arange(seq_len)[:, None] * 10000.0 ** (-np.arange(HD // 2) * 2.0 / HD)
    cos_key = jnp.asarray(np.concatenate([np.cos(angles)] * 2, 1), F32)
    sin_key = jnp.asarray(np.concatenate([-np.sin(angles), np.sin(angles)], 1), F32)
    used = min(group, group * TOPK * 5 // (4 * owners))
    sel_ffn = jnp.transpose(place_ffn, (2, 0, 1)).reshape(group, -1)
    units = gate_weight.shape[2]
    slots = att_cap
    head_rows = columns * slots
    block = (2, owners, slots, piece)
    (
        first_full,
        out_full,
        normed,
        gains,
        inv_one,
        queries,
        pairs,
        row_info,
        cos_slot,
        sin_slot,
        place,
        mixed,
        state,
        inv_two,
        features_all,
        hidden,
        d_both,
        d_parts,
        output_part,
    ) = call_kernel(
        first_kernel,
        3,
        [
            ((dps, owners * local, HD + head_width), BF),
            ((dps, owners * local, head_width), BF),
            ((2, owners, group, width // 2), BF),
            ((2, width), F32),
            ((group, 1), F32),
            ((owners, head_rows, HD), BF),
            ((2, seq_len, HD), BF),
            ((owners * head_rows, HD), F32),
            ((rows, HD), F32),
            ((rows, HD), F32),
            ((owners, slots, group), BF),
            ((rows, head_width), BF),
            ((group, width), F32),
            ((group, 1), F32),
            ((2, dps, owners * used, piece), BF),
            ((owners * used, units), BF),
            ((2, owners * used, units), BF),
            ((2,) + block, BF),
            ((group, piece), BF),
        ],
        [
            ((2, dps, owners * used, piece), BF),
            ((2, owners, slots, width // 2), BF),
            ((2, owners, slots, width // 2), BF),
            ((owners, 8, group), F32),
            ((dps, owners, 8, HD), F32),
            ((owners, owners, group), F32),
            ((owners, group, 1), F32),
            ((owners, head_rows, HD), BF),
            ((owners, head_rows, HD), BF),
            ((owners, head_rows, HD), BF),
        ]
        + [(block, BF)] * 5
        + [
            ((shares, group, piece), BF),
            ((owners, slots, width // 2), BF),
            ((owners, slots, width // 2), BF),
            ((2, dps, width // dps, units), BF),
            ((dps, units, piece), BF),
            ((2, owners * used, units), F32),
        ],
        [24, 24, 5, 2 * owners, 2 * owners]
        + [owners] * 4
        + [11, 11]
        + [owners] * 4
        + [2 * owners] * 4
        + [shares, shares]
        + [owners] * 4
        + [dps, dps]
        + [owners + dps] * 2,
        [
            tokens[0],
            marks,
            own_gains,
            pack_one,
            pack_two,
            gate_weight[0],
            up_weight[0],
            down_weight[0],
            cotangent[0],
            sel_ffn,
            gate_slot.reshape(-1, 1),
            pick_att.reshape(TOPK, group, rows),
            att_gate.T[:, :, None],
            pick_ffn.reshape(TOPK, group, rows),
            ffn_gate.T[:, :, None],
            ends,
            cos_key,
            sin_key,
        ],
        far_args=(3, 4, 5, 6, 7),
        far_outs=(14,),
    )

    grad_width = head_width + HD + head_width
    (
        output,
        input_grad,
        gain_grads,
        query_grad,
        out_grad,
        kv_grad,
        gate_grad,
        up_grad,
        down_grad,
        *_,
    ) = call_kernel(
        back_kernel,
        1,
        [
            ((group, width), BF),
            ((group, width), F32),
            ((2, HD), F32),
            ((owners, local, head_width), F32),
            ((owners, local, head_width), F32),
            ((2, local, head_width), F32),
            ((piece, units), F32),
            ((piece, units), F32),
            ((units, piece), F32),
            ((dps, 2 * owners * used, units), BF),
            ((dps, owners * used, units), BF),
        ],
        [
            ((1, width), F32),
            ((2, owners, slots, width // 2), BF),
            ((seq_len, head_width + HD), BF),
            (block, BF),
            ((shares, group, piece), BF),
            ((owners, slots, width // 2), BF),
            ((owners, head_rows, HD), BF),
            ((owners, head_rows, HD), BF),
            ((owners, head_rows, HD), BF),
            ((owners, head_rows, HD), BF),
            ((seq_len, HD), BF),
            ((seq_len, HD), BF),
            ((seq_len, HD), F32),
            ((seq_len, HD), F32),
            ((2, owners, group, piece), BF),
            ((2, owners, group, piece), BF),
            ((2, owners, group, piece), BF),
            ((2, owners, group, piece), BF),
            ((shares, 2, group, piece), BF),
            ((dps, piece, grad_width), BF),
            ((2, piece // 2, grad_width), BF),
            ((2, piece, grad_width), BF),
            ((owners, local, grad_width), BF),
            ((width // HD, 8, HD), F32),
            ((dps * owners, 8, HD), F32),
            ((dps, owners * local, HD + head_width), BF),
            ((2, owners, group, width // 2), BF),
            ((dps, owners * used, piece), BF),
            ((dps, owners * used, units), BF),
            ((dps, piece, owners * used), BF),
            ((2, piece, 2 * HD), F32),
            ((2, 2 * HD, piece), F32),
        ],
        [
            3,
            3,
            2 * owners,
            2 * owners,
            shares,
            shares,
            owners,
            owners,
            owners,
            owners,
            owners,
            owners,
            8,
            8,
            8,
            2,
            2,
            2 * owners,
            2 * owners,
            shares,
            shares,
            4,
            4,
            owners,
            owners,
            dps * owners,
            dps * owners,
            2,
        ],
        [
            d_parts,
            sel_ffn,
            state,
            inv_two,
            cotangent[0],
            gains,
            jnp.transpose(pick_att, (2, 3, 0, 1)).reshape(rows, -1),
            att_gate.T[:, :, None],
            out_full,
            queries,
            pairs,
            row_info,
            cos_slot,
            sin_slot,
            cos_key,
            -sin_key,
            place,
            d_both.reshape(2 * owners * used, units),
            hidden,
            output_part,
            tokens[0],
            inv_one,
            mixed,
            first_full,
            normed,
            features_all,
        ],
        far_args=(17, 18, 23, 24, 25),
        far_outs=(6, 7, 8, 9, 10),
    )
    chunk = HD // local
    place = lax.rem(own, chunk) * local
    gain_grads = lax.dynamic_slice_in_dim(gain_grads, place, local, 1)
    kv_grad = jnp.swapaxes(kv_grad, 0, 1)
    out_grad = jnp.swapaxes(out_grad, 1, 2)
    return (
        output[None],
        input_grad[None],
        kv_grad,
        query_grad,
        out_grad,
        gain_grads[0],
        gain_grads[1],
        gate_grad[None],
        up_grad[None],
        down_grad[None],
    )


def solution(mesh):
    in_specs = (
        P("dp", "expert", None),
        P("dp", "expert", None),
        P("dp", None),
        P("dp", "expert", None),
        P("dp", "expert", None),
        P("dp", "expert", None),
        P("dp", "expert", None),
        P(("dp", "expert"), None, "tensor"),
        P(None, ("dp", "expert"), "tensor"),
        P(None, "tensor", ("dp", "expert")),
        P(("dp", "expert")),
        P(("dp", "expert")),
        P("expert", "dp", "tensor"),
        P("expert", "dp", "tensor"),
        P("expert", "tensor", "dp"),
    )
    out_specs = (
        P("dp", "expert", None),
        P("dp", "expert", None),
        P(("dp", "expert"), None, "tensor"),
        P(None, ("dp", "expert"), "tensor"),
        P(None, "tensor", ("dp", "expert")),
        P(("dp", "expert")),
        P(("dp", "expert")),
        P("expert", "dp", "tensor"),
        P("expert", "dp", "tensor"),
        P("expert", "tensor", "dp"),
    )
    return jax.shard_map(
        per_device, mesh=mesh, in_specs=in_specs, out_specs=out_specs, check_vma=False
    )
```

```python
import jax
import jax.numpy as jnp
import numpy as np
from jax import lax
from jax.experimental import pallas as pl
from jax.experimental.pallas import tpu as pltpu
from jax.sharding import PartitionSpec as P

HD = 128
ATT_EXP = 8
TOPK = 2
EPSILON = 1e-06
BF = jnp.bfloat16
F32 = jnp.float32


def remote(src, dst, send, recv, device):
    return pltpu.make_async_remote_copy(
        src_ref=src,
        dst_ref=dst,
        send_sem=send,
        recv_sem=recv,
        device_id=device,
        device_id_type=pl.DeviceIdType.MESH,
    )


def each(count, body, start=1):
    def step(index, carry):
        body(index)
        return carry

    lax.fori_loop(start, count, step, 0)


def mm(left, right, left_dim=1, right_dim=0, precision=None):
    return lax.dot_general(
        left,
        right,
        (((left_dim,), (right_dim,)), ((), ())),
        precision=precision,
        preferred_element_type=F32,
    )


def enter(own, half, core, owners, around=(), greeted=0):
    semaphore = pltpu.get_barrier_semaphore()
    for index in around:
        pl.semaphore_signal(
            semaphore, inc=1, device_id={"dp": index}, device_id_type=pl.DeviceIdType.MESH
        )

    def hello(expert, tensor):
        pl.semaphore_signal(
            semaphore,
            inc=1,
            device_id={"expert": expert, "tensor": tensor},
            device_id_type=pl.DeviceIdType.MESH,
        )

    def column(step):
        hello(
            lax.rem(own + lax.div(step, 2), owners),
            2 * lax.rem(half + lax.rem(step, 2), 2) + core,
        )

    each(2 * owners, column)
    hello(own, 2 * half + 1 - core)
    hello(own, 2 * (1 - half) + 1 - core)
    pl.semaphore_wait(semaphore, 2 * owners + 1 + len(around) + greeted)


def send_home(merged, landing, sends, recvs, own, half, core, owners):
    def outgoing(step):
        to, side = lax.rem(own + lax.div(step, 2), owners), lax.rem(half + lax.rem(step, 2), 2)
        return remote(
            merged.at[side, to],
            landing.at[half, own],
            sends.at[step],
            recvs.at[step],
            {"expert": to, "tensor": 2 * side + core},
        )

    each(2 * owners, lambda step: outgoing(step).start())
    landing[half, own] = merged[half, own]
    return outgoing


def wait_home(outgoing, owners):
    each(2 * owners, lambda step: outgoing(step).wait())


def share_start(slices, sends, recvs, own, share, shares):
    def copy(step):
        return remote(
            slices.at[share],
            slices.at[share],
            sends.at[step],
            recvs.at[step],
            {"expert": own, "tensor": lax.rem(share + step, shares)},
        )

    each(shares, lambda step: copy(step).start())
    return copy


def share_slices(slices, sends, recvs, own, share, shares):
    copy = share_start(slices, sends, recvs, own, share, shares)
    each(shares, lambda step: copy(step).wait())


class Ring:
    def __init__(self, buffer, sends, recvs, base, index, count):
        self.buffer, self.sends, self.recvs, self.base = buffer, sends, recvs, base
        self.index = index
        self.after, self.before = lax.rem(index + 1, count), lax.rem(index + count - 1, count)
        self.cut = buffer.shape[1] // 2

    def copy(self, kind, source=None):
        buffer, cut = self.buffer, self.cut
        if kind < 2:
            src = buffer.at[self.index] if source is None else source
            dst = buffer.at[self.index]
        elif kind == 2:
            src = dst = buffer.at[self.before, pl.ds(0, cut)]
        else:
            src = dst = buffer.at[self.after, pl.ds(cut, cut)]
        place = self.base + kind
        device = {"dp": self.after if kind % 2 == 0 else self.before}
        return remote(src, dst, self.sends.at[place], self.recvs.at[place], device)

    def start(self, source=None):
        self.copy(0, source).start()
        self.copy(1, source).start()

    def forward(self):
        self.copy(0).wait_recv()
        self.copy(2).start()
        self.copy(1).wait_recv()
        self.copy(3).start()

    def finish(self):
        self.copy(2).wait_recv()
        self.copy(3).wait_recv()

    def drain(self, source=None):
        self.copy(0, source).wait_send()
        self.copy(1, source).wait_send()
        self.copy(2).wait_send()
        self.copy(3).wait_send()


def first_kernel(
    tokens,
    marks,
    own_gains,
    pack_one,
    pack_two,
    gate_weight,
    up_weight,
    down_weight,
    upstream,
    lengths,
    cos_key,
    sin_key,
    first_full,
    out_full,
    normed,
    gains,
    inv_one,
    queries,
    pairs,
    row_info,
    cos_slot,
    sin_slot,
    place,
    mixed,
    state,
    inv_two,
    features_all,
    hidden,
    d_both,
    d_parts,
    output_part,
    sel_ffn,
    sel_att,
    gate_columns,
    pick_ffn,
    features,
    expert_in,
    expert_grad,
    routes,
    gain_parts,
    slot_keys,
    inv_all,
    heads_out,
    mixed_out,
    mixed_in,
    far,
    near,
    sibling,
    landing,
    landing_two,
    slices,
    rows_out,
    grads_out,
    gate_up,
    down,
    act,
    ring_send,
    ring_recv,
    local,
    pack_send,
    pack_recv,
    token_send,
    token_recv,
    mark_send,
    mark_recv,
    one_send,
    one_recv,
    head_send,
    head_recv,
    back_send,
    back_recv,
    home_send,
    home_recv,
    home_two_send,
    home_two_recv,
    slice_send,
    slice_recv,
    row_send,
    row_recv,
    grad_send,
    grad_recv,
    feature_send,
    feature_recv,
    gain_send,
    gain_recv,
):
    own, share, dp = lax.axis_index("expert"), lax.axis_index("tensor"), lax.axis_index("dp")
    owners, shares, dps = heads_out.shape[0], slices.shape[0], first_full.shape[0]
    half, core = lax.div(share, 2), lax.rem(share, 2)
    group, piece = slices.shape[1], slices.shape[2]
    width = shares * piece
    wide = width // 2
    slots = rows_out.shape[1]
    rows = owners * slots
    head_rows = heads_out.shape[1]
    columns = owners // 2
    part = lax.rem(own, 2)
    local_rows = pack_one.shape[1]
    units = gate_weight.shape[1]
    other = {"expert": own, "tensor": 2 * half + 1 - core}
    enter(own, half, core, owners, [lax.rem(dp + step, dps) for step in range(1, dps)])

    down_ring = Ring(down, ring_send, ring_recv, 0, dp, dps)
    one_ring = Ring(first_full, ring_send, ring_recv, 4, dp, dps)
    two_ring = Ring(out_full, ring_send, ring_recv, 8, dp, dps)
    up_ring = Ring(gate_up.at[1], ring_send, ring_recv, 12, dp, dps)
    low, high = pl.ds(0, piece // 2), pl.ds(piece // 2, piece // 2)
    low_ring = Ring(gate_up.at[0, :, low], ring_send, ring_recv, 16, dp, dps)
    high_ring = Ring(gate_up.at[0, :, high], ring_send, ring_recv, 20, dp, dps)
    own_rows = pl.ds(pl.multiple_of(own * local_rows, local_rows), local_rows)

    def to_owner(src, dst, sends, recvs, step):
        to = lax.rem(own + step, owners)
        device = {"expert": to, "tensor": share}
        return remote(src(to), dst, sends.at[step], recvs.at[step], device)

    def pack_copy(step):
        return to_owner(pack_one.at.__getitem__, first_full.at[dp, own_rows], pack_send, pack_recv, step)

    def second_copy(step):
        to = lax.rem(own + step, owners)
        return remote(
            pack_two.at[to],
            out_full.at[dp, own_rows],
            pack_send.at[owners + step],
            pack_recv.at[owners + step],
            {"expert": to, "tensor": share},
        )

    def token_copy(step):
        start = pl.multiple_of(core * wide, wide)
        return to_owner(
            lambda to: tokens.at[:, pl.ds(start, wide)],
            normed.at[core, own],
            token_send,
            token_recv,
            step,
        )

    def mark_copy(step):
        return to_owner(lambda to: marks, routes.at[own], mark_send, mark_recv, step)

    each(owners, lambda step: pack_copy(step).start())
    each(owners, lambda step: mark_copy(step).start())

    def gain_copy(step):
        return to_owner(lambda to: own_gains, gain_parts.at[dp, own], gain_send, gain_recv, step)

    def far_gain_copy(step):
        to = lax.rem(dp + step, dps)
        place = owners + step
        return remote(
            gain_parts.at[dp],
            gain_parts.at[dp],
            gain_send.at[place],
            gain_recv.at[place],
            {"dp": to},
        )

    gain_parts[dp, own] = own_gains[...]
    each(owners, lambda step: gain_copy(step).start())
    low_ring.start(gate_weight.at[low])
    own_copies = [
        pltpu.make_async_copy(pack_one.at[own], first_full.at[dp, own_rows], local.at[0]),
        pltpu.make_async_copy(pack_two.at[own], out_full.at[dp, own_rows], local.at[1]),
        pltpu.make_async_copy(gate_weight, gate_up.at[0, dp], local.at[2]),
        pltpu.make_async_copy(up_weight, gate_up.at[1, dp], local.at[3]),
        pltpu.make_async_copy(down_weight, down.at[dp], local.at[4]),
    ]
    for copy in own_copies:
        copy.start()
    routes[own] = marks[...]
    normed[core, own] = tokens[:, pl.ds(pl.multiple_of(core * wide, wide), wide)]

    own_copies[0].wait()
    each(owners, lambda step: pack_copy(step).wait())
    one_ring.start()
    high_ring.start(gate_weight.at[high])
    each(owners, lambda step: token_copy(step).start())
    each(owners, lambda step: second_copy(step).start())
    each(owners, lambda step: mark_copy(step).wait())
    each(owners, lambda step: gain_copy(step).wait())
    each(dps, lambda step: far_gain_copy(step).start())

    def picked_rows(source, out, scale):
        for index in range(2):
            cut = pl.ds(pl.multiple_of(core * wide + index * piece, piece), piece)
            taken = mm(sel_ffn[...], source[:, cut])
            if scale is not None:
                taken = taken * scale
            taken = taken.astype(BF).reshape(owners, slots, piece)
            out[:, :, index * piece : (index + 1) * piece] = taken


    def grad_copy(step):
        return to_owner(grads_out.at.__getitem__, expert_grad.at[core, own], grad_send, grad_recv, step)

    token_rows = lax.broadcasted_iota(jnp.int32, (group, group), 0)
    token_columns = lax.broadcasted_iota(jnp.int32, (group, group), 1)
    before = (token_rows < token_columns).astype(F32).astype(BF)
    token_names = token_rows.astype(F32).astype(BF)
    slot_names = lax.broadcasted_iota(jnp.int32, (slots, group), 0).astype(F32)
    first_routes = jnp.concatenate([routes[index, 0:1, :] for index in range(owners)], 0)
    second_routes = jnp.concatenate([routes[index, 1:2, :] for index in range(owners)], 0)

    def map_keys(name):
        member = (first_routes == name) | (second_routes == name)
        rank = mm(jnp.where(member, 1.0, 0.0).astype(BF), before)
        return jnp.where(member, rank, -1.0)

    for name in range(owners):
        slot_keys[name] = map_keys(float(name))

    gate_columns[...] = jnp.transpose(marks[...])
    names = lax.broadcasted_iota(jnp.int32, (owners, group), 0).astype(F32)
    member = (marks[2:3, :] == names) | (marks[3:4, :] == names)
    rank = mm(jnp.where(member, 1.0, 0.0).astype(BF), before)
    ffn_keys = jnp.where(member, rank, -1.0)
    gate_slots = []
    for name in range(owners):
        cut = slice(name * slots, (name + 1) * slots)
        key = slot_keys[name, pl.ds(own, 1), :]
        hot = jnp.where(key == slot_names, 1.0, 0.0)
        for choice in range(TOPK):
            chosen_here = jnp.where(marks[choice : choice + 1, :] == float(name), hot, 0.0)
            sel_att[cut, choice * group : (choice + 1) * group] = chosen_here.astype(BF)
        hot = jnp.where(ffn_keys[name : name + 1, :] == slot_names, 1.0, 0.0)
        sel_ffn[cut, :] = hot.astype(BF)
        gate = jnp.zeros((slots, 1), F32)
        for choice in range(TOPK):
            chosen_here = jnp.where(marks[2 + choice : 3 + choice, :] == float(name), hot, 0.0)
            pick_ffn[cut, choice * group : (choice + 1) * group] = chosen_here.astype(BF)
            weighed = chosen_here * marks[6 + choice : 7 + choice, :]
            gate = gate + jnp.sum(weighed, 1, keepdims=True)
        gate_slots.append(gate)
    picked_rows(upstream, grads_out, jnp.concatenate(gate_slots, 0))

    def one_hot(name, block):
        key = slot_keys[name, pl.ds(block, 1), :]
        return jnp.where(key == slot_names, 1.0, 0.0)

    def table(hot, array, block):
        span = pl.ds(pl.multiple_of(block * group, group), group)
        return mm(hot, array[span, :], precision=lax.Precision.HIGHEST)

    def row_block(index, carry):
        name, block = lax.div(index, columns), part * columns + lax.rem(index, columns)
        hot = one_hot(name, block)
        pos = mm(hot.astype(BF), token_names) + (block * group).astype(F32)
        start, bound = jnp.zeros_like(pos), jnp.zeros((1, group), F32)
        for document in range(lengths.shape[0]):
            bound = bound + lengths[document : document + 1, :]
            start = jnp.maximum(start, jnp.where(bound <= pos, bound, 0.0))
        span = pl.ds(pl.multiple_of(index * slots, slots), slots)
        row_info[span, 0:1] = pos[:, 0:1]
        row_info[span, 1:2] = start[:, 0:1]
        return carry

    lax.fori_loop(0, owners * columns, row_block, 0)

    each(owners, lambda step: token_copy(step).wait())
    across = remote(normed.at[core], normed.at[core], one_send.at[0], one_recv.at[0], other)
    across.start()
    each(owners, lambda step: grad_copy(step).start())
    expert_grad[core, own] = grads_out[own]
    own_copies[1].wait()
    each(owners, lambda step: second_copy(step).wait())
    one_ring.forward()
    two_ring.start()
    low_ring.forward()
    up_ring.start(up_weight)
    across.wait()

    def squares(index, carry):
        low, high = normed[0, index].astype(F32), normed[1, index].astype(F32)
        total = jnp.sum(low * low, 1, keepdims=True) + jnp.sum(high * high, 1, keepdims=True)
        inv_all[index] = lax.rsqrt(total / width + EPSILON)
        return carry

    lax.fori_loop(0, owners, squares, 0)
    inv_one[...] = inv_all[own]
    one_ring.finish()

    each(dps, lambda step: far_gain_copy(step).wait())
    left = lax.broadcasted_iota(jnp.int32, (8, HD), 1) < HD // 2
    for index in range(dps * owners // 2):
        name, side = index // columns, 2 * (index % columns)
        turned = pltpu.roll(gain_parts[name, side + 1], HD // 2, 1)
        joined = jnp.where(left, gain_parts[name, side], turned)
        gains[:, index * HD : (index + 1) * HD] = joined[0:2, :]

    chosen = expert_in
    def norm_block(index, carry):
        hot = one_hot(own, index)
        place[index] = hot.astype(BF)
        span = pl.ds(pl.multiple_of(index * slots, slots), slots)
        cos_slot[span, :] = table(hot, cos_key, index)
        sin_slot[span, :] = table(hot, sin_key, index)
        for side in range(2):
            cut = slice(side * wide, (side + 1) * wide)
            rounded = normed[side, index].astype(F32) * inv_all[index] * gains[0:1, cut]
            rounded = rounded.astype(BF)
            normed[side, index] = rounded
            chosen[side, index] = mm(hot.astype(BF), rounded).astype(BF)
        return carry

    lax.fori_loop(0, owners, norm_block, 0)
    query = jnp.zeros((rows, columns * HD), F32)
    for index in range(dps):
        cut = slice((index % 2) * piece, (index % 2 + 1) * piece)
        taken = chosen[index // 2, :, :, cut].reshape(rows, piece)
        query = query + mm(taken, first_full[index, :, HD:])
    for column in range(columns):
        head = query[:, column * HD : (column + 1) * HD]
        head = (head * cos_slot[...] + pltpu.roll(head, HD // 2, 1) * sin_slot[...]).astype(BF)
        for side in range(2):
            heads_out[2 * column + side] = head[side * head_rows : (side + 1) * head_rows]

    def head_copy(step):
        return to_owner(heads_out.at.__getitem__, queries.at[own], head_send, head_recv, step)

    each(owners, lambda step: head_copy(step).start())
    queries[own] = heads_out[own]

    first = part == 0

    def key_block(index, carry):
        taken = jnp.zeros((group, HD), F32)
        for step in range(dps):
            cut = slice((step % 2) * piece, (step % 2 + 1) * piece)
            taken = taken + mm(normed[step // 2, index, :, cut], first_full[step, :, :HD])
        span = pl.ds(pl.multiple_of(index * group, group), group)
        turned = taken * cos_key[span, :] + pltpu.roll(taken, HD // 2, 1) * sin_key[span, :]
        pairs[part, span, :] = jnp.where(first, turned, taken).astype(BF)
        return carry

    lax.fori_loop(0, owners, key_block, 0)
    pair = {"expert": own + 1 - 2 * part, "tensor": share}
    swapped = remote(pairs.at[part], pairs.at[part], one_send.at[10], one_recv.at[10], pair)
    swapped.start()

    scale = HD ** (-0.5)
    key_pos = lax.broadcasted_iota(jnp.int32, (1, owners * group), 1).astype(F32)

    def attend(index):
        span = pl.ds(pl.multiple_of(index * head_rows, head_rows), head_rows)
        scores = mm(queries[index], pairs[0], 1, 1) * scale
        visible = (key_pos <= row_info[span, 0:1]) & (key_pos >= row_info[span, 1:2])
        scores = jnp.where(visible, scores, -1e30)
        top = jnp.max(scores, 1, keepdims=True)
        shifted = jnp.exp(scores - top)
        total = jnp.sum(shifted, 1, keepdims=True)
        row_info[span, 2:3] = top + jnp.log(total)
        probs = (shifted / total).astype(BF)
        mixed_out[index] = mm(probs, pairs[1]).astype(BF)

    def back_copy(step):
        to = lax.rem(own + owners - step, owners)
        return remote(
            mixed_out.at[to],
            mixed_in.at[own],
            back_send.at[step],
            back_recv.at[step],
            {"expert": to, "tensor": share},
        )

    def attend_other(step):
        head_copy(step).wait()
        attend(lax.rem(own + owners - step, owners))
        back_copy(step).start()

    swapped.wait()
    attend(own)
    mixed_in[own] = mixed_out[own]
    each(owners, attend_other)
    two_ring.forward()
    high_ring.forward()
    down_ring.start(down_weight)
    two_ring.finish()
    each(owners, lambda step: back_copy(step).wait())
    for column in range(columns):
        for side in range(2):
            mixed[
                side * head_rows : (side + 1) * head_rows, column * HD : (column + 1) * HD
            ] = mixed_in[2 * column + side]

    def chip_sum(product, far, near, sibling, base):
        def across(side):
            place = base + side
            return remote(far.at[side], sibling.at[side], one_send.at[place], one_recv.at[place], other)

        for side in range(2):
            far[side] = product(2 * side + 1 - core)
            across(side).start()
        for side in range(2):
            near[side] = product(2 * side + core)
        for side in range(2):
            across(side).wait()
            near[side] = (near[side].astype(F32) + sibling[side].astype(F32)).astype(BF)

    def at_tokens(pick, gate, landing):
        total = jnp.zeros((group, piece), F32)
        for choice in range(TOPK):
            span = slice(choice * group, (choice + 1) * group)
            taken = mm(pick[:, span], landing[0].reshape(rows, piece), 0, 0)
            taken = taken + mm(pick[:, span], landing[1].reshape(rows, piece), 0, 0)
            total = total + gate_columns[:, gate + choice : gate + choice + 1] * taken
        return total

    def map_product(index):
        return mm(mixed[...], out_full[index], 1, 1).astype(BF).reshape(owners, slots, piece)

    chip_sum(map_product, far, near, sibling, 1)
    outgoing = send_home(near, landing, home_send, home_recv, own, half, core, owners)
    up_ring.forward()
    wait_home(outgoing, owners)
    slices[share] = at_tokens(sel_att, 4, landing).astype(BF)
    share_slices(slices, slice_send, slice_recv, own, share, shares)

    total = jnp.zeros((group, 1), F32)
    for index in range(shares):
        cut = slice(index * piece, (index + 1) * piece)
        value = tokens[:, cut].astype(F32) + slices[index].astype(F32)
        state[:, cut] = value
        total = total + jnp.sum(value * value, 1, keepdims=True)
    inv = lax.rsqrt(total / width + EPSILON)
    inv_two[...] = inv
    for index in range(2):
        cut = pl.ds(pl.multiple_of(core * wide + index * piece, piece), piece)
        rounded = (state[:, cut] * inv * gains[1:2, cut]).astype(BF)
        taken = mm(sel_ffn[...], rounded).astype(BF).reshape(owners, slots, piece)
        rows_out[:, :, index * piece : (index + 1) * piece] = taken

    def row_copy(step):
        return to_owner(rows_out.at.__getitem__, expert_in.at[core, own], row_send, row_recv, step)

    each(owners, lambda step: row_copy(step).start())
    expert_in[core, own] = rows_out[own]
    each(owners, lambda step: grad_copy(step).wait())
    across = remote(expert_grad.at[core], expert_grad.at[core], one_send.at[5], one_recv.at[5], other)
    across.start()
    each(owners, lambda step: row_copy(step).wait())
    across_rows = remote(expert_in.at[core], expert_in.at[core], one_send.at[6], one_recv.at[6], other)
    across_rows.start()
    across.wait()
    across_rows.wait()

    used = hidden.shape[0] // owners

    def tight(array):
        pieces = [array[index * slots : index * slots + used] for index in range(owners)]
        return jnp.concatenate(pieces, 0)

    def loose(array):
        blank = jnp.zeros((slots - used, array.shape[1]), F32)
        pieces = []
        for index in range(owners):
            pieces += [array[index * used : (index + 1) * used], blank]
        return jnp.concatenate(pieces, 0).astype(BF).reshape(owners, slots, piece)

    for index in range(dps):
        cut = slice((index % 2) * piece, (index % 2 + 1) * piece)
        for side, source in enumerate((expert_in, expert_grad)):
            taken = source[index // 2, :, :, cut].reshape(rows, piece).astype(F32)
            features[side, index] = tight(taken).astype(BF)
    def feature_copy(step):
        to = lax.rem(dp + step, dps)
        return remote(
            features.at[core, to],
            features_all.at[core, dp],
            feature_send.at[step],
            feature_recv.at[step],
            {"dp": to},
        )

    keep = pltpu.make_async_copy(features.at[core, dp], features_all.at[core, dp], feature_send.at[0])
    keep.start()
    for copy in own_copies[2:]:
        copy.wait()
    tile = 2 * HD

    def unit_tiles(body):
        def step(index, carry):
            body(pl.ds(pl.multiple_of(index * tile, tile), tile))
            return carry

        lax.fori_loop(0, units // tile, step, 0)
        if units % tile:
            body(pl.ds(units - units % tile, units % tile))

    low_ring.finish()
    high_ring.finish()

    def gate_tile(cut):
        total = mm(features[0, 0], gate_up[0, 0, :, cut])
        for index in range(1, dps):
            total = total + mm(features[0, index], gate_up[0, index, :, cut])
        act[0, :, cut] = total

    unit_tiles(gate_tile)
    down_ring.forward()
    up_ring.finish()

    def up_tile(cut):
        up = mm(features[0, 0], gate_up[1, 0, :, cut])
        for index in range(1, dps):
            up = up + mm(features[0, index], gate_up[1, index, :, cut])
        act[1, :, cut] = up
        gate = act[0, :, cut]
        hidden[:, cut] = (gate / (1.0 + jnp.exp(-gate)) * up).astype(BF)

    unit_tiles(up_tile)
    down_ring.finish()
    each(dps, lambda step: feature_copy(step).start())
    chip_sum(lambda index: loose(mm(hidden[...], down[index])), far, near, sibling, 7)
    outgoing_two = send_home(
        near, landing_two, home_two_send, home_two_recv, own, half, core, owners
    )

    def grad_tile(cut):
        grad = mm(features[1, 0], down[0, cut, :], 1, 1)
        for index in range(1, dps):
            grad = grad + mm(features[1, index], down[index, cut, :], 1, 1)
        gate, up = act[0, :, cut], act[1, :, cut]
        sigma = 1.0 / (1.0 + jnp.exp(-gate))
        d_both[0, :, cut] = (grad * up * sigma * (1.0 + gate * (1.0 - sigma))).astype(BF)
        d_both[1, :, cut] = (grad * gate * sigma).astype(BF)

    unit_tiles(grad_tile)
    for index in range(dps):
        total = mm(d_both[0], gate_up[0, index], 1, 1) + mm(d_both[1], gate_up[1, index], 1, 1)
        d_parts[index % 2, index // 2] = loose(total)
    keep.wait()
    each(dps, lambda step: feature_copy(step).wait())
    across = remote(
        features_all.at[core], features_all.at[core], one_send.at[9], one_recv.at[9], other
    )
    across.start()
    wait_home(outgoing_two, owners)
    rest = at_tokens(pick_ffn, 6, landing_two)
    span = pl.ds(pl.multiple_of(share * piece, piece), piece)
    output_part[...] = (state[:, span] + rest).astype(BF)
    across.wait()
    one_ring.drain()
    two_ring.drain()
    low_ring.drain(gate_weight.at[low])
    high_ring.drain(gate_weight.at[high])
    up_ring.drain(up_weight)
    down_ring.drain(down_weight)


def back_kernel(
    parts,
    sel_ffn,
    state,
    inv_two,
    upstream,
    gains,
    sel_att,
    gate_columns,
    out_full,
    queries,
    pairs,
    row_info,
    cos_slot,
    sin_slot,
    cos_key,
    sin_key,
    place,
    d_both,
    hidden,
    output_part,
    tokens,
    inv_one,
    mixed,
    far_weights,
    far_normed,
    far_features,
    output,
    input_grad,
    gain_grads,
    maps_in,
    gate_grad,
    up_grad,
    down_grad,
    d_both_all,
    hidden_all,
    d_gain_two,
    d_rows,
    d_proj,
    return_in,
    parts_joined,
    rows_out,
    heads_out,
    heads_in,
    queries_out,
    queries_in,
    pair_out,
    pair_in,
    d_keys,
    d_values,
    far,
    near,
    sibling,
    landing,
    slices,
    map_grads,
    early,
    late,
    gain_out,
    gain_in,
    gain_mid,
    gain_last,
    weights,
    normed,
    features,
    acts,
    features_turned,
    wide_tiles,
    tall_tiles,
    first_send,
    first_recv,
    return_send,
    return_recv,
    join_send,
    join_recv,
    row_send,
    row_recv,
    head_send,
    head_recv,
    back_send,
    back_recv,
    ring_send,
    ring_recv,
    local,
    one_send,
    one_recv,
    home_send,
    home_recv,
    slice_send,
    slice_recv,
    step_send,
    step_recv,
    map_send,
    map_recv,
    gain_send,
    gain_recv,
    tile_sem,
):
    own, share = lax.axis_index("expert"), lax.axis_index("tensor")
    owners, shares = heads_out.shape[0], parts_joined.shape[0]
    half, core = lax.div(share, 2), lax.rem(share, 2)
    piece, width = parts_joined.shape[2], state.shape[1]
    slots = rows_out.shape[1]
    rows = owners * slots
    wide = width // 2
    head_rows = heads_out.shape[1]
    columns = owners // 2
    other = {"expert": own, "tensor": 2 * half + 1 - core}
    dp, dps = lax.axis_index("dp"), d_both_all.shape[0]

    enter(own, half, core, owners, [lax.rem(dp + step, dps) for step in range(1, dps)])
    loads = [
        pltpu.make_async_copy(far_weights, weights, local.at[4]),
        pltpu.make_async_copy(far_normed, normed, local.at[5]),
        pltpu.make_async_copy(far_features.at[1], features, local.at[6]),
        pltpu.make_async_copy(far_features.at[0], acts.at[:, :, pl.ds(0, width // shares)], local.at[2]),
    ]
    for copy in loads:
        copy.start()

    both_ring = Ring(d_both_all, ring_send, ring_recv, 0, dp, dps)
    both_ring.start(d_both)
    hidden_ring = Ring(hidden_all, ring_send, ring_recv, 4, dp, dps)
    hidden_ring.start(hidden)

    used_slots = pl.ds(0, slots)
    return_near, return_out = sibling.at[:, :, used_slots], near.at[:, :, used_slots]
    across = remote(parts.at[1 - core], return_near, first_send.at[0], first_recv.at[0], other)
    across.start()
    across.wait()
    for side in range(2):
        return_out[side] = (parts[core, side].astype(F32) + return_near[side].astype(F32)).astype(BF)
    outgoing = send_home(return_out, return_in, return_send, return_recv, own, half, core, owners)
    wait_home(outgoing, owners)
    total = mm(sel_ffn[...], return_in[0].reshape(rows, piece), 0, 0)
    total = total + mm(sel_ffn[...], return_in[1].reshape(rows, piece), 0, 0)
    parts_joined[share] = total.astype(BF)
    share_slices(parts_joined, join_send, join_recv, own, share, shares)

    inv = inv_two[...]
    mean = jnp.zeros_like(inv)
    for index in range(shares):
        cut = slice(index * piece, (index + 1) * piece)
        grad, value = parts_joined[index].astype(F32), state[:, cut]
        mean = mean + jnp.sum(value * gains[1:2, cut] * grad, 1, keepdims=True)
        d_gain_two[:, cut] = jnp.sum(grad * value * inv, 0, keepdims=True)
    mean = mean * (inv * inv * inv / width)
    for index in range(shares):
        cut = slice(index * piece, (index + 1) * piece)
        grad = gains[1:2, cut] * parts_joined[index].astype(F32)
        input_grad[:, cut] = upstream[:, cut].astype(F32) + inv * grad - state[:, cut] * mean

    for index in range(2):
        start = pl.multiple_of(core * wide + index * piece, piece)
        grad = input_grad[:, pl.ds(start, piece)]
        both = jnp.concatenate(
            [(gate_columns[:, 4:5] * grad).astype(BF), (gate_columns[:, 5:6] * grad).astype(BF)], 0
        )
        picked = mm(sel_att[...], both).astype(BF).reshape(owners, slots, piece)
        rows_out[:, :, index * piece : (index + 1) * piece] = picked

    def row_copy(step):
        to = lax.rem(own + step, owners)
        return remote(
            rows_out.at[to],
            d_rows.at[core, own],
            row_send.at[step],
            row_recv.at[step],
            {"expert": to, "tensor": share},
        )

    each(owners, lambda step: row_copy(step).start())
    d_rows[core, own] = rows_out[own]
    each(owners, lambda step: row_copy(step).wait())
    across = remote(d_rows.at[core], d_rows.at[core], first_send.at[1], first_recv.at[1], other)
    across.start()

    def half_product(side):
        taken = d_rows[side].reshape(rows, wide)
        return mm(taken[:, :piece], out_full[2 * side]) + mm(taken[:, piece:], out_full[2 * side + 1])

    d_mixed = half_product(core)
    across.wait()
    d_mixed = (d_mixed + half_product(1 - core)).astype(BF)
    for column in range(columns):
        for part in range(2):
            heads_out[2 * column + part] = d_mixed[
                part * head_rows : (part + 1) * head_rows, column * HD : (column + 1) * HD
            ]

    def head_copy(step):
        to = lax.rem(own + step, owners)
        return remote(
            heads_out.at[to],
            heads_in.at[own],
            head_send.at[step],
            head_recv.at[step],
            {"expert": to, "tensor": share},
        )

    each(owners, lambda step: head_copy(step).start())
    heads_in[own] = heads_out[own]

    scale = HD ** (-0.5)
    key_pos = lax.broadcasted_iota(jnp.int32, (1, pairs.shape[1]), 1).astype(F32)
    d_keys[...] = jnp.zeros_like(d_keys)
    d_values[...] = jnp.zeros_like(d_values)

    def attend(index):
        span = pl.ds(pl.multiple_of(index * head_rows, head_rows), head_rows)
        query, key, value, grad = queries[index], pairs[0], pairs[1], heads_in[index]
        scores = mm(query, key, 1, 1) * scale
        visible = (key_pos <= row_info[span, 0:1]) & (key_pos >= row_info[span, 1:2])
        probs = jnp.where(visible, jnp.exp(scores - row_info[span, 2:3]), 0.0)
        d_probs = mm(grad, value, 1, 1)
        delta = jnp.sum(probs * d_probs, 1, keepdims=True)
        d_scores = (probs * (d_probs - delta)).astype(BF)
        queries_out[index] = (mm(d_scores, key) * scale).astype(BF)
        d_keys[...] += mm(d_scores, query, 0, 0)
        d_values[...] += mm(probs.astype(BF), grad, 0, 0)

    def query_copy(step):
        to = lax.rem(own + owners - step, owners)
        return remote(
            queries_out.at[to],
            queries_in.at[own],
            back_send.at[step],
            back_recv.at[step],
            {"expert": to, "tensor": share},
        )

    def attend_other(step):
        head_copy(step).wait()
        attend(lax.rem(own + owners - step, owners))
        query_copy(step).start()

    attend(own)
    queries_in[own] = queries_out[own]
    each(owners, attend_other)
    both_ring.forward()

    first = lax.rem(own, 2) == 0
    pair_out[...] = jnp.where(first, d_values[...], d_keys[...] * scale).astype(BF)
    pair = {"expert": own + 1 - 2 * lax.rem(own, 2), "tensor": share}
    across = remote(pair_out, pair_in, first_send.at[2], first_recv.at[2], pair)
    across.start()
    each(owners, lambda step: query_copy(step).wait())
    group = place.shape[2]
    for part in range(2):
        for index in range(columns):
            block = part * columns + index
            cut = slice(index * slots, (index + 1) * slots)
            span = slice(block * slots, (block + 1) * slots)
            turned = []
            for column in range(columns):
                grad = queries_in[2 * column + part, cut, :].astype(F32)
                back = pltpu.roll(grad, HD // 2, 1) * sin_slot[span, :]
                turned.append((grad * cos_slot[span, :] - back).astype(BF))
            picked = jnp.concatenate(turned, 1)
            d_proj[block * group : (block + 1) * group, : columns * HD] = mm(
                place[block], picked, 0, 0
            ).astype(BF)
    across.wait()
    mine = jnp.where(first, d_keys[...] * scale, d_values[...]) + pair_in[...].astype(F32)
    turned = mine * cos_key[...] + pltpu.roll(mine, HD // 2, 1) * sin_key[...]
    d_proj[:, columns * HD :] = jnp.where(first, turned, mine).astype(BF)

    group, piece = near.shape[2], near.shape[3]
    head_width = d_proj.shape[1] - HD
    local_rows = maps_in.shape[1]
    used, units = acts.shape[1], acts.shape[2]
    after, before = lax.rem(dp + 1, dps), lax.rem(dp + dps - 1, dps)
    facing = lax.rem(dp + 2, dps)
    for copy in loads:
        copy.wait()
    for index in range(dps):
        features_turned[index] = jnp.transpose(acts[index, :, :piece].astype(F32)).astype(BF)

    class load:
        def __init__(self, side):
            rows_here = pl.ds(0 if side == 2 else side * used, used)
            mine, others = (hidden, hidden_all) if side == 2 else (d_both, d_both_all)
            self.copies = [pltpu.make_async_copy(mine.at[rows_here], acts.at[dp], local.at[0])]
            for step in range(1, dps):
                index = lax.rem(dp + step, dps)
                self.copies.append(
                    pltpu.make_async_copy(
                        others.at[index, rows_here], acts.at[index], local.at[8 + step]
                    )
                )

        def start(self):
            for copy in self.copies:
                copy.start()

        def wait(self):
            for copy in self.copies:
                copy.wait()

    def map_grad(index):
        cut = pl.ds(pl.multiple_of(lax.rem(index, 2) * piece, piece), piece)
        inputs = normed[lax.div(index, 2), :, :, cut].reshape(owners * group, piece)
        outs = d_rows[lax.div(index, 2), :, :, cut].reshape(-1, piece)
        return mm(inputs, d_proj[...], 0, 0), mm(outs, mixed[...], 0, 0)

    middle = head_width + HD

    def keep_grad(index):
        ins, outs = map_grad(index)
        map_grads[index, :, :middle] = ins.astype(BF)
        map_grads[index, :, middle:] = outs.astype(BF)

    cut = piece // 2

    def step_copy(kind):
        to = {"dp": after if kind % 2 == 0 else before}
        sems = (step_send.at[kind], step_recv.at[kind])
        if kind < 2:
            span = pl.ds(kind * cut, cut)
            return remote(map_grads.at[facing, span], early.at[kind], *sems, to)
        return remote(map_grads.at[after if kind == 2 else before], late.at[kind - 2], *sems, to)

    keep_grad(facing)
    step_copy(0).start()
    step_copy(1).start()

    def product(index):
        queries = mm(d_proj[:, :head_width], weights[index, :, HD:], 1, 1)
        side = mm(d_proj[:, head_width:], weights[index, :, :HD], 1, 1)
        return (queries + side).reshape(owners, group, piece)

    def across(side):
        return remote(far.at[side], sibling.at[side], one_send.at[side], one_recv.at[side], other)

    for side in range(2):
        far[side] = product(2 * side + 1 - core).astype(BF)
        across(side).start()
    for side in range(2):
        near[side] = product(2 * side + core).astype(BF)
    for side in range(2):
        across(side).wait()
        near[side] = (near[side].astype(F32) + sibling[side].astype(F32)).astype(BF)
    outgoing = send_home(near, landing, home_send, home_recv, own, half, core, owners)

    keep_grad(after)
    keep_grad(before)
    step_copy(0).wait()
    step_copy(1).wait()
    top, bottom = slice(0, cut), slice(cut, 2 * cut)
    map_grads[after, top] = (map_grads[after, top].astype(F32) + early[0].astype(F32)).astype(BF)
    map_grads[before, bottom] = (
        map_grads[before, bottom].astype(F32) + early[1].astype(F32)
    ).astype(BF)
    step_copy(2).start()
    step_copy(3).start()
    hidden_ring.forward()
    keep_grad(dp)
    both_ring.finish()
    load(0).start()

    tile = 2 * HD
    whole, rest = units // tile, units % tile
    def unit_tiles(product, out, rows_first):
        def store(slot, span, size):
            if rows_first:
                return pltpu.make_async_copy(
                    tall_tiles.at[slot, pl.ds(0, size)], out.at[span], tile_sem.at[slot]
                )
            return pltpu.make_async_copy(
                wide_tiles.at[slot, :, pl.ds(0, size)], out.at[:, span], tile_sem.at[slot]
            )

        def put(slot, value, size):
            if rows_first:
                tall_tiles[slot, :size] = value
            else:
                wide_tiles[slot, :, :size] = value

        def pair(index, carry):
            for slot in range(2):
                span = pl.ds(pl.multiple_of((2 * index + slot) * tile, tile), tile)

                @pl.when(index > 0)
                def _(slot=slot, span=span):
                    store(slot, span, tile).wait()

                put(slot, product(span), tile)
                store(slot, span, tile).start()
            return carry

        lax.fori_loop(0, whole // 2, pair, 0)
        spans = [(0, pl.ds((whole - 2) * tile, tile), tile), (1, pl.ds((whole - 1) * tile, tile), tile)]
        for slot, span, size in spans:
            store(slot, span, size).wait()
        if whole % 2:
            span = pl.ds((whole - 1) * tile, tile)
            put(0, product(span), tile)
            store(0, span, tile).start()
        if rest:
            tail = pl.ds(whole * tile, rest)
            put(1, product(tail), rest)
            store(1, tail, rest).start()
            store(1, tail, rest).wait()
        if whole % 2:
            store(0, span, tile).wait()

    def wide_product(span):
        total = mm(features_turned[0], acts[0, :, span])
        for index in range(1, dps):
            total = total + mm(features_turned[index], acts[index, :, span])
        return total

    def tall_product(span):
        total = mm(acts[0, :, span], features[0], 0, 0)
        for index in range(1, dps):
            total = total + mm(acts[index, :, span], features[index], 0, 0)
        return total

    wait_home(outgoing, owners)
    total = jnp.zeros((group, piece), F32)
    for side in range(2):
        for index in range(owners):
            total = total + landing[side, index].astype(F32)
    slices[share, 0] = total.astype(BF)
    slices[share, 1] = output_part[...]
    joining = share_start(slices, slice_send, slice_recv, own, share, shares)
    load(0).wait()
    unit_tiles(wide_product, gate_grad, False)
    load(1).start()

    step_copy(2).wait()
    step_copy(3).wait()
    map_grads[dp] = (
        map_grads[dp].astype(F32) + late[0].astype(F32) + late[1].astype(F32)
    ).astype(BF)

    def home_rows(index):
        return pl.ds(pl.multiple_of(index * local_rows, local_rows), local_rows)

    def map_copy(step):
        to = lax.rem(own + step, owners)
        return remote(
            map_grads.at[dp, home_rows(to)],
            maps_in.at[own],
            map_send.at[step],
            map_recv.at[step],
            {"expert": to, "tensor": share},
        )

    each(owners, lambda step: map_copy(step).start())
    maps_in[own] = map_grads[dp, home_rows(own), :]

    each(shares, lambda step: joining(step).wait())
    inv = inv_one[...]
    mean = jnp.zeros_like(inv)
    for index in range(shares):
        span = slice(index * piece, (index + 1) * piece)
        grad, value = slices[index, 0].astype(F32), tokens[:, span].astype(F32)
        output[:, span] = slices[index, 1]
        mean = mean + jnp.sum(value * gains[0:1, span] * grad, 1, keepdims=True)
        gain_one = jnp.sum(grad * value * inv, 0, keepdims=True)
        for chunk in range(piece // HD):
            lanes = slice(chunk * HD, (chunk + 1) * HD)
            place = index * (piece // HD) + chunk
            gain_out[index, chunk, 0:1] = gain_one[:, lanes]
            gain_out[index, chunk, 1:2] = d_gain_two[:, place * HD : (place + 1) * HD]

    def gain_copy(step):
        to = lax.rem(own + step, owners)
        return remote(
            gain_out.at[:, lax.div(to, 2)],
            gain_in.at[own],
            gain_send.at[step],
            gain_recv.at[step],
            {"expert": to, "tensor": share},
        )

    def far_gain_copy(step):
        to = lax.rem(dp + step, dps)
        return remote(
            gain_mid.at[to],
            gain_last.at[dp],
            gain_send.at[owners + step],
            gain_recv.at[owners + step],
            {"dp": to},
        )

    each(owners, lambda step: gain_copy(step).start())
    gain_in[own] = gain_out[:, lax.div(own, 2)]
    mean = mean * (inv * inv * inv / width)
    for index in range(shares):
        span = slice(index * piece, (index + 1) * piece)
        grad = gains[0:1, span] * slices[index, 0].astype(F32)
        value = tokens[:, span].astype(F32)
        input_grad[:, span] = input_grad[:, span] + inv * grad - value * mean
    load(1).wait()
    unit_tiles(wide_product, up_grad, False)
    each(owners, lambda step: gain_copy(step).wait())
    total = gain_in[0]
    for index in range(1, owners):
        total = total + gain_in[index]
    gain_mid[...] = total
    each(dps, lambda step: far_gain_copy(step).start())
    gain_last[dp] = gain_mid[dp]
    hidden_ring.finish()
    load(2).start()
    load(2).wait()
    unit_tiles(tall_product, down_grad, True)
    each(dps, lambda step: far_gain_copy(step).wait())
    total = gain_last[0, 0:2]
    for index in range(1, dps):
        total = total + gain_last[index, 0:2]
    gain_grads[...] = total
    each(owners, lambda step: map_copy(step).wait())
    both_ring.drain(d_both)
    hidden_ring.drain(hidden)


def call_kernel(kernel, collective_id, outs, scratch, semaphores, args, far_args=(), far_outs=()):
    def specs(count, far):
        spaces = [pl.ANY if index in far else pltpu.VMEM for index in range(count)]
        return [pl.BlockSpec(memory_space=space) for space in spaces]

    return pl.pallas_call(
        kernel,
        out_shape=[jax.ShapeDtypeStruct(shape, dtype) for shape, dtype in outs],
        in_specs=specs(len(args), far_args),
        out_specs=specs(len(outs), far_outs),
        scratch_shapes=[pltpu.VMEM(shape, dtype) for shape, dtype in scratch]
        + [pltpu.SemaphoreType.DMA((count,)) for count in semaphores],
        compiler_params=pltpu.CompilerParams(
            collective_id=collective_id, has_side_effects=True, vmem_limit_bytes=60 * 2**20
        ),
    )(*args)


def per_device(
    tokens,
    cotangent,
    doc_lengths,
    att_routes,
    att_gates,
    ffn_routes,
    ffn_gates,
    kv_weight,
    query_weight,
    out_weight,
    attn_gain,
    ffn_gain,
    gate_weight,
    up_weight,
    down_weight,
):
    _, group, width = tokens.shape
    owners = lax.axis_size("expert")
    shares = lax.axis_size("tensor")
    dps = lax.axis_size("dp")
    own = lax.axis_index("expert")
    share = lax.axis_index("tensor")
    columns = owners // 2
    column_half = own % 2
    att_cap = -(-min(group, group * TOPK * 5 // (4 * ATT_EXP)) // 16) * 16
    ffn_cap = -(-min(group, group * TOPK * 5 // (4 * owners)) // 16) * 16
    rows = owners * att_cap
    seq_len = owners * group
    piece = width // shares
    local = kv_weight.shape[0]
    head_width = kv_weight.shape[2]

    kv_parts = jnp.transpose(kv_weight.reshape(local, 2, columns, HD), (2, 1, 0, 3))
    pack_one = jnp.concatenate([kv_parts.reshape(owners, local, HD), query_weight], 2)
    own_gains = jnp.stack([attn_gain, ffn_gain]).astype(F32)
    own_gains = jnp.pad(own_gains, ((0, 8 - 2), (0, HD - local)))
    pack_two = jnp.swapaxes(out_weight, 1, 2)
    marks = jnp.concatenate(
        [
            att_routes[0].T.astype(F32),
            ffn_routes[0].T.astype(F32),
            att_gates[0].T,
            ffn_gates[0].T,
        ],
        0,
    )
    lengths = jnp.broadcast_to(doc_lengths[0].astype(F32)[:, None], (doc_lengths.shape[1], HD))
    angles = np.arange(seq_len)[:, None] * 10000.0 ** (-np.arange(HD // 2) * 2.0 / HD)
    cos_key = jnp.asarray(np.concatenate([np.cos(angles)] * 2, 1), F32)
    sin_key = jnp.asarray(np.concatenate([-np.sin(angles), np.sin(angles)], 1), F32)
    used = min(group, group * TOPK * 5 // (4 * owners))
    units = gate_weight.shape[2]
    slots = att_cap
    head_rows = columns * slots
    block = (2, owners, slots, piece)
    (
        first_full,
        out_full,
        normed,
        gains,
        inv_one,
        queries,
        pairs,
        row_info,
        cos_slot,
        sin_slot,
        place,
        mixed,
        state,
        inv_two,
        features_all,
        hidden,
        d_both,
        d_parts,
        output_part,
        sel_ffn,
        sel_att,
        gate_columns,
    ) = call_kernel(
        first_kernel,
        3,
        [
            ((dps, owners * local, HD + head_width), BF),
            ((dps, owners * local, head_width), BF),
            ((2, owners, group, width // 2), BF),
            ((2, width), F32),
            ((group, 1), F32),
            ((owners, head_rows, HD), BF),
            ((2, seq_len, HD), BF),
            ((owners * head_rows, HD), F32),
            ((rows, HD), F32),
            ((rows, HD), F32),
            ((owners, slots, group), BF),
            ((rows, head_width), BF),
            ((group, width), F32),
            ((group, 1), F32),
            ((2, dps, owners * used, piece), BF),
            ((owners * used, units), BF),
            ((2, owners * used, units), BF),
            ((2,) + block, BF),
            ((group, piece), BF),
            ((rows, group), BF),
            ((rows, TOPK * group), BF),
            ((group, 8), F32),
        ],
        [
            ((rows, TOPK * group), BF),
            ((2, dps, owners * used, piece), BF),
            ((2, owners, slots, width // 2), BF),
            ((2, owners, slots, width // 2), BF),
            ((owners, 8, group), F32),
            ((dps, owners, 8, HD), F32),
            ((owners, owners, group), F32),
            ((owners, group, 1), F32),
            ((owners, head_rows, HD), BF),
            ((owners, head_rows, HD), BF),
            ((owners, head_rows, HD), BF),
        ]
        + [(block, BF)] * 5
        + [
            ((shares, group, piece), BF),
            ((owners, slots, width // 2), BF),
            ((owners, slots, width // 2), BF),
            ((2, dps, width // dps, units), BF),
            ((dps, units, piece), BF),
            ((2, owners * used, units), F32),
        ],
        [24, 24, 5, 2 * owners, 2 * owners]
        + [owners] * 4
        + [11, 11]
        + [owners] * 4
        + [2 * owners] * 4
        + [shares, shares]
        + [owners] * 4
        + [dps, dps]
        + [owners + dps] * 2,
        [
            tokens[0],
            marks,
            own_gains,
            pack_one,
            pack_two,
            gate_weight[0],
            up_weight[0],
            down_weight[0],
            cotangent[0],
            lengths,
            cos_key,
            sin_key,
        ],
        far_args=(3, 4, 5, 6, 7),
        far_outs=(14,),
    )

    grad_width = head_width + HD + head_width
    (
        output,
        input_grad,
        gain_grads,
        map_grads,
        gate_grad,
        up_grad,
        down_grad,
        *_,
    ) = call_kernel(
        back_kernel,
        1,
        [
            ((group, width), BF),
            ((group, width), F32),
            ((2, HD), F32),
            ((owners, local, grad_width), BF),
            ((piece, units), F32),
            ((piece, units), F32),
            ((units, piece), F32),
            ((dps, 2 * owners * used, units), BF),
            ((dps, owners * used, units), BF),
        ],
        [
            ((1, width), F32),
            ((2, owners, slots, width // 2), BF),
            ((seq_len, head_width + HD), BF),
            (block, BF),
            ((shares, group, piece), BF),
            ((owners, slots, width // 2), BF),
            ((owners, head_rows, HD), BF),
            ((owners, head_rows, HD), BF),
            ((owners, head_rows, HD), BF),
            ((owners, head_rows, HD), BF),
            ((seq_len, HD), BF),
            ((seq_len, HD), BF),
            ((seq_len, HD), F32),
            ((seq_len, HD), F32),
            ((2, owners, group, piece), BF),
            ((2, owners, group, piece), BF),
            ((2, owners, group, piece), BF),
            ((2, owners, group, piece), BF),
            ((shares, 2, group, piece), BF),
            ((dps, piece, grad_width), BF),
            ((2, piece // 2, grad_width), BF),
            ((2, piece, grad_width), BF),
            ((dps, owners // 2, 8, HD), F32),
            ((owners, dps, 8, HD), F32),
            ((dps, 8, HD), F32),
            ((dps, 8, HD), F32),
            ((dps, owners * local, HD + head_width), BF),
            ((2, owners, group, width // 2), BF),
            ((dps, owners * used, piece), BF),
            ((dps, owners * used, units), BF),
            ((dps, piece, owners * used), BF),
            ((2, piece, 2 * HD), F32),
            ((2, 2 * HD, piece), F32),
        ],
        [
            3,
            3,
            2 * owners,
            2 * owners,
            shares,
            shares,
            owners,
            owners,
            owners,
            owners,
            owners,
            owners,
            8,
            8,
            12,
            2,
            2,
            2 * owners,
            2 * owners,
            shares,
            shares,
            4,
            4,
            owners,
            owners,
            owners + dps,
            owners + dps,
            2,
        ],
        [
            d_parts,
            sel_ffn,
            state,
            inv_two,
            cotangent[0],
            gains,
            sel_att,
            gate_columns,
            out_full,
            queries,
            pairs,
            row_info,
            cos_slot,
            sin_slot,
            cos_key,
            -sin_key,
            place,
            d_both.reshape(2 * owners * used, units),
            hidden,
            output_part,
            tokens[0],
            inv_one,
            mixed,
            first_full,
            normed,
            features_all,
        ],
        far_args=(17, 18, 23, 24, 25),
        far_outs=(4, 5, 6, 7, 8),
    )
    chunk = HD // local
    place = lax.rem(own, chunk) * local
    gain_grads = lax.dynamic_slice_in_dim(gain_grads, place, local, 1)
    query_grad = map_grads[:, :, :head_width].astype(F32)
    out_grad = jnp.swapaxes(map_grads[:, :, head_width + HD :].astype(F32), 1, 2)
    kv_grad = map_grads[:, :, head_width : head_width + HD].reshape(columns, 2, local, HD)
    kv_grad = jnp.transpose(kv_grad, (2, 1, 0, 3)).reshape(local, 2, head_width).astype(F32)
    return (
        output[None],
        input_grad[None],
        kv_grad,
        query_grad,
        out_grad,
        gain_grads[0],
        gain_grads[1],
        gate_grad[None],
        up_grad[None],
        down_grad[None],
    )


def solution(mesh):
    in_specs = (
        P("dp", "expert", None),
        P("dp", "expert", None),
        P("dp", None),
        P("dp", "expert", None),
        P("dp", "expert", None),
        P("dp", "expert", None),
        P("dp", "expert", None),
        P(("dp", "expert"), None, "tensor"),
        P(None, ("dp", "expert"), "tensor"),
        P(None, "tensor", ("dp", "expert")),
        P(("dp", "expert")),
        P(("dp", "expert")),
        P("expert", "dp", "tensor"),
        P("expert", "dp", "tensor"),
        P("expert", "tensor", "dp"),
    )
    out_specs = (
        P("dp", "expert", None),
        P("dp", "expert", None),
        P(("dp", "expert"), None, "tensor"),
        P(None, ("dp", "expert"), "tensor"),
        P(None, "tensor", ("dp", "expert")),
        P(("dp", "expert")),
        P(("dp", "expert")),
        P("expert", "dp", "tensor"),
        P("expert", "dp", "tensor"),
        P("expert", "tensor", "dp"),
    )
    return jax.shard_map(
        per_device, mesh=mesh, in_specs=in_specs, out_specs=out_specs, check_vma=False
    )
```

```python
import jax
import jax.numpy as jnp
import numpy as np
from jax import lax
from jax.experimental import pallas as pl
from jax.experimental.pallas import tpu as pltpu
from jax.sharding import PartitionSpec as P

HD = 128
ATT_EXP = 8
TOPK = 2
EPSILON = 1e-06
BF = jnp.bfloat16
F32 = jnp.float32


def remote(src, dst, send, recv, device):
    return pltpu.make_async_remote_copy(
        src_ref=src,
        dst_ref=dst,
        send_sem=send,
        recv_sem=recv,
        device_id=device,
        device_id_type=pl.DeviceIdType.MESH,
    )


def each(count, body, start=1):
    def step(index, carry):
        body(index)
        return carry

    lax.fori_loop(start, count, step, 0)


def mm(left, right, left_dim=1, right_dim=0, precision=None):
    return lax.dot_general(
        left,
        right,
        (((left_dim,), (right_dim,)), ((), ())),
        precision=precision,
        preferred_element_type=F32,
    )


def enter(own, half, core, owners, around=(), greeted=0):
    semaphore = pltpu.get_barrier_semaphore()
    for index in around:
        pl.semaphore_signal(
            semaphore, inc=1, device_id={"dp": index}, device_id_type=pl.DeviceIdType.MESH
        )

    def hello(expert, tensor):
        pl.semaphore_signal(
            semaphore,
            inc=1,
            device_id={"expert": expert, "tensor": tensor},
            device_id_type=pl.DeviceIdType.MESH,
        )

    def column(step):
        hello(
            lax.rem(own + lax.div(step, 2), owners),
            2 * lax.rem(half + lax.rem(step, 2), 2) + core,
        )

    each(2 * owners, column)
    hello(own, 2 * half + 1 - core)
    hello(own, 2 * (1 - half) + 1 - core)
    pl.semaphore_wait(semaphore, 2 * owners + 1 + len(around) + greeted)


def send_home(merged, landing, sends, recvs, own, half, core, owners):
    def outgoing(step):
        to, side = lax.rem(own + lax.div(step, 2), owners), lax.rem(half + lax.rem(step, 2), 2)
        return remote(
            merged.at[side, to],
            landing.at[half, own],
            sends.at[step],
            recvs.at[step],
            {"expert": to, "tensor": 2 * side + core},
        )

    each(2 * owners, lambda step: outgoing(step).start())
    landing[half, own] = merged[half, own]
    return outgoing


def wait_home(outgoing, owners):
    each(2 * owners, lambda step: outgoing(step).wait())


def share_start(slices, sends, recvs, own, share, shares):
    def copy(step):
        return remote(
            slices.at[share],
            slices.at[share],
            sends.at[step],
            recvs.at[step],
            {"expert": own, "tensor": lax.rem(share + step, shares)},
        )

    each(shares, lambda step: copy(step).start())
    return copy


def share_slices(slices, sends, recvs, own, share, shares):
    copy = share_start(slices, sends, recvs, own, share, shares)
    each(shares, lambda step: copy(step).wait())


class Ring:
    def __init__(self, buffer, sends, recvs, base, index, count):
        self.buffer, self.sends, self.recvs, self.base = buffer, sends, recvs, base
        self.index = index
        self.after, self.before = lax.rem(index + 1, count), lax.rem(index + count - 1, count)
        self.cut = buffer.shape[1] // 2

    def copy(self, kind, source=None):
        buffer, cut = self.buffer, self.cut
        if kind < 2:
            src = buffer.at[self.index] if source is None else source
            dst = buffer.at[self.index]
        elif kind == 2:
            src = dst = buffer.at[self.before, pl.ds(0, cut)]
        else:
            src = dst = buffer.at[self.after, pl.ds(cut, cut)]
        place = self.base + kind
        device = {"dp": self.after if kind % 2 == 0 else self.before}
        return remote(src, dst, self.sends.at[place], self.recvs.at[place], device)

    def start(self, source=None):
        self.copy(0, source).start()
        self.copy(1, source).start()

    def forward(self):
        self.copy(0).wait_recv()
        self.copy(2).start()
        self.copy(1).wait_recv()
        self.copy(3).start()

    def finish(self):
        self.copy(2).wait_recv()
        self.copy(3).wait_recv()

    def drain(self, source=None):
        self.copy(0, source).wait_send()
        self.copy(1, source).wait_send()
        self.copy(2).wait_send()
        self.copy(3).wait_send()


def first_kernel(
    tokens,
    marks,
    own_gains,
    pack_one,
    query_weight,
    pack_two,
    gate_weight,
    up_weight,
    down_weight,
    upstream,
    lengths,
    cos_key,
    sin_key,
    far_first,
    far_out,
    far_normed,
    gains,
    inv_one,
    queries,
    pairs,
    row_info,
    cos_slot,
    sin_slot,
    place,
    mixed,
    state,
    inv_two,
    features_all,
    hidden,
    d_both,
    d_parts,
    output_part,
    sel_ffn,
    sel_att,
    gate_columns,
    first_full,
    out_full,
    normed,
    pick_ffn,
    features,
    expert_in,
    expert_grad,
    routes,
    gain_parts,
    slot_keys,
    inv_all,
    heads_out,
    mixed_out,
    mixed_in,
    far,
    near,
    sibling,
    landing,
    landing_two,
    slices,
    rows_out,
    grads_out,
    gate_up,
    down,
    act,
    ring_send,
    ring_recv,
    local,
    pack_send,
    pack_recv,
    token_send,
    token_recv,
    mark_send,
    mark_recv,
    one_send,
    one_recv,
    head_send,
    head_recv,
    back_send,
    back_recv,
    home_send,
    home_recv,
    home_two_send,
    home_two_recv,
    slice_send,
    slice_recv,
    row_send,
    row_recv,
    grad_send,
    grad_recv,
    feature_send,
    feature_recv,
    gain_send,
    gain_recv,
):
    own, share, dp = lax.axis_index("expert"), lax.axis_index("tensor"), lax.axis_index("dp")
    owners, shares, dps = heads_out.shape[0], slices.shape[0], first_full.shape[0]
    half, core = lax.div(share, 2), lax.rem(share, 2)
    group, piece = slices.shape[1], slices.shape[2]
    width = shares * piece
    wide = width // 2
    slots = rows_out.shape[1]
    rows = owners * slots
    head_rows = heads_out.shape[1]
    columns = owners // 2
    part = lax.rem(own, 2)
    local_rows = pack_one.shape[1]
    units = gate_weight.shape[1]
    other = {"expert": own, "tensor": 2 * half + 1 - core}
    enter(own, half, core, owners, [lax.rem(dp + step, dps) for step in range(1, dps)])

    down_ring = Ring(down, ring_send, ring_recv, 0, dp, dps)
    one_ring = Ring(first_full, ring_send, ring_recv, 4, dp, dps)
    two_ring = Ring(out_full, ring_send, ring_recv, 8, dp, dps)
    up_ring = Ring(gate_up.at[1], ring_send, ring_recv, 12, dp, dps)
    low, high = pl.ds(0, piece // 2), pl.ds(piece // 2, piece // 2)
    low_ring = Ring(gate_up.at[0, :, low], ring_send, ring_recv, 16, dp, dps)
    high_ring = Ring(gate_up.at[0, :, high], ring_send, ring_recv, 20, dp, dps)
    own_rows = pl.ds(pl.multiple_of(own * local_rows, local_rows), local_rows)

    def to_owner(src, dst, sends, recvs, step):
        to = lax.rem(own + step, owners)
        device = {"expert": to, "tensor": share}
        return remote(src(to), dst, sends.at[step], recvs.at[step], device)

    key_cut, query_cut = pl.ds(0, HD), pl.ds(HD, first_full.shape[2] - HD)

    def pack_copy(step):
        target = first_full.at[dp, own_rows, key_cut]
        return to_owner(pack_one.at.__getitem__, target, pack_send, pack_recv, step)

    def query_part_copy(step):
        to = lax.rem(own + step, owners)
        return remote(
            query_weight.at[to],
            first_full.at[dp, own_rows, query_cut],
            pack_send.at[2 * owners + step],
            pack_recv.at[2 * owners + step],
            {"expert": to, "tensor": share},
        )

    def second_copy(step):
        to = lax.rem(own + step, owners)
        return remote(
            pack_two.at[to],
            out_full.at[dp, own_rows],
            pack_send.at[owners + step],
            pack_recv.at[owners + step],
            {"expert": to, "tensor": share},
        )

    def token_copy(step):
        start = pl.multiple_of(core * wide, wide)
        return to_owner(
            lambda to: tokens.at[:, pl.ds(start, wide)],
            normed.at[core, own],
            token_send,
            token_recv,
            step,
        )

    def mark_copy(step):
        return to_owner(lambda to: marks, routes.at[own], mark_send, mark_recv, step)

    each(owners, lambda step: query_part_copy(step).start())
    each(owners, lambda step: pack_copy(step).start())
    each(owners, lambda step: mark_copy(step).start())

    def gain_copy(step):
        return to_owner(lambda to: own_gains, gain_parts.at[dp, own], gain_send, gain_recv, step)

    def far_gain_copy(step):
        to = lax.rem(dp + step, dps)
        place = owners + step
        return remote(
            gain_parts.at[dp],
            gain_parts.at[dp],
            gain_send.at[place],
            gain_recv.at[place],
            {"dp": to},
        )

    gain_parts[dp, own] = own_gains[...]
    each(owners, lambda step: gain_copy(step).start())
    low_ring.start(gate_weight.at[low])
    own_copies = [
        pltpu.make_async_copy(pack_one.at[own], first_full.at[dp, own_rows, key_cut], local.at[0]),
        pltpu.make_async_copy(pack_two.at[own], out_full.at[dp, own_rows], local.at[1]),
        pltpu.make_async_copy(gate_weight, gate_up.at[0, dp], local.at[2]),
        pltpu.make_async_copy(up_weight, gate_up.at[1, dp], local.at[3]),
        pltpu.make_async_copy(down_weight, down.at[dp], local.at[4]),
    ]
    for copy in own_copies:
        copy.start()
    routes[own] = marks[...]
    normed[core, own] = tokens[:, pl.ds(pl.multiple_of(core * wide, wide), wide)]

    own_query = pltpu.make_async_copy(
        query_weight.at[own], first_full.at[dp, own_rows, query_cut], local.at[8]
    )
    own_query.start()
    own_copies[0].wait()
    own_query.wait()
    each(owners, lambda step: query_part_copy(step).wait())
    each(owners, lambda step: pack_copy(step).wait())
    one_ring.start()
    high_ring.start(gate_weight.at[high])
    each(owners, lambda step: token_copy(step).start())
    each(owners, lambda step: second_copy(step).start())
    each(owners, lambda step: mark_copy(step).wait())
    each(owners, lambda step: gain_copy(step).wait())
    each(dps, lambda step: far_gain_copy(step).start())

    def picked_rows(source, out, scale):
        for index in range(2):
            cut = pl.ds(pl.multiple_of(core * wide + index * piece, piece), piece)
            taken = mm(sel_ffn[...], source[:, cut])
            if scale is not None:
                taken = taken * scale
            taken = taken.astype(BF).reshape(owners, slots, piece)
            out[:, :, index * piece : (index + 1) * piece] = taken


    def grad_copy(step):
        return to_owner(grads_out.at.__getitem__, expert_grad.at[core, own], grad_send, grad_recv, step)

    token_rows = lax.broadcasted_iota(jnp.int32, (group, group), 0)
    token_columns = lax.broadcasted_iota(jnp.int32, (group, group), 1)
    before = (token_rows < token_columns).astype(F32).astype(BF)
    token_names = token_rows.astype(F32).astype(BF)
    slot_names = lax.broadcasted_iota(jnp.int32, (slots, group), 0).astype(F32)
    first_routes = jnp.concatenate([routes[index, 0:1, :] for index in range(owners)], 0)
    second_routes = jnp.concatenate([routes[index, 1:2, :] for index in range(owners)], 0)

    def map_keys(name):
        member = (first_routes == name) | (second_routes == name)
        rank = mm(jnp.where(member, 1.0, 0.0).astype(BF), before)
        return jnp.where(member, rank, -1.0)

    for name in range(owners):
        slot_keys[name] = map_keys(float(name))

    gate_columns[...] = jnp.transpose(marks[...])
    names = lax.broadcasted_iota(jnp.int32, (owners, group), 0).astype(F32)
    member = (marks[2:3, :] == names) | (marks[3:4, :] == names)
    rank = mm(jnp.where(member, 1.0, 0.0).astype(BF), before)
    ffn_keys = jnp.where(member, rank, -1.0)
    gate_slots = []
    for name in range(owners):
        cut = slice(name * slots, (name + 1) * slots)
        key = slot_keys[name, pl.ds(own, 1), :]
        hot = jnp.where(key == slot_names, 1.0, 0.0)
        for choice in range(TOPK):
            chosen_here = jnp.where(marks[choice : choice + 1, :] == float(name), hot, 0.0)
            sel_att[cut, choice * group : (choice + 1) * group] = chosen_here.astype(BF)
        hot = jnp.where(ffn_keys[name : name + 1, :] == slot_names, 1.0, 0.0)
        sel_ffn[cut, :] = hot.astype(BF)
        gate = jnp.zeros((slots, 1), F32)
        for choice in range(TOPK):
            chosen_here = jnp.where(marks[2 + choice : 3 + choice, :] == float(name), hot, 0.0)
            pick_ffn[cut, choice * group : (choice + 1) * group] = chosen_here.astype(BF)
            weighed = chosen_here * marks[6 + choice : 7 + choice, :]
            gate = gate + jnp.sum(weighed, 1, keepdims=True)
        gate_slots.append(gate)
    picked_rows(upstream, grads_out, jnp.concatenate(gate_slots, 0))

    def one_hot(name, block):
        key = slot_keys[name, pl.ds(block, 1), :]
        return jnp.where(key == slot_names, 1.0, 0.0)

    def table(hot, array, block):
        span = pl.ds(pl.multiple_of(block * group, group), group)
        return mm(hot, array[span, :], precision=lax.Precision.HIGHEST)

    def row_block(index, carry):
        name, block = lax.div(index, columns), part * columns + lax.rem(index, columns)
        hot = one_hot(name, block)
        pos = mm(hot.astype(BF), token_names) + (block * group).astype(F32)
        start, bound = jnp.zeros_like(pos), jnp.zeros((1, group), F32)
        for document in range(lengths.shape[0]):
            bound = bound + lengths[document : document + 1, :]
            start = jnp.maximum(start, jnp.where(bound <= pos, bound, 0.0))
        span = pl.ds(pl.multiple_of(index * slots, slots), slots)
        row_info[span, 0:1] = pos[:, 0:1]
        row_info[span, 1:2] = start[:, 0:1]
        return carry

    lax.fori_loop(0, owners * columns, row_block, 0)

    each(owners, lambda step: token_copy(step).wait())
    across = remote(normed.at[core], normed.at[core], one_send.at[0], one_recv.at[0], other)
    across.start()
    each(owners, lambda step: grad_copy(step).start())
    expert_grad[core, own] = grads_out[own]
    own_copies[1].wait()
    each(owners, lambda step: second_copy(step).wait())
    one_ring.forward()
    two_ring.start()
    low_ring.forward()
    up_ring.start(up_weight)
    across.wait()

    def squares(index, carry):
        low, high = normed[0, index].astype(F32), normed[1, index].astype(F32)
        total = jnp.sum(low * low, 1, keepdims=True) + jnp.sum(high * high, 1, keepdims=True)
        inv_all[index] = lax.rsqrt(total / width + EPSILON)
        return carry

    lax.fori_loop(0, owners, squares, 0)
    inv_one[...] = inv_all[own]
    one_ring.finish()
    kept = [pltpu.make_async_copy(first_full, far_first, local.at[5])]
    kept[0].start()

    each(dps, lambda step: far_gain_copy(step).wait())
    left = lax.broadcasted_iota(jnp.int32, (8, HD), 1) < HD // 2
    for index in range(dps * owners // 2):
        name, side = index // columns, 2 * (index % columns)
        turned = pltpu.roll(gain_parts[name, side + 1], HD // 2, 1)
        joined = jnp.where(left, gain_parts[name, side], turned)
        gains[:, index * HD : (index + 1) * HD] = joined[0:2, :]

    chosen = expert_in
    def norm_block(index, carry):
        hot = one_hot(own, index)
        place[index] = hot.astype(BF)
        span = pl.ds(pl.multiple_of(index * slots, slots), slots)
        cos_slot[span, :] = table(hot, cos_key, index)
        sin_slot[span, :] = table(hot, sin_key, index)
        for side in range(2):
            cut = slice(side * wide, (side + 1) * wide)
            rounded = normed[side, index].astype(F32) * inv_all[index] * gains[0:1, cut]
            rounded = rounded.astype(BF)
            normed[side, index] = rounded
            chosen[side, index] = mm(hot.astype(BF), rounded).astype(BF)
        return carry

    lax.fori_loop(0, owners, norm_block, 0)
    kept.append(pltpu.make_async_copy(normed, far_normed, local.at[6]))
    kept[1].start()
    query = jnp.zeros((rows, columns * HD), F32)
    for index in range(dps):
        cut = slice((index % 2) * piece, (index % 2 + 1) * piece)
        taken = chosen[index // 2, :, :, cut].reshape(rows, piece)
        query = query + mm(taken, first_full[index, :, HD:])
    for column in range(columns):
        head = query[:, column * HD : (column + 1) * HD]
        head = (head * cos_slot[...] + pltpu.roll(head, HD // 2, 1) * sin_slot[...]).astype(BF)
        for side in range(2):
            heads_out[2 * column + side] = head[side * head_rows : (side + 1) * head_rows]

    def head_copy(step):
        return to_owner(heads_out.at.__getitem__, queries.at[own], head_send, head_recv, step)

    each(owners, lambda step: head_copy(step).start())
    queries[own] = heads_out[own]

    first = part == 0

    def key_block(index, carry):
        taken = jnp.zeros((group, HD), F32)
        for step in range(dps):
            cut = slice((step % 2) * piece, (step % 2 + 1) * piece)
            taken = taken + mm(normed[step // 2, index, :, cut], first_full[step, :, :HD])
        span = pl.ds(pl.multiple_of(index * group, group), group)
        turned = taken * cos_key[span, :] + pltpu.roll(taken, HD // 2, 1) * sin_key[span, :]
        pairs[part, span, :] = jnp.where(first, turned, taken).astype(BF)
        return carry

    lax.fori_loop(0, owners, key_block, 0)
    pair = {"expert": own + 1 - 2 * part, "tensor": share}
    swapped = remote(pairs.at[part], pairs.at[part], one_send.at[10], one_recv.at[10], pair)
    swapped.start()

    scale = HD ** (-0.5)
    key_pos = lax.broadcasted_iota(jnp.int32, (1, owners * group), 1).astype(F32)

    def attend(index):
        span = pl.ds(pl.multiple_of(index * head_rows, head_rows), head_rows)
        scores = mm(queries[index], pairs[0], 1, 1) * scale
        visible = (key_pos <= row_info[span, 0:1]) & (key_pos >= row_info[span, 1:2])
        scores = jnp.where(visible, scores, -1e30)
        top = jnp.max(scores, 1, keepdims=True)
        shifted = jnp.exp(scores - top)
        total = jnp.sum(shifted, 1, keepdims=True)
        row_info[span, 2:3] = top + jnp.log(total)
        probs = (shifted / total).astype(BF)
        mixed_out[index] = mm(probs, pairs[1]).astype(BF)

    def back_copy(step):
        to = lax.rem(own + owners - step, owners)
        return remote(
            mixed_out.at[to],
            mixed_in.at[own],
            back_send.at[step],
            back_recv.at[step],
            {"expert": to, "tensor": share},
        )

    def attend_other(step):
        head_copy(step).wait()
        attend(lax.rem(own + owners - step, owners))
        back_copy(step).start()

    swapped.wait()
    attend(own)
    mixed_in[own] = mixed_out[own]
    each(owners, attend_other)
    two_ring.forward()
    high_ring.forward()
    down_ring.start(down_weight)
    two_ring.finish()
    kept.append(pltpu.make_async_copy(out_full, far_out, local.at[7]))
    kept[2].start()
    each(owners, lambda step: back_copy(step).wait())
    for column in range(columns):
        for side in range(2):
            mixed[
                side * head_rows : (side + 1) * head_rows, column * HD : (column + 1) * HD
            ] = mixed_in[2 * column + side]

    def chip_start(product, base):
        def across(side):
            place = base + side
            return remote(far.at[side], sibling.at[side], one_send.at[place], one_recv.at[place], other)

        for side in range(2):
            far[side] = product(2 * side + 1 - core)
            across(side).start()
        for side in range(2):
            near[side] = product(2 * side + core)

        def finish():
            for side in range(2):
                across(side).wait()
                near[side] = (near[side].astype(F32) + sibling[side].astype(F32)).astype(BF)

        return finish

    def at_tokens(pick, gate, landing):
        total = jnp.zeros((group, piece), F32)
        for choice in range(TOPK):
            span = slice(choice * group, (choice + 1) * group)
            taken = mm(pick[:, span], landing[0].reshape(rows, piece), 0, 0)
            taken = taken + mm(pick[:, span], landing[1].reshape(rows, piece), 0, 0)
            total = total + gate_columns[:, gate + choice : gate + choice + 1] * taken
        return total

    def map_product(index):
        return mm(mixed[...], out_full[index], 1, 1).astype(BF).reshape(owners, slots, piece)

    chip_start(map_product, 1)()
    outgoing = send_home(near, landing, home_send, home_recv, own, half, core, owners)
    up_ring.forward()
    wait_home(outgoing, owners)
    slices[share] = at_tokens(sel_att, 4, landing).astype(BF)
    share_slices(slices, slice_send, slice_recv, own, share, shares)

    total = jnp.zeros((group, 1), F32)
    for index in range(shares):
        cut = slice(index * piece, (index + 1) * piece)
        value = tokens[:, cut].astype(F32) + slices[index].astype(F32)
        state[:, cut] = value
        total = total + jnp.sum(value * value, 1, keepdims=True)
    inv = lax.rsqrt(total / width + EPSILON)
    inv_two[...] = inv
    for index in range(2):
        cut = pl.ds(pl.multiple_of(core * wide + index * piece, piece), piece)
        rounded = (state[:, cut] * inv * gains[1:2, cut]).astype(BF)
        taken = mm(sel_ffn[...], rounded).astype(BF).reshape(owners, slots, piece)
        rows_out[:, :, index * piece : (index + 1) * piece] = taken

    def row_copy(step):
        return to_owner(rows_out.at.__getitem__, expert_in.at[core, own], row_send, row_recv, step)

    each(owners, lambda step: row_copy(step).start())
    expert_in[core, own] = rows_out[own]
    each(owners, lambda step: grad_copy(step).wait())
    across = remote(expert_grad.at[core], expert_grad.at[core], one_send.at[5], one_recv.at[5], other)
    across.start()
    each(owners, lambda step: row_copy(step).wait())
    across_rows = remote(expert_in.at[core], expert_in.at[core], one_send.at[6], one_recv.at[6], other)
    across_rows.start()
    across.wait()
    across_rows.wait()

    used = hidden.shape[0] // owners

    def tight(array):
        pieces = [array[index * slots : index * slots + used] for index in range(owners)]
        return jnp.concatenate(pieces, 0)

    def loose(array):
        blank = jnp.zeros((slots - used, array.shape[1]), F32)
        pieces = []
        for index in range(owners):
            pieces += [array[index * used : (index + 1) * used], blank]
        return jnp.concatenate(pieces, 0).astype(BF).reshape(owners, slots, piece)

    for index in range(dps):
        cut = slice((index % 2) * piece, (index % 2 + 1) * piece)
        for side, source in enumerate((expert_in, expert_grad)):
            taken = source[index // 2, :, :, cut].reshape(rows, piece).astype(F32)
            features[side, index] = tight(taken).astype(BF)
    def feature_copy(step):
        to = lax.rem(dp + step, dps)
        return remote(
            features.at[core, to],
            features_all.at[core, dp],
            feature_send.at[step],
            feature_recv.at[step],
            {"dp": to},
        )

    keep = pltpu.make_async_copy(features.at[core, dp], features_all.at[core, dp], feature_send.at[0])
    keep.start()
    for copy in own_copies[2:]:
        copy.wait()
    tile = 2 * HD

    def unit_tiles(body):
        def step(index, carry):
            body(pl.ds(pl.multiple_of(index * tile, tile), tile))
            return carry

        lax.fori_loop(0, units // tile, step, 0)
        if units % tile:
            body(pl.ds(units - units % tile, units % tile))

    low_ring.finish()
    high_ring.finish()

    def gate_tile(cut):
        total = mm(features[0, 0], gate_up[0, 0, :, cut])
        for index in range(1, dps):
            total = total + mm(features[0, index], gate_up[0, index, :, cut])
        act[0, :, cut] = total

    unit_tiles(gate_tile)
    down_ring.forward()
    up_ring.finish()

    def up_tile(cut):
        up = mm(features[0, 0], gate_up[1, 0, :, cut])
        for index in range(1, dps):
            up = up + mm(features[0, index], gate_up[1, index, :, cut])
        act[1, :, cut] = up
        gate = act[0, :, cut]
        hidden[:, cut] = (gate / (1.0 + jnp.exp(-gate)) * up).astype(BF)

    unit_tiles(up_tile)
    down_ring.finish()
    each(dps, lambda step: feature_copy(step).start())
    finish_sum = chip_start(lambda index: loose(mm(hidden[...], down[index])), 7)

    def grad_tile(cut):
        grad = mm(features[1, 0], down[0, cut, :], 1, 1)
        for index in range(1, dps):
            grad = grad + mm(features[1, index], down[index, cut, :], 1, 1)
        gate, up = act[0, :, cut], act[1, :, cut]
        sigma = 1.0 / (1.0 + jnp.exp(-gate))
        d_both[0, :, cut] = (grad * up * sigma * (1.0 + gate * (1.0 - sigma))).astype(BF)
        d_both[1, :, cut] = (grad * gate * sigma).astype(BF)

    unit_tiles(grad_tile)
    finish_sum()
    outgoing_two = send_home(
        near, landing_two, home_two_send, home_two_recv, own, half, core, owners
    )
    for index in range(dps):
        total = mm(d_both[0], gate_up[0, index], 1, 1) + mm(d_both[1], gate_up[1, index], 1, 1)
        d_parts[index % 2, index // 2] = loose(total)
    keep.wait()
    each(dps, lambda step: feature_copy(step).wait())
    across = remote(
        features_all.at[core], features_all.at[core], one_send.at[9], one_recv.at[9], other
    )
    across.start()
    wait_home(outgoing_two, owners)
    rest = at_tokens(pick_ffn, 6, landing_two)
    span = pl.ds(pl.multiple_of(share * piece, piece), piece)
    output_part[...] = (state[:, span] + rest).astype(BF)
    across.wait()
    for copy in kept:
        copy.wait()
    one_ring.drain()
    two_ring.drain()
    low_ring.drain(gate_weight.at[low])
    high_ring.drain(gate_weight.at[high])
    up_ring.drain(up_weight)
    down_ring.drain(down_weight)


def back_kernel(
    parts,
    sel_ffn,
    state,
    inv_two,
    upstream,
    gains,
    sel_att,
    gate_columns,
    out_full,
    queries,
    pairs,
    row_info,
    cos_slot,
    sin_slot,
    cos_key,
    sin_key,
    place,
    d_both,
    hidden,
    output_part,
    tokens,
    inv_one,
    mixed,
    far_weights,
    far_normed,
    far_features,
    output,
    input_grad,
    gain_grads,
    maps_in,
    gate_grad,
    up_grad,
    down_grad,
    d_both_all,
    hidden_all,
    d_gain_two,
    d_rows,
    d_proj,
    return_in,
    parts_joined,
    rows_out,
    heads_out,
    heads_in,
    queries_out,
    queries_in,
    pair_out,
    pair_in,
    d_keys,
    d_values,
    far,
    near,
    sibling,
    landing,
    slices,
    map_grads,
    early,
    late,
    gain_out,
    gain_in,
    gain_mid,
    gain_last,
    weights,
    normed,
    features,
    acts,
    features_turned,
    wide_tiles,
    tall_tiles,
    first_send,
    first_recv,
    return_send,
    return_recv,
    join_send,
    join_recv,
    row_send,
    row_recv,
    head_send,
    head_recv,
    back_send,
    back_recv,
    ring_send,
    ring_recv,
    local,
    one_send,
    one_recv,
    home_send,
    home_recv,
    slice_send,
    slice_recv,
    step_send,
    step_recv,
    map_send,
    map_recv,
    gain_send,
    gain_recv,
    tile_sem,
):
    own, share = lax.axis_index("expert"), lax.axis_index("tensor")
    owners, shares = heads_out.shape[0], parts_joined.shape[0]
    half, core = lax.div(share, 2), lax.rem(share, 2)
    piece, width = parts_joined.shape[2], state.shape[1]
    slots = rows_out.shape[1]
    rows = owners * slots
    wide = width // 2
    head_rows = heads_out.shape[1]
    columns = owners // 2
    other = {"expert": own, "tensor": 2 * half + 1 - core}
    dp, dps = lax.axis_index("dp"), d_both_all.shape[0]

    enter(own, half, core, owners, [lax.rem(dp + step, dps) for step in range(1, dps)])
    loads = [
        pltpu.make_async_copy(far_weights, weights, local.at[4]),
        pltpu.make_async_copy(far_normed, normed, local.at[5]),
        pltpu.make_async_copy(far_features.at[1], features, local.at[6]),
        pltpu.make_async_copy(far_features.at[0], acts.at[:, :, pl.ds(0, width // shares)], local.at[2]),
    ]
    for copy in loads:
        copy.start()

    both_ring = Ring(d_both_all, ring_send, ring_recv, 0, dp, dps)
    both_ring.start(d_both)
    hidden_ring = Ring(hidden_all, ring_send, ring_recv, 4, dp, dps)
    hidden_ring.start(hidden)

    used_slots = pl.ds(0, slots)
    return_near, return_out = sibling.at[:, :, used_slots], near.at[:, :, used_slots]
    across = remote(parts.at[1 - core], return_near, first_send.at[0], first_recv.at[0], other)
    across.start()
    across.wait()
    for side in range(2):
        return_out[side] = (parts[core, side].astype(F32) + return_near[side].astype(F32)).astype(BF)
    outgoing = send_home(return_out, return_in, return_send, return_recv, own, half, core, owners)
    loads[3].wait()
    for index in range(dps):
        features_turned[index] = jnp.transpose(acts[index, :, :piece].astype(F32)).astype(BF)
    wait_home(outgoing, owners)
    total = mm(sel_ffn[...], return_in[0].reshape(rows, piece), 0, 0)
    total = total + mm(sel_ffn[...], return_in[1].reshape(rows, piece), 0, 0)
    parts_joined[share] = total.astype(BF)
    share_slices(parts_joined, join_send, join_recv, own, share, shares)

    inv = inv_two[...]
    mean = jnp.zeros_like(inv)
    for index in range(shares):
        cut = slice(index * piece, (index + 1) * piece)
        grad, value = parts_joined[index].astype(F32), state[:, cut]
        mean = mean + jnp.sum(value * gains[1:2, cut] * grad, 1, keepdims=True)
        d_gain_two[:, cut] = jnp.sum(grad * value * inv, 0, keepdims=True)
    mean = mean * (inv * inv * inv / width)
    for index in range(shares):
        cut = slice(index * piece, (index + 1) * piece)
        grad = gains[1:2, cut] * parts_joined[index].astype(F32)
        input_grad[:, cut] = upstream[:, cut].astype(F32) + inv * grad - state[:, cut] * mean

    for index in range(2):
        start = pl.multiple_of(core * wide + index * piece, piece)
        grad = input_grad[:, pl.ds(start, piece)]
        both = jnp.concatenate(
            [(gate_columns[:, 4:5] * grad).astype(BF), (gate_columns[:, 5:6] * grad).astype(BF)], 0
        )
        picked = mm(sel_att[...], both).astype(BF).reshape(owners, slots, piece)
        rows_out[:, :, index * piece : (index + 1) * piece] = picked

    def row_copy(step):
        to = lax.rem(own + step, owners)
        return remote(
            rows_out.at[to],
            d_rows.at[core, own],
            row_send.at[step],
            row_recv.at[step],
            {"expert": to, "tensor": share},
        )

    each(owners, lambda step: row_copy(step).start())
    d_rows[core, own] = rows_out[own]
    each(owners, lambda step: row_copy(step).wait())
    across = remote(d_rows.at[core], d_rows.at[core], first_send.at[1], first_recv.at[1], other)
    across.start()

    def half_product(side):
        taken = d_rows[side].reshape(rows, wide)
        return mm(taken[:, :piece], out_full[2 * side]) + mm(taken[:, piece:], out_full[2 * side + 1])

    d_mixed = half_product(core)
    across.wait()
    d_mixed = (d_mixed + half_product(1 - core)).astype(BF)
    for column in range(columns):
        for part in range(2):
            heads_out[2 * column + part] = d_mixed[
                part * head_rows : (part + 1) * head_rows, column * HD : (column + 1) * HD
            ]

    def head_copy(step):
        to = lax.rem(own + step, owners)
        return remote(
            heads_out.at[to],
            heads_in.at[own],
            head_send.at[step],
            head_recv.at[step],
            {"expert": to, "tensor": share},
        )

    each(owners, lambda step: head_copy(step).start())
    heads_in[own] = heads_out[own]
    middle = columns * HD + HD
    for index in range(dps):
        cut = slice((index % 2) * piece, (index % 2 + 1) * piece)
        outs = d_rows[index // 2, :, :, cut].reshape(rows, piece)
        map_grads[index, :, middle:] = mm(outs, mixed[...], 0, 0).astype(BF)

    scale = HD ** (-0.5)
    key_pos = lax.broadcasted_iota(jnp.int32, (1, pairs.shape[1]), 1).astype(F32)
    d_keys[...] = jnp.zeros_like(d_keys)
    d_values[...] = jnp.zeros_like(d_values)

    def attend(index):
        span = pl.ds(pl.multiple_of(index * head_rows, head_rows), head_rows)
        query, key, value, grad = queries[index], pairs[0], pairs[1], heads_in[index]
        scores = mm(query, key, 1, 1) * scale
        visible = (key_pos <= row_info[span, 0:1]) & (key_pos >= row_info[span, 1:2])
        probs = jnp.where(visible, jnp.exp(scores - row_info[span, 2:3]), 0.0)
        d_probs = mm(grad, value, 1, 1)
        delta = jnp.sum(probs * d_probs, 1, keepdims=True)
        d_scores = (probs * (d_probs - delta)).astype(BF)
        queries_out[index] = (mm(d_scores, key) * scale).astype(BF)
        d_keys[...] += mm(d_scores, query, 0, 0)
        d_values[...] += mm(probs.astype(BF), grad, 0, 0)

    def query_copy(step):
        to = lax.rem(own + owners - step, owners)
        return remote(
            queries_out.at[to],
            queries_in.at[own],
            back_send.at[step],
            back_recv.at[step],
            {"expert": to, "tensor": share},
        )

    def attend_other(step):
        head_copy(step).wait()
        attend(lax.rem(own + owners - step, owners))
        query_copy(step).start()

    attend(own)
    queries_in[own] = queries_out[own]
    each(owners, attend_other)
    both_ring.forward()

    first = lax.rem(own, 2) == 0
    pair_out[...] = jnp.where(first, d_values[...], d_keys[...] * scale).astype(BF)
    pair = {"expert": own + 1 - 2 * lax.rem(own, 2), "tensor": share}
    across = remote(pair_out, pair_in, first_send.at[2], first_recv.at[2], pair)
    across.start()
    each(owners, lambda step: query_copy(step).wait())
    group = place.shape[2]
    for part in range(2):
        for index in range(columns):
            block = part * columns + index
            cut = slice(index * slots, (index + 1) * slots)
            span = slice(block * slots, (block + 1) * slots)
            turned = []
            for column in range(columns):
                grad = queries_in[2 * column + part, cut, :].astype(F32)
                back = pltpu.roll(grad, HD // 2, 1) * sin_slot[span, :]
                turned.append((grad * cos_slot[span, :] - back).astype(BF))
            picked = jnp.concatenate(turned, 1)
            d_proj[block * group : (block + 1) * group, : columns * HD] = mm(
                place[block], picked, 0, 0
            ).astype(BF)
    across.wait()
    mine = jnp.where(first, d_keys[...] * scale, d_values[...]) + pair_in[...].astype(F32)
    turned = mine * cos_key[...] + pltpu.roll(mine, HD // 2, 1) * sin_key[...]
    d_proj[:, columns * HD :] = jnp.where(first, turned, mine).astype(BF)

    group, piece = near.shape[2], near.shape[3]
    head_width = d_proj.shape[1] - HD
    local_rows = maps_in.shape[1]
    used, units = acts.shape[1], acts.shape[2]
    after, before = lax.rem(dp + 1, dps), lax.rem(dp + dps - 1, dps)
    facing = lax.rem(dp + 2, dps)
    for copy in loads[:3]:
        copy.wait()

    class load:
        def __init__(self, side):
            rows_here = pl.ds(0 if side == 2 else side * used, used)
            mine, others = (hidden, hidden_all) if side == 2 else (d_both, d_both_all)
            self.copies = [pltpu.make_async_copy(mine.at[rows_here], acts.at[dp], local.at[0])]
            for step in range(1, dps):
                index = lax.rem(dp + step, dps)
                self.copies.append(
                    pltpu.make_async_copy(
                        others.at[index, rows_here], acts.at[index], local.at[8 + step]
                    )
                )

        def start(self):
            for copy in self.copies:
                copy.start()

        def wait(self):
            for copy in self.copies:
                copy.wait()

    def map_grad(index):
        cut = pl.ds(pl.multiple_of(lax.rem(index, 2) * piece, piece), piece)
        inputs = normed[lax.div(index, 2), :, :, cut].reshape(owners * group, piece)
        return mm(inputs, d_proj[...], 0, 0)

    def keep_grad(index):
        map_grads[index, :, :middle] = map_grad(index).astype(BF)

    cut = piece // 2

    def step_copy(kind):
        to = {"dp": after if kind % 2 == 0 else before}
        sems = (step_send.at[kind], step_recv.at[kind])
        if kind < 2:
            span = pl.ds(kind * cut, cut)
            return remote(map_grads.at[facing, span], early.at[kind], *sems, to)
        return remote(map_grads.at[after if kind == 2 else before], late.at[kind - 2], *sems, to)

    keep_grad(facing)
    step_copy(0).start()
    step_copy(1).start()

    def product(index):
        queries = mm(d_proj[:, :head_width], weights[index, :, HD:], 1, 1)
        side = mm(d_proj[:, head_width:], weights[index, :, :HD], 1, 1)
        return (queries + side).reshape(owners, group, piece)

    def across(side):
        return remote(far.at[side], sibling.at[side], one_send.at[side], one_recv.at[side], other)

    for side in range(2):
        far[side] = product(2 * side + 1 - core).astype(BF)
        across(side).start()
    for side in range(2):
        near[side] = product(2 * side + core).astype(BF)
    for side in range(2):
        across(side).wait()
        near[side] = (near[side].astype(F32) + sibling[side].astype(F32)).astype(BF)
    outgoing = send_home(near, landing, home_send, home_recv, own, half, core, owners)

    keep_grad(after)
    keep_grad(before)
    step_copy(0).wait()
    step_copy(1).wait()
    top, bottom = slice(0, cut), slice(cut, 2 * cut)
    map_grads[after, top] = (map_grads[after, top].astype(F32) + early[0].astype(F32)).astype(BF)
    map_grads[before, bottom] = (
        map_grads[before, bottom].astype(F32) + early[1].astype(F32)
    ).astype(BF)
    step_copy(2).start()
    step_copy(3).start()
    hidden_ring.forward()
    both_ring.finish()
    load(0).start()
    keep_grad(dp)

    tile = 2 * HD
    whole, rest = units // tile, units % tile
    def unit_tiles(product, out, rows_first):
        def store(slot, span, size):
            if rows_first:
                return pltpu.make_async_copy(
                    tall_tiles.at[slot, pl.ds(0, size)], out.at[span], tile_sem.at[slot]
                )
            return pltpu.make_async_copy(
                wide_tiles.at[slot, :, pl.ds(0, size)], out.at[:, span], tile_sem.at[slot]
            )

        def put(slot, value, size):
            if rows_first:
                tall_tiles[slot, :size] = value.astype(BF)
            else:
                wide_tiles[slot, :, :size] = value.astype(BF)

        def pair(index, carry):
            for slot in range(2):
                span = pl.ds(pl.multiple_of((2 * index + slot) * tile, tile), tile)

                @pl.when(index > 0)
                def _(slot=slot, span=span):
                    store(slot, span, tile).wait()

                put(slot, product(span), tile)
                store(slot, span, tile).start()
            return carry

        lax.fori_loop(0, whole // 2, pair, 0)
        spans = [(0, pl.ds((whole - 2) * tile, tile), tile), (1, pl.ds((whole - 1) * tile, tile), tile)]
        for slot, span, size in spans:
            store(slot, span, size).wait()
        if whole % 2:
            span = pl.ds((whole - 1) * tile, tile)
            put(0, product(span), tile)
            store(0, span, tile).start()
        if rest:
            tail = pl.ds(whole * tile, rest)
            put(1, product(tail), rest)
            store(1, tail, rest).start()
            store(1, tail, rest).wait()
        if whole % 2:
            store(0, span, tile).wait()

    def wide_product(span):
        total = mm(features_turned[0], acts[0, :, span])
        for index in range(1, dps):
            total = total + mm(features_turned[index], acts[index, :, span])
        return total

    def tall_product(span):
        total = mm(acts[0, :, span], features[0], 0, 0)
        for index in range(1, dps):
            total = total + mm(acts[index, :, span], features[index], 0, 0)
        return total

    load(0).wait()
    unit_tiles(wide_product, gate_grad, False)
    load(1).start()

    wait_home(outgoing, owners)
    total = jnp.zeros((group, piece), F32)
    for side in range(2):
        for index in range(owners):
            total = total + landing[side, index].astype(F32)
    slices[share, 0] = total.astype(BF)
    slices[share, 1] = output_part[...]
    joining = share_start(slices, slice_send, slice_recv, own, share, shares)

    step_copy(2).wait()
    step_copy(3).wait()
    map_grads[dp] = (
        map_grads[dp].astype(F32) + late[0].astype(F32) + late[1].astype(F32)
    ).astype(BF)

    def home_rows(index):
        return pl.ds(pl.multiple_of(index * local_rows, local_rows), local_rows)

    def map_copy(step):
        to = lax.rem(own + step, owners)
        return remote(
            map_grads.at[dp, home_rows(to)],
            maps_in.at[own],
            map_send.at[step],
            map_recv.at[step],
            {"expert": to, "tensor": share},
        )

    each(owners, lambda step: map_copy(step).start())
    maps_in[own] = map_grads[dp, home_rows(own), :]

    load(1).wait()
    unit_tiles(wide_product, up_grad, False)

    each(shares, lambda step: joining(step).wait())
    inv = inv_one[...]
    mean = jnp.zeros_like(inv)
    for index in range(shares):
        span = slice(index * piece, (index + 1) * piece)
        grad, value = slices[index, 0].astype(F32), tokens[:, span].astype(F32)
        output[:, span] = slices[index, 1]
        mean = mean + jnp.sum(value * gains[0:1, span] * grad, 1, keepdims=True)
        gain_one = jnp.sum(grad * value * inv, 0, keepdims=True)
        for chunk in range(piece // HD):
            lanes = slice(chunk * HD, (chunk + 1) * HD)
            place = index * (piece // HD) + chunk
            gain_out[index, chunk, 0:1] = gain_one[:, lanes]
            gain_out[index, chunk, 1:2] = d_gain_two[:, place * HD : (place + 1) * HD]

    def gain_copy(step):
        to = lax.rem(own + step, owners)
        return remote(
            gain_out.at[:, lax.div(to, 2)],
            gain_in.at[own],
            gain_send.at[step],
            gain_recv.at[step],
            {"expert": to, "tensor": share},
        )

    def far_gain_copy(step):
        to = lax.rem(dp + step, dps)
        return remote(
            gain_mid.at[to],
            gain_last.at[dp],
            gain_send.at[owners + step],
            gain_recv.at[owners + step],
            {"dp": to},
        )

    each(owners, lambda step: gain_copy(step).start())
    gain_in[own] = gain_out[:, lax.div(own, 2)]
    mean = mean * (inv * inv * inv / width)
    for index in range(shares):
        span = slice(index * piece, (index + 1) * piece)
        grad = gains[0:1, span] * slices[index, 0].astype(F32)
        value = tokens[:, span].astype(F32)
        input_grad[:, span] = input_grad[:, span] + inv * grad - value * mean
    hidden_ring.finish()
    load(2).start()
    each(owners, lambda step: gain_copy(step).wait())
    total = gain_in[0]
    for index in range(1, owners):
        total = total + gain_in[index]
    gain_mid[...] = total
    each(dps, lambda step: far_gain_copy(step).start())
    gain_last[dp] = gain_mid[dp]
    load(2).wait()
    unit_tiles(tall_product, down_grad, True)
    each(dps, lambda step: far_gain_copy(step).wait())
    total = gain_last[0, 0:2]
    for index in range(1, dps):
        total = total + gain_last[index, 0:2]
    gain_grads[...] = total
    each(owners, lambda step: map_copy(step).wait())
    both_ring.drain(d_both)
    hidden_ring.drain(hidden)


def call_kernel(kernel, collective_id, outs, scratch, semaphores, args, far_args=(), far_outs=()):
    def specs(count, far):
        spaces = [pl.ANY if index in far else pltpu.VMEM for index in range(count)]
        return [pl.BlockSpec(memory_space=space) for space in spaces]

    return pl.pallas_call(
        kernel,
        out_shape=[jax.ShapeDtypeStruct(shape, dtype) for shape, dtype in outs],
        in_specs=specs(len(args), far_args),
        out_specs=specs(len(outs), far_outs),
        scratch_shapes=[pltpu.VMEM(shape, dtype) for shape, dtype in scratch]
        + [pltpu.SemaphoreType.DMA((count,)) for count in semaphores],
        compiler_params=pltpu.CompilerParams(
            collective_id=collective_id, has_side_effects=True, vmem_limit_bytes=60 * 2**20
        ),
    )(*args)


def per_device(
    tokens,
    cotangent,
    doc_lengths,
    att_routes,
    att_gates,
    ffn_routes,
    ffn_gates,
    kv_weight,
    query_weight,
    out_weight,
    attn_gain,
    ffn_gain,
    gate_weight,
    up_weight,
    down_weight,
):
    _, group, width = tokens.shape
    owners = lax.axis_size("expert")
    shares = lax.axis_size("tensor")
    dps = lax.axis_size("dp")
    own = lax.axis_index("expert")
    share = lax.axis_index("tensor")
    columns = owners // 2
    column_half = own % 2
    att_cap = -(-min(group, group * TOPK * 5 // (4 * ATT_EXP)) // 16) * 16
    ffn_cap = -(-min(group, group * TOPK * 5 // (4 * owners)) // 16) * 16
    rows = owners * att_cap
    seq_len = owners * group
    piece = width // shares
    local = kv_weight.shape[0]
    head_width = kv_weight.shape[2]

    kv_parts = jnp.transpose(kv_weight.reshape(local, 2, columns, HD), (2, 1, 0, 3))
    pack_one = kv_parts.reshape(owners, local, HD)
    own_gains = jnp.stack([attn_gain, ffn_gain]).astype(F32)
    own_gains = jnp.pad(own_gains, ((0, 8 - 2), (0, HD - local)))
    pack_two = jnp.swapaxes(out_weight, 1, 2)
    marks = jnp.concatenate(
        [
            att_routes[0].T.astype(F32),
            ffn_routes[0].T.astype(F32),
            att_gates[0].T,
            ffn_gates[0].T,
        ],
        0,
    )
    lengths = jnp.broadcast_to(doc_lengths[0].astype(F32)[:, None], (doc_lengths.shape[1], HD))
    angles = np.arange(seq_len)[:, None] * 10000.0 ** (-np.arange(HD // 2) * 2.0 / HD)
    cos_key = jnp.asarray(np.concatenate([np.cos(angles)] * 2, 1), F32)
    sin_key = jnp.asarray(np.concatenate([-np.sin(angles), np.sin(angles)], 1), F32)
    used = min(group, group * TOPK * 5 // (4 * owners))
    units = gate_weight.shape[2]
    slots = att_cap
    head_rows = columns * slots
    block = (2, owners, slots, piece)
    (
        first_full,
        out_full,
        normed,
        gains,
        inv_one,
        queries,
        pairs,
        row_info,
        cos_slot,
        sin_slot,
        place,
        mixed,
        state,
        inv_two,
        features_all,
        hidden,
        d_both,
        d_parts,
        output_part,
        sel_ffn,
        sel_att,
        gate_columns,
    ) = call_kernel(
        first_kernel,
        3,
        [
            ((dps, owners * local, HD + head_width), BF),
            ((dps, owners * local, head_width), BF),
            ((2, owners, group, width // 2), BF),
            ((2, width), F32),
            ((group, 1), F32),
            ((owners, head_rows, HD), BF),
            ((2, seq_len, HD), BF),
            ((owners * head_rows, HD), F32),
            ((rows, HD), F32),
            ((rows, HD), F32),
            ((owners, slots, group), BF),
            ((rows, head_width), BF),
            ((group, width), F32),
            ((group, 1), F32),
            ((2, dps, owners * used, piece), BF),
            ((owners * used, units), BF),
            ((2, owners * used, units), BF),
            ((2,) + block, BF),
            ((group, piece), BF),
            ((rows, group), BF),
            ((rows, TOPK * group), BF),
            ((group, 8), F32),
        ],
        [
            ((dps, owners * local, HD + head_width), BF),
            ((dps, owners * local, head_width), BF),
            ((2, owners, group, width // 2), BF),
            ((rows, TOPK * group), BF),
            ((2, dps, owners * used, piece), BF),
            ((2, owners, slots, width // 2), BF),
            ((2, owners, slots, width // 2), BF),
            ((owners, 8, group), F32),
            ((dps, owners, 8, HD), F32),
            ((owners, owners, group), F32),
            ((owners, group, 1), F32),
            ((owners, head_rows, HD), BF),
            ((owners, head_rows, HD), BF),
            ((owners, head_rows, HD), BF),
        ]
        + [(block, BF)] * 5
        + [
            ((shares, group, piece), BF),
            ((owners, slots, width // 2), BF),
            ((owners, slots, width // 2), BF),
            ((2, dps, width // dps, units), BF),
            ((dps, units, piece), BF),
            ((2, owners * used, units), F32),
        ],
        [24, 24, 9, 3 * owners, 3 * owners]
        + [owners] * 4
        + [11, 11]
        + [owners] * 4
        + [2 * owners] * 4
        + [shares, shares]
        + [owners] * 4
        + [dps, dps]
        + [owners + dps] * 2,
        [
            tokens[0],
            marks,
            own_gains,
            pack_one,
            query_weight,
            pack_two,
            gate_weight[0],
            up_weight[0],
            down_weight[0],
            cotangent[0],
            lengths,
            cos_key,
            sin_key,
        ],
        far_args=(3, 4, 5, 6, 7, 8),
        far_outs=(0, 1, 2, 14),
    )

    grad_width = head_width + HD + head_width
    (
        output,
        input_grad,
        gain_grads,
        map_grads,
        gate_grad,
        up_grad,
        down_grad,
        *_,
    ) = call_kernel(
        back_kernel,
        1,
        [
            ((group, width), BF),
            ((group, width), F32),
            ((2, HD), F32),
            ((owners, local, grad_width), BF),
            ((piece, units), BF),
            ((piece, units), BF),
            ((units, piece), BF),
            ((dps, 2 * owners * used, units), BF),
            ((dps, owners * used, units), BF),
        ],
        [
            ((1, width), F32),
            ((2, owners, slots, width // 2), BF),
            ((seq_len, head_width + HD), BF),
            (block, BF),
            ((shares, group, piece), BF),
            ((owners, slots, width // 2), BF),
            ((owners, head_rows, HD), BF),
            ((owners, head_rows, HD), BF),
            ((owners, head_rows, HD), BF),
            ((owners, head_rows, HD), BF),
            ((seq_len, HD), BF),
            ((seq_len, HD), BF),
            ((seq_len, HD), F32),
            ((seq_len, HD), F32),
            ((2, owners, group, piece), BF),
            ((2, owners, group, piece), BF),
            ((2, owners, group, piece), BF),
            ((2, owners, group, piece), BF),
            ((shares, 2, group, piece), BF),
            ((dps, piece, grad_width), BF),
            ((2, piece // 2, grad_width), BF),
            ((2, piece, grad_width), BF),
            ((dps, owners // 2, 8, HD), F32),
            ((owners, dps, 8, HD), F32),
            ((dps, 8, HD), F32),
            ((dps, 8, HD), F32),
            ((dps, owners * local, HD + head_width), BF),
            ((2, owners, group, width // 2), BF),
            ((dps, owners * used, piece), BF),
            ((dps, owners * used, units), BF),
            ((dps, piece, owners * used), BF),
            ((2, piece, 2 * HD), BF),
            ((2, 2 * HD, piece), BF),
        ],
        [
            3,
            3,
            2 * owners,
            2 * owners,
            shares,
            shares,
            owners,
            owners,
            owners,
            owners,
            owners,
            owners,
            8,
            8,
            12,
            2,
            2,
            2 * owners,
            2 * owners,
            shares,
            shares,
            4,
            4,
            owners,
            owners,
            owners + dps,
            owners + dps,
            2,
        ],
        [
            d_parts,
            sel_ffn,
            state,
            inv_two,
            cotangent[0],
            gains,
            sel_att,
            gate_columns,
            out_full,
            queries,
            pairs,
            row_info,
            cos_slot,
            sin_slot,
            cos_key,
            -sin_key,
            place,
            d_both.reshape(2 * owners * used, units),
            hidden,
            output_part,
            tokens[0],
            inv_one,
            mixed,
            first_full,
            normed,
            features_all,
        ],
        far_args=(17, 18, 23, 24, 25),
        far_outs=(4, 5, 6, 7, 8),
    )
    chunk = HD // local
    place = lax.rem(own, chunk) * local
    gain_grads = lax.dynamic_slice_in_dim(gain_grads, place, local, 1)
    query_grad = map_grads[:, :, :head_width].astype(F32)
    out_grad = jnp.swapaxes(map_grads[:, :, head_width + HD :].astype(F32), 1, 2)
    kv_grad = map_grads[:, :, head_width : head_width + HD].reshape(columns, 2, local, HD)
    kv_grad = jnp.transpose(kv_grad, (2, 1, 0, 3)).reshape(local, 2, head_width).astype(F32)
    return (
        output[None],
        input_grad[None],
        kv_grad,
        query_grad,
        out_grad,
        gain_grads[0],
        gain_grads[1],
        gate_grad[None].astype(F32),
        up_grad[None].astype(F32),
        down_grad[None].astype(F32),
    )


def solution(mesh):
    in_specs = (
        P("dp", "expert", None),
        P("dp", "expert", None),
        P("dp", None),
        P("dp", "expert", None),
        P("dp", "expert", None),
        P("dp", "expert", None),
        P("dp", "expert", None),
        P(("dp", "expert"), None, "tensor"),
        P(None, ("dp", "expert"), "tensor"),
        P(None, "tensor", ("dp", "expert")),
        P(("dp", "expert")),
        P(("dp", "expert")),
        P("expert", "dp", "tensor"),
        P("expert", "dp", "tensor"),
        P("expert", "tensor", "dp"),
    )
    out_specs = (
        P("dp", "expert", None),
        P("dp", "expert", None),
        P(("dp", "expert"), None, "tensor"),
        P(None, ("dp", "expert"), "tensor"),
        P(None, "tensor", ("dp", "expert")),
        P(("dp", "expert")),
        P(("dp", "expert")),
        P("expert", "dp", "tensor"),
        P("expert", "dp", "tensor"),
        P("expert", "tensor", "dp"),
    )
    return jax.shard_map(
        per_device, mesh=mesh, in_specs=in_specs, out_specs=out_specs, check_vma=False
    )
```

```python
import jax
import jax.numpy as jnp
import numpy as np
from jax import lax
from jax.experimental import pallas as pl
from jax.experimental.pallas import tpu as pltpu
from jax.sharding import PartitionSpec as P

HD = 128
ATT_EXP = 8
TOPK = 2
EPSILON = 1e-06
BF = jnp.bfloat16
F32 = jnp.float32


def remote(src, dst, send, recv, device):
    return pltpu.make_async_remote_copy(
        src_ref=src,
        dst_ref=dst,
        send_sem=send,
        recv_sem=recv,
        device_id=device,
        device_id_type=pl.DeviceIdType.MESH,
    )


def each(count, body, start=1):
    def step(index, carry):
        body(index)
        return carry

    lax.fori_loop(start, count, step, 0)


def mm(left, right, left_dim=1, right_dim=0, precision=None):
    return lax.dot_general(
        left,
        right,
        (((left_dim,), (right_dim,)), ((), ())),
        precision=precision,
        preferred_element_type=F32,
    )


def enter(own, half, core, owners, around=(), greeted=0):
    semaphore = pltpu.get_barrier_semaphore()
    for index in around:
        pl.semaphore_signal(
            semaphore, inc=1, device_id={"dp": index}, device_id_type=pl.DeviceIdType.MESH
        )

    def hello(expert, tensor):
        pl.semaphore_signal(
            semaphore,
            inc=1,
            device_id={"expert": expert, "tensor": tensor},
            device_id_type=pl.DeviceIdType.MESH,
        )

    def column(step):
        hello(
            lax.rem(own + lax.div(step, 2), owners),
            2 * lax.rem(half + lax.rem(step, 2), 2) + core,
        )

    each(2 * owners, column)
    hello(own, 2 * half + 1 - core)
    hello(own, 2 * (1 - half) + 1 - core)
    pl.semaphore_wait(semaphore, 2 * owners + 1 + len(around) + greeted)


def send_home(merged, landing, sends, recvs, own, half, core, owners):
    def outgoing(step):
        to, side = lax.rem(own + lax.div(step, 2), owners), lax.rem(half + lax.rem(step, 2), 2)
        return remote(
            merged.at[side, to],
            landing.at[half, own],
            sends.at[step],
            recvs.at[step],
            {"expert": to, "tensor": 2 * side + core},
        )

    each(2 * owners, lambda step: outgoing(step).start())
    landing[half, own] = merged[half, own]
    return outgoing


def wait_home(outgoing, owners):
    each(2 * owners, lambda step: outgoing(step).wait())


def share_start(slices, sends, recvs, own, share, shares):
    def copy(step):
        return remote(
            slices.at[share],
            slices.at[share],
            sends.at[step],
            recvs.at[step],
            {"expert": own, "tensor": lax.rem(share + step, shares)},
        )

    each(shares, lambda step: copy(step).start())
    return copy


def share_slices(slices, sends, recvs, own, share, shares):
    copy = share_start(slices, sends, recvs, own, share, shares)
    each(shares, lambda step: copy(step).wait())


class Ring:
    def __init__(self, buffer, sends, recvs, base, index, count):
        self.buffer, self.sends, self.recvs, self.base = buffer, sends, recvs, base
        self.index = index
        self.after, self.before = lax.rem(index + 1, count), lax.rem(index + count - 1, count)
        self.cut = buffer.shape[1] // 2

    def copy(self, kind, source=None):
        buffer, cut = self.buffer, self.cut
        if kind < 2:
            src = buffer.at[self.index] if source is None else source
            dst = buffer.at[self.index]
        elif kind == 2:
            src = dst = buffer.at[self.before, pl.ds(0, cut)]
        else:
            src = dst = buffer.at[self.after, pl.ds(cut, cut)]
        place = self.base + kind
        device = {"dp": self.after if kind % 2 == 0 else self.before}
        return remote(src, dst, self.sends.at[place], self.recvs.at[place], device)

    def start(self, source=None):
        self.copy(0, source).start()
        self.copy(1, source).start()

    def forward(self):
        self.copy(0).wait_recv()
        self.copy(2).start()
        self.copy(1).wait_recv()
        self.copy(3).start()

    def finish(self):
        self.copy(2).wait_recv()
        self.copy(3).wait_recv()

    def drain(self, source=None):
        self.copy(0, source).wait_send()
        self.copy(1, source).wait_send()
        self.copy(2).wait_send()
        self.copy(3).wait_send()


def first_kernel(
    tokens,
    marks,
    own_gains,
    pack_one,
    query_weight,
    pack_two,
    gate_weight,
    up_weight,
    down_weight,
    upstream,
    lengths,
    cos_key,
    sin_key,
    far_first,
    far_out,
    far_normed,
    gains,
    inv_one,
    queries,
    pairs,
    row_info,
    cos_slot,
    sin_slot,
    place,
    mixed,
    state,
    inv_two,
    features_all,
    hidden,
    d_both,
    d_parts,
    output_part,
    sel_ffn,
    sel_att,
    gate_columns,
    first_full,
    out_full,
    normed,
    pick_ffn,
    features,
    expert_in,
    expert_grad,
    routes,
    gain_parts,
    slot_keys,
    inv_all,
    heads_out,
    mixed_out,
    mixed_in,
    far,
    near,
    sibling,
    landing,
    landing_two,
    sibling_two,
    slices,
    rows_out,
    grads_out,
    gate_up,
    down,
    act,
    ring_send,
    ring_recv,
    local,
    pack_send,
    pack_recv,
    token_send,
    token_recv,
    mark_send,
    mark_recv,
    one_send,
    one_recv,
    head_send,
    head_recv,
    back_send,
    back_recv,
    home_send,
    home_recv,
    home_two_send,
    home_two_recv,
    slice_send,
    slice_recv,
    row_send,
    row_recv,
    grad_send,
    grad_recv,
    feature_send,
    feature_recv,
    gain_send,
    gain_recv,
):
    own, share, dp = lax.axis_index("expert"), lax.axis_index("tensor"), lax.axis_index("dp")
    owners, shares, dps = heads_out.shape[0], slices.shape[0], first_full.shape[0]
    half, core = lax.div(share, 2), lax.rem(share, 2)
    group, piece = slices.shape[1], slices.shape[2]
    width = shares * piece
    wide = width // 2
    slots = rows_out.shape[1]
    rows = owners * slots
    head_rows = heads_out.shape[1]
    columns = owners // 2
    part = lax.rem(own, 2)
    local_rows = pack_one.shape[1]
    units = gate_weight.shape[1]
    other = {"expert": own, "tensor": 2 * half + 1 - core}
    enter(own, half, core, owners, [lax.rem(dp + step, dps) for step in range(1, dps)])

    down_ring = Ring(down, ring_send, ring_recv, 0, dp, dps)
    one_ring = Ring(first_full, ring_send, ring_recv, 4, dp, dps)
    two_ring = Ring(out_full, ring_send, ring_recv, 8, dp, dps)
    up_ring = Ring(gate_up.at[1], ring_send, ring_recv, 12, dp, dps)
    low, high = pl.ds(0, piece // 2), pl.ds(piece // 2, piece // 2)
    low_ring = Ring(gate_up.at[0, :, low], ring_send, ring_recv, 16, dp, dps)
    high_ring = Ring(gate_up.at[0, :, high], ring_send, ring_recv, 20, dp, dps)
    own_rows = pl.ds(pl.multiple_of(own * local_rows, local_rows), local_rows)

    def to_owner(src, dst, sends, recvs, step):
        to = lax.rem(own + step, owners)
        device = {"expert": to, "tensor": share}
        return remote(src(to), dst, sends.at[step], recvs.at[step], device)

    key_cut, query_cut = pl.ds(0, HD), pl.ds(HD, first_full.shape[2] - HD)

    def pack_copy(step):
        target = first_full.at[dp, own_rows, key_cut]
        return to_owner(pack_one.at.__getitem__, target, pack_send, pack_recv, step)

    def query_part_copy(step):
        to = lax.rem(own + step, owners)
        return remote(
            query_weight.at[to],
            first_full.at[dp, own_rows, query_cut],
            pack_send.at[2 * owners + step],
            pack_recv.at[2 * owners + step],
            {"expert": to, "tensor": share},
        )

    def second_copy(step):
        to = lax.rem(own + step, owners)
        return remote(
            pack_two.at[to],
            out_full.at[dp, own_rows],
            pack_send.at[owners + step],
            pack_recv.at[owners + step],
            {"expert": to, "tensor": share},
        )

    def token_copy(step):
        start = pl.multiple_of(core * wide, wide)
        return to_owner(
            lambda to: tokens.at[:, pl.ds(start, wide)],
            normed.at[core, own],
            token_send,
            token_recv,
            step,
        )

    def mark_copy(step):
        return to_owner(lambda to: marks, routes.at[own], mark_send, mark_recv, step)

    each(owners, lambda step: query_part_copy(step).start())
    each(owners, lambda step: pack_copy(step).start())
    each(owners, lambda step: mark_copy(step).start())

    def gain_copy(step):
        return to_owner(lambda to: own_gains, gain_parts.at[dp, own], gain_send, gain_recv, step)

    def far_gain_copy(step):
        to = lax.rem(dp + step, dps)
        place = owners + step
        return remote(
            gain_parts.at[dp],
            gain_parts.at[dp],
            gain_send.at[place],
            gain_recv.at[place],
            {"dp": to},
        )

    gain_parts[dp, own] = own_gains[...]
    each(owners, lambda step: gain_copy(step).start())
    low_ring.start(gate_weight.at[low])
    own_copies = [
        pltpu.make_async_copy(pack_one.at[own], first_full.at[dp, own_rows, key_cut], local.at[0]),
        pltpu.make_async_copy(pack_two.at[own], out_full.at[dp, own_rows], local.at[1]),
        pltpu.make_async_copy(gate_weight, gate_up.at[0, dp], local.at[2]),
        pltpu.make_async_copy(up_weight, gate_up.at[1, dp], local.at[3]),
        pltpu.make_async_copy(down_weight, down.at[dp], local.at[4]),
    ]
    for copy in own_copies:
        copy.start()
    routes[own] = marks[...]
    normed[core, own] = tokens[:, pl.ds(pl.multiple_of(core * wide, wide), wide)]

    own_query = pltpu.make_async_copy(
        query_weight.at[own], first_full.at[dp, own_rows, query_cut], local.at[8]
    )
    own_query.start()
    own_copies[0].wait()
    own_query.wait()
    each(owners, lambda step: query_part_copy(step).wait())
    each(owners, lambda step: pack_copy(step).wait())
    one_ring.start()
    high_ring.start(gate_weight.at[high])
    each(owners, lambda step: token_copy(step).start())
    each(owners, lambda step: second_copy(step).start())
    each(owners, lambda step: mark_copy(step).wait())
    each(owners, lambda step: gain_copy(step).wait())
    each(dps, lambda step: far_gain_copy(step).start())

    def picked_rows(source, out, scale):
        for index in range(2):
            cut = pl.ds(pl.multiple_of(core * wide + index * piece, piece), piece)
            taken = mm(sel_ffn[...], source[:, cut])
            if scale is not None:
                taken = taken * scale
            taken = taken.astype(BF).reshape(owners, slots, piece)
            out[:, :, index * piece : (index + 1) * piece] = taken


    def grad_copy(step):
        return to_owner(grads_out.at.__getitem__, expert_grad.at[core, own], grad_send, grad_recv, step)

    token_rows = lax.broadcasted_iota(jnp.int32, (group, group), 0)
    token_columns = lax.broadcasted_iota(jnp.int32, (group, group), 1)
    before = (token_rows < token_columns).astype(F32).astype(BF)
    token_names = token_rows.astype(F32).astype(BF)
    slot_names = lax.broadcasted_iota(jnp.int32, (slots, group), 0).astype(F32)
    first_routes = jnp.concatenate([routes[index, 0:1, :] for index in range(owners)], 0)
    second_routes = jnp.concatenate([routes[index, 1:2, :] for index in range(owners)], 0)

    def map_keys(name):
        member = (first_routes == name) | (second_routes == name)
        rank = mm(jnp.where(member, 1.0, 0.0).astype(BF), before)
        return jnp.where(member, rank, -1.0)

    for name in range(owners):
        slot_keys[name] = map_keys(float(name))

    gate_columns[...] = jnp.transpose(marks[...])
    names = lax.broadcasted_iota(jnp.int32, (owners, group), 0).astype(F32)
    member = (marks[2:3, :] == names) | (marks[3:4, :] == names)
    rank = mm(jnp.where(member, 1.0, 0.0).astype(BF), before)
    ffn_keys = jnp.where(member, rank, -1.0)
    gate_slots = []
    for name in range(owners):
        cut = slice(name * slots, (name + 1) * slots)
        key = slot_keys[name, pl.ds(own, 1), :]
        hot = jnp.where(key == slot_names, 1.0, 0.0)
        for choice in range(TOPK):
            chosen_here = jnp.where(marks[choice : choice + 1, :] == float(name), hot, 0.0)
            sel_att[cut, choice * group : (choice + 1) * group] = chosen_here.astype(BF)
        hot = jnp.where(ffn_keys[name : name + 1, :] == slot_names, 1.0, 0.0)
        sel_ffn[cut, :] = hot.astype(BF)
        gate = jnp.zeros((slots, 1), F32)
        for choice in range(TOPK):
            chosen_here = jnp.where(marks[2 + choice : 3 + choice, :] == float(name), hot, 0.0)
            pick_ffn[cut, choice * group : (choice + 1) * group] = chosen_here.astype(BF)
            weighed = chosen_here * marks[6 + choice : 7 + choice, :]
            gate = gate + jnp.sum(weighed, 1, keepdims=True)
        gate_slots.append(gate)
    picked_rows(upstream, grads_out, jnp.concatenate(gate_slots, 0))

    def one_hot(name, block):
        key = slot_keys[name, pl.ds(block, 1), :]
        return jnp.where(key == slot_names, 1.0, 0.0)

    def table(hot, array, block):
        span = pl.ds(pl.multiple_of(block * group, group), group)
        return mm(hot, array[span, :], precision=lax.Precision.HIGHEST)

    def row_block(index, carry):
        name, block = lax.div(index, columns), part * columns + lax.rem(index, columns)
        hot = one_hot(name, block)
        pos = mm(hot.astype(BF), token_names) + (block * group).astype(F32)
        start, bound = jnp.zeros_like(pos), jnp.zeros((1, group), F32)
        for document in range(lengths.shape[0]):
            bound = bound + lengths[document : document + 1, :]
            start = jnp.maximum(start, jnp.where(bound <= pos, bound, 0.0))
        span = pl.ds(pl.multiple_of(index * slots, slots), slots)
        row_info[span, 0:1] = pos[:, 0:1]
        row_info[span, 1:2] = start[:, 0:1]
        return carry

    lax.fori_loop(0, owners * columns, row_block, 0)

    each(owners, lambda step: token_copy(step).wait())
    across = remote(normed.at[core], normed.at[core], one_send.at[0], one_recv.at[0], other)
    across.start()
    each(owners, lambda step: grad_copy(step).start())
    expert_grad[core, own] = grads_out[own]
    own_copies[1].wait()
    each(owners, lambda step: second_copy(step).wait())
    one_ring.forward()
    two_ring.start()
    low_ring.forward()
    up_ring.start(up_weight)
    across.wait()

    def squares(index, carry):
        low, high = normed[0, index].astype(F32), normed[1, index].astype(F32)
        total = jnp.sum(low * low, 1, keepdims=True) + jnp.sum(high * high, 1, keepdims=True)
        inv_all[index] = lax.rsqrt(total / width + EPSILON)
        return carry

    lax.fori_loop(0, owners, squares, 0)
    inv_one[...] = inv_all[own]
    one_ring.finish()
    kept = [pltpu.make_async_copy(first_full, far_first, local.at[5])]
    kept[0].start()

    each(dps, lambda step: far_gain_copy(step).wait())
    left = lax.broadcasted_iota(jnp.int32, (8, HD), 1) < HD // 2
    for index in range(dps * owners // 2):
        name, side = index // columns, 2 * (index % columns)
        turned = pltpu.roll(gain_parts[name, side + 1], HD // 2, 1)
        joined = jnp.where(left, gain_parts[name, side], turned)
        gains[:, index * HD : (index + 1) * HD] = joined[0:2, :]

    chosen = expert_in
    def norm_block(index, carry):
        hot = one_hot(own, index)
        place[index] = hot.astype(BF)
        span = pl.ds(pl.multiple_of(index * slots, slots), slots)
        cos_slot[span, :] = table(hot, cos_key, index)
        sin_slot[span, :] = table(hot, sin_key, index)
        for side in range(2):
            cut = slice(side * wide, (side + 1) * wide)
            rounded = normed[side, index].astype(F32) * inv_all[index] * gains[0:1, cut]
            rounded = rounded.astype(BF)
            normed[side, index] = rounded
            chosen[side, index] = mm(hot.astype(BF), rounded).astype(BF)
        return carry

    lax.fori_loop(0, owners, norm_block, 0)
    kept.append(pltpu.make_async_copy(normed, far_normed, local.at[6]))
    kept[1].start()
    query = jnp.zeros((rows, columns * HD), F32)
    for index in range(dps):
        cut = slice((index % 2) * piece, (index % 2 + 1) * piece)
        taken = chosen[index // 2, :, :, cut].reshape(rows, piece)
        query = query + mm(taken, first_full[index, :, HD:])
    for column in range(columns):
        head = query[:, column * HD : (column + 1) * HD]
        head = (head * cos_slot[...] + pltpu.roll(head, HD // 2, 1) * sin_slot[...]).astype(BF)
        for side in range(2):
            heads_out[2 * column + side] = head[side * head_rows : (side + 1) * head_rows]

    def head_copy(step):
        return to_owner(heads_out.at.__getitem__, queries.at[own], head_send, head_recv, step)

    each(owners, lambda step: head_copy(step).start())
    queries[own] = heads_out[own]

    first = part == 0

    def key_block(index, carry):
        taken = jnp.zeros((group, HD), F32)
        for step in range(dps):
            cut = slice((step % 2) * piece, (step % 2 + 1) * piece)
            taken = taken + mm(normed[step // 2, index, :, cut], first_full[step, :, :HD])
        span = pl.ds(pl.multiple_of(index * group, group), group)
        turned = taken * cos_key[span, :] + pltpu.roll(taken, HD // 2, 1) * sin_key[span, :]
        pairs[part, span, :] = jnp.where(first, turned, taken).astype(BF)
        return carry

    lax.fori_loop(0, owners, key_block, 0)
    pair = {"expert": own + 1 - 2 * part, "tensor": share}
    swapped = remote(pairs.at[part], pairs.at[part], one_send.at[10], one_recv.at[10], pair)
    swapped.start()

    scale = HD ** (-0.5)
    key_pos = lax.broadcasted_iota(jnp.int32, (1, owners * group), 1).astype(F32)

    def attend(index):
        span = pl.ds(pl.multiple_of(index * head_rows, head_rows), head_rows)
        scores = mm(queries[index], pairs[0], 1, 1) * scale
        visible = (key_pos <= row_info[span, 0:1]) & (key_pos >= row_info[span, 1:2])
        scores = jnp.where(visible, scores, -1e30)
        top = jnp.max(scores, 1, keepdims=True)
        shifted = jnp.exp(scores - top)
        total = jnp.sum(shifted, 1, keepdims=True)
        row_info[span, 2:3] = top + jnp.log(total)
        probs = (shifted / total).astype(BF)
        mixed_out[index] = mm(probs, pairs[1]).astype(BF)

    def back_copy(step):
        to = lax.rem(own + owners - step, owners)
        return remote(
            mixed_out.at[to],
            mixed_in.at[own],
            back_send.at[step],
            back_recv.at[step],
            {"expert": to, "tensor": share},
        )

    def attend_other(step):
        head_copy(step).wait()
        attend(lax.rem(own + owners - step, owners))
        back_copy(step).start()

    swapped.wait()
    attend(own)
    mixed_in[own] = mixed_out[own]
    each(owners, attend_other)
    two_ring.forward()
    high_ring.forward()
    down_ring.start(down_weight)
    two_ring.finish()
    kept.append(pltpu.make_async_copy(out_full, far_out, local.at[7]))
    kept[2].start()
    each(owners, lambda step: back_copy(step).wait())
    for column in range(columns):
        for side in range(2):
            mixed[
                side * head_rows : (side + 1) * head_rows, column * HD : (column + 1) * HD
            ] = mixed_in[2 * column + side]

    def chip_start(product, base, near, sibling):
        def across(side):
            place = base + side
            return remote(far.at[side], sibling.at[side], one_send.at[place], one_recv.at[place], other)

        for side in range(2):
            far[side] = product(2 * side + 1 - core)
            across(side).start()
        for side in range(2):
            near[side] = product(2 * side + core)

        def finish():
            for side in range(2):
                across(side).wait()
                near[side] = (near[side].astype(F32) + sibling[side].astype(F32)).astype(BF)

        return finish

    def at_tokens(pick, gate, landing):
        total = jnp.zeros((group, piece), F32)
        for choice in range(TOPK):
            span = slice(choice * group, (choice + 1) * group)
            taken = mm(pick[:, span], landing[0].reshape(rows, piece), 0, 0)
            taken = taken + mm(pick[:, span], landing[1].reshape(rows, piece), 0, 0)
            total = total + gate_columns[:, gate + choice : gate + choice + 1] * taken
        return total

    def map_product(index):
        return mm(mixed[...], out_full[index], 1, 1).astype(BF).reshape(owners, slots, piece)

    chip_start(map_product, 1, near, sibling)()
    outgoing = send_home(near, landing, home_send, home_recv, own, half, core, owners)
    up_ring.forward()
    wait_home(outgoing, owners)
    slices[share] = at_tokens(sel_att, 4, landing).astype(BF)
    share_slices(slices, slice_send, slice_recv, own, share, shares)

    total = jnp.zeros((group, 1), F32)
    for index in range(shares):
        cut = slice(index * piece, (index + 1) * piece)
        value = tokens[:, cut].astype(F32) + slices[index].astype(F32)
        state[:, cut] = value
        total = total + jnp.sum(value * value, 1, keepdims=True)
    inv = lax.rsqrt(total / width + EPSILON)
    inv_two[...] = inv
    for index in range(2):
        cut = pl.ds(pl.multiple_of(core * wide + index * piece, piece), piece)
        rounded = (state[:, cut] * inv * gains[1:2, cut]).astype(BF)
        taken = mm(sel_ffn[...], rounded).astype(BF).reshape(owners, slots, piece)
        rows_out[:, :, index * piece : (index + 1) * piece] = taken

    def row_copy(step):
        return to_owner(rows_out.at.__getitem__, expert_in.at[core, own], row_send, row_recv, step)

    each(owners, lambda step: row_copy(step).start())
    expert_in[core, own] = rows_out[own]
    each(owners, lambda step: grad_copy(step).wait())
    across = remote(expert_grad.at[core], expert_grad.at[core], one_send.at[5], one_recv.at[5], other)
    across.start()
    each(owners, lambda step: row_copy(step).wait())
    across_rows = remote(expert_in.at[core], expert_in.at[core], one_send.at[6], one_recv.at[6], other)
    across_rows.start()
    across.wait()
    across_rows.wait()

    used = hidden.shape[0] // owners

    def tight(array):
        pieces = [array[index * slots : index * slots + used] for index in range(owners)]
        return jnp.concatenate(pieces, 0)

    def loose(array):
        blank = jnp.zeros((slots - used, array.shape[1]), F32)
        pieces = []
        for index in range(owners):
            pieces += [array[index * used : (index + 1) * used], blank]
        return jnp.concatenate(pieces, 0).astype(BF).reshape(owners, slots, piece)

    for index in range(dps):
        cut = slice((index % 2) * piece, (index % 2 + 1) * piece)
        for side, source in enumerate((expert_in, expert_grad)):
            taken = source[index // 2, :, :, cut].reshape(rows, piece).astype(F32)
            features[side, index] = tight(taken).astype(BF)
    def feature_copy(step):
        to = lax.rem(dp + step, dps)
        return remote(
            features.at[core, to],
            features_all.at[core, dp],
            feature_send.at[step],
            feature_recv.at[step],
            {"dp": to},
        )

    keep = pltpu.make_async_copy(features.at[core, dp], features_all.at[core, dp], feature_send.at[0])
    keep.start()
    for copy in own_copies[2:]:
        copy.wait()
    tile = 2 * HD

    def unit_tiles(body):
        def step(index, carry):
            body(pl.ds(pl.multiple_of(index * tile, tile), tile))
            return carry

        lax.fori_loop(0, units // tile, step, 0)
        if units % tile:
            body(pl.ds(units - units % tile, units % tile))

    low_ring.finish()
    high_ring.finish()

    def gate_tile(cut):
        total = mm(features[0, 0], gate_up[0, 0, :, cut])
        for index in range(1, dps):
            total = total + mm(features[0, index], gate_up[0, index, :, cut])
        act[0, :, cut] = total

    unit_tiles(gate_tile)
    down_ring.forward()
    up_ring.finish()

    def up_tile(cut):
        up = mm(features[0, 0], gate_up[1, 0, :, cut])
        for index in range(1, dps):
            up = up + mm(features[0, index], gate_up[1, index, :, cut])
        act[1, :, cut] = up
        gate = act[0, :, cut]
        hidden[:, cut] = (gate / (1.0 + jnp.exp(-gate)) * up).astype(BF)

    unit_tiles(up_tile)
    down_ring.finish()
    each(dps, lambda step: feature_copy(step).start())
    finish_sum = chip_start(lambda index: loose(mm(hidden[...], down[index])), 7, near, sibling)

    def grad_tile(cut):
        grad = mm(features[1, 0], down[0, cut, :], 1, 1)
        for index in range(1, dps):
            grad = grad + mm(features[1, index], down[index, cut, :], 1, 1)
        gate, up = act[0, :, cut], act[1, :, cut]
        sigma = 1.0 / (1.0 + jnp.exp(-gate))
        d_both[0, :, cut] = (grad * up * sigma * (1.0 + gate * (1.0 - sigma))).astype(BF)
        d_both[1, :, cut] = (grad * gate * sigma).astype(BF)

    unit_tiles(grad_tile)
    finish_sum()
    outgoing_two = send_home(
        near, landing_two, home_two_send, home_two_recv, own, half, core, owners
    )

    def input_product(index):
        total = mm(d_both[0], gate_up[0, index], 1, 1)
        return loose(total + mm(d_both[1], gate_up[1, index], 1, 1))

    finish_parts = chip_start(input_product, 11, d_parts, sibling_two)
    keep.wait()
    each(dps, lambda step: feature_copy(step).wait())
    across = remote(
        features_all.at[core], features_all.at[core], one_send.at[9], one_recv.at[9], other
    )
    across.start()
    wait_home(outgoing_two, owners)
    rest = at_tokens(pick_ffn, 6, landing_two)
    span = pl.ds(pl.multiple_of(share * piece, piece), piece)
    output_part[...] = (state[:, span] + rest).astype(BF)
    finish_parts()
    across.wait()
    for copy in kept:
        copy.wait()
    one_ring.drain()
    two_ring.drain()
    low_ring.drain(gate_weight.at[low])
    high_ring.drain(gate_weight.at[high])
    up_ring.drain(up_weight)
    down_ring.drain(down_weight)


def back_kernel(
    parts,
    sel_ffn,
    state,
    inv_two,
    upstream,
    gains,
    sel_att,
    gate_columns,
    out_full,
    queries,
    pairs,
    row_info,
    cos_slot,
    sin_slot,
    cos_key,
    sin_key,
    place,
    d_both,
    hidden,
    output_part,
    tokens,
    inv_one,
    mixed,
    far_weights,
    far_normed,
    far_features,
    output,
    input_grad,
    gain_grads,
    maps_in,
    gate_grad,
    up_grad,
    down_grad,
    d_both_all,
    hidden_all,
    d_gain_two,
    d_rows,
    d_proj,
    return_in,
    parts_joined,
    rows_out,
    heads_out,
    heads_in,
    queries_out,
    queries_in,
    pair_out,
    pair_in,
    d_keys,
    d_values,
    far,
    near,
    sibling,
    landing,
    slices,
    map_grads,
    early,
    late,
    gain_out,
    gain_in,
    gain_mid,
    gain_last,
    weights,
    normed,
    features,
    acts,
    features_turned,
    wide_tiles,
    tall_tiles,
    first_send,
    first_recv,
    return_send,
    return_recv,
    join_send,
    join_recv,
    row_send,
    row_recv,
    head_send,
    head_recv,
    back_send,
    back_recv,
    ring_send,
    ring_recv,
    local,
    one_send,
    one_recv,
    home_send,
    home_recv,
    slice_send,
    slice_recv,
    step_send,
    step_recv,
    map_send,
    map_recv,
    gain_send,
    gain_recv,
    tile_sem,
):
    own, share = lax.axis_index("expert"), lax.axis_index("tensor")
    owners, shares = heads_out.shape[0], parts_joined.shape[0]
    half, core = lax.div(share, 2), lax.rem(share, 2)
    piece, width = parts_joined.shape[2], state.shape[1]
    slots = rows_out.shape[1]
    rows = owners * slots
    wide = width // 2
    head_rows = heads_out.shape[1]
    columns = owners // 2
    other = {"expert": own, "tensor": 2 * half + 1 - core}
    dp, dps = lax.axis_index("dp"), d_both_all.shape[0]

    enter(own, half, core, owners, [lax.rem(dp + step, dps) for step in range(1, dps)])
    loads = [
        pltpu.make_async_copy(far_weights, weights, local.at[4]),
        pltpu.make_async_copy(far_normed, normed, local.at[5]),
        pltpu.make_async_copy(far_features.at[1], features, local.at[6]),
        pltpu.make_async_copy(far_features.at[0], acts.at[:, :, pl.ds(0, width // shares)], local.at[2]),
    ]
    for copy in loads:
        copy.start()

    both_ring = Ring(d_both_all, ring_send, ring_recv, 0, dp, dps)
    both_ring.start(d_both)
    hidden_ring = Ring(hidden_all, ring_send, ring_recv, 4, dp, dps)
    hidden_ring.start(hidden)

    outgoing = send_home(parts, return_in, return_send, return_recv, own, half, core, owners)
    loads[3].wait()
    for index in range(dps):
        features_turned[index] = jnp.transpose(acts[index, :, :piece].astype(F32)).astype(BF)
    wait_home(outgoing, owners)
    total = mm(sel_ffn[...], return_in[0].reshape(rows, piece), 0, 0)
    total = total + mm(sel_ffn[...], return_in[1].reshape(rows, piece), 0, 0)
    parts_joined[share] = total.astype(BF)
    share_slices(parts_joined, join_send, join_recv, own, share, shares)

    inv = inv_two[...]
    mean = jnp.zeros_like(inv)
    for index in range(shares):
        cut = slice(index * piece, (index + 1) * piece)
        grad, value = parts_joined[index].astype(F32), state[:, cut]
        mean = mean + jnp.sum(value * gains[1:2, cut] * grad, 1, keepdims=True)
        d_gain_two[:, cut] = jnp.sum(grad * value * inv, 0, keepdims=True)
    mean = mean * (inv * inv * inv / width)
    for index in range(shares):
        cut = slice(index * piece, (index + 1) * piece)
        grad = gains[1:2, cut] * parts_joined[index].astype(F32)
        input_grad[:, cut] = upstream[:, cut].astype(F32) + inv * grad - state[:, cut] * mean

    for index in range(2):
        start = pl.multiple_of(core * wide + index * piece, piece)
        grad = input_grad[:, pl.ds(start, piece)]
        both = jnp.concatenate(
            [(gate_columns[:, 4:5] * grad).astype(BF), (gate_columns[:, 5:6] * grad).astype(BF)], 0
        )
        picked = mm(sel_att[...], both).astype(BF).reshape(owners, slots, piece)
        rows_out[:, :, index * piece : (index + 1) * piece] = picked

    def row_copy(step):
        to = lax.rem(own + step, owners)
        return remote(
            rows_out.at[to],
            d_rows.at[core, own],
            row_send.at[step],
            row_recv.at[step],
            {"expert": to, "tensor": share},
        )

    each(owners, lambda step: row_copy(step).start())
    d_rows[core, own] = rows_out[own]
    each(owners, lambda step: row_copy(step).wait())
    across = remote(d_rows.at[core], d_rows.at[core], first_send.at[1], first_recv.at[1], other)
    across.start()

    def half_product(side):
        taken = d_rows[side].reshape(rows, wide)
        return mm(taken[:, :piece], out_full[2 * side]) + mm(taken[:, piece:], out_full[2 * side + 1])

    d_mixed = half_product(core)
    across.wait()
    d_mixed = (d_mixed + half_product(1 - core)).astype(BF)
    for column in range(columns):
        for part in range(2):
            heads_out[2 * column + part] = d_mixed[
                part * head_rows : (part + 1) * head_rows, column * HD : (column + 1) * HD
            ]

    def head_copy(step):
        to = lax.rem(own + step, owners)
        return remote(
            heads_out.at[to],
            heads_in.at[own],
            head_send.at[step],
            head_recv.at[step],
            {"expert": to, "tensor": share},
        )

    each(owners, lambda step: head_copy(step).start())
    heads_in[own] = heads_out[own]
    middle = columns * HD + HD
    for index in range(dps):
        cut = slice((index % 2) * piece, (index % 2 + 1) * piece)
        outs = d_rows[index // 2, :, :, cut].reshape(rows, piece)
        map_grads[index, :, middle:] = mm(outs, mixed[...], 0, 0).astype(BF)

    scale = HD ** (-0.5)
    key_pos = lax.broadcasted_iota(jnp.int32, (1, pairs.shape[1]), 1).astype(F32)
    d_keys[...] = jnp.zeros_like(d_keys)
    d_values[...] = jnp.zeros_like(d_values)

    def attend(index):
        span = pl.ds(pl.multiple_of(index * head_rows, head_rows), head_rows)
        query, key, value, grad = queries[index], pairs[0], pairs[1], heads_in[index]
        scores = mm(query, key, 1, 1) * scale
        visible = (key_pos <= row_info[span, 0:1]) & (key_pos >= row_info[span, 1:2])
        probs = jnp.where(visible, jnp.exp(scores - row_info[span, 2:3]), 0.0)
        d_probs = mm(grad, value, 1, 1)
        delta = jnp.sum(probs * d_probs, 1, keepdims=True)
        d_scores = (probs * (d_probs - delta)).astype(BF)
        queries_out[index] = (mm(d_scores, key) * scale).astype(BF)
        d_keys[...] += mm(d_scores, query, 0, 0)
        d_values[...] += mm(probs.astype(BF), grad, 0, 0)

    def query_copy(step):
        to = lax.rem(own + owners - step, owners)
        return remote(
            queries_out.at[to],
            queries_in.at[own],
            back_send.at[step],
            back_recv.at[step],
            {"expert": to, "tensor": share},
        )

    def attend_other(step):
        head_copy(step).wait()
        attend(lax.rem(own + owners - step, owners))
        query_copy(step).start()

    attend(own)
    queries_in[own] = queries_out[own]
    each(owners, attend_other)
    both_ring.forward()

    first = lax.rem(own, 2) == 0
    pair_out[...] = jnp.where(first, d_values[...], d_keys[...] * scale).astype(BF)
    pair = {"expert": own + 1 - 2 * lax.rem(own, 2), "tensor": share}
    across = remote(pair_out, pair_in, first_send.at[2], first_recv.at[2], pair)
    across.start()
    each(owners, lambda step: query_copy(step).wait())
    group = place.shape[2]
    for part in range(2):
        for index in range(columns):
            block = part * columns + index
            cut = slice(index * slots, (index + 1) * slots)
            span = slice(block * slots, (block + 1) * slots)
            turned = []
            for column in range(columns):
                grad = queries_in[2 * column + part, cut, :].astype(F32)
                back = pltpu.roll(grad, HD // 2, 1) * sin_slot[span, :]
                turned.append((grad * cos_slot[span, :] - back).astype(BF))
            picked = jnp.concatenate(turned, 1)
            d_proj[block * group : (block + 1) * group, : columns * HD] = mm(
                place[block], picked, 0, 0
            ).astype(BF)
    across.wait()
    mine = jnp.where(first, d_keys[...] * scale, d_values[...]) + pair_in[...].astype(F32)
    turned = mine * cos_key[...] + pltpu.roll(mine, HD // 2, 1) * sin_key[...]
    d_proj[:, columns * HD :] = jnp.where(first, turned, mine).astype(BF)

    group, piece = near.shape[2], near.shape[3]
    head_width = d_proj.shape[1] - HD
    local_rows = maps_in.shape[1]
    used, units = acts.shape[1], acts.shape[2]
    after, before = lax.rem(dp + 1, dps), lax.rem(dp + dps - 1, dps)
    facing = lax.rem(dp + 2, dps)
    for copy in loads[:3]:
        copy.wait()

    class load:
        def __init__(self, side):
            rows_here = pl.ds(0 if side == 2 else side * used, used)
            mine, others = (hidden, hidden_all) if side == 2 else (d_both, d_both_all)
            self.copies = [pltpu.make_async_copy(mine.at[rows_here], acts.at[dp], local.at[0])]
            for step in range(1, dps):
                index = lax.rem(dp + step, dps)
                self.copies.append(
                    pltpu.make_async_copy(
                        others.at[index, rows_here], acts.at[index], local.at[8 + step]
                    )
                )

        def start(self):
            for copy in self.copies:
                copy.start()

        def wait(self):
            for copy in self.copies:
                copy.wait()

    def map_grad(index):
        cut = pl.ds(pl.multiple_of(lax.rem(index, 2) * piece, piece), piece)
        inputs = normed[lax.div(index, 2), :, :, cut].reshape(owners * group, piece)
        return mm(inputs, d_proj[...], 0, 0)

    def keep_grad(index):
        map_grads[index, :, :middle] = map_grad(index).astype(BF)

    cut = piece // 2

    def step_copy(kind):
        to = {"dp": after if kind % 2 == 0 else before}
        sems = (step_send.at[kind], step_recv.at[kind])
        if kind < 2:
            span = pl.ds(kind * cut, cut)
            return remote(map_grads.at[facing, span], early.at[kind], *sems, to)
        return remote(map_grads.at[after if kind == 2 else before], late.at[kind - 2], *sems, to)

    keep_grad(facing)
    step_copy(0).start()
    step_copy(1).start()

    def product(index):
        queries = mm(d_proj[:, :head_width], weights[index, :, HD:], 1, 1)
        side = mm(d_proj[:, head_width:], weights[index, :, :HD], 1, 1)
        return (queries + side).reshape(owners, group, piece)

    def across(side):
        return remote(far.at[side], sibling.at[side], one_send.at[side], one_recv.at[side], other)

    for side in range(2):
        far[side] = product(2 * side + 1 - core).astype(BF)
        across(side).start()
    for side in range(2):
        near[side] = product(2 * side + core).astype(BF)
    for side in range(2):
        across(side).wait()
        near[side] = (near[side].astype(F32) + sibling[side].astype(F32)).astype(BF)
    outgoing = send_home(near, landing, home_send, home_recv, own, half, core, owners)

    keep_grad(after)
    keep_grad(before)
    step_copy(0).wait()
    step_copy(1).wait()
    top, bottom = slice(0, cut), slice(cut, 2 * cut)
    map_grads[after, top] = (map_grads[after, top].astype(F32) + early[0].astype(F32)).astype(BF)
    map_grads[before, bottom] = (
        map_grads[before, bottom].astype(F32) + early[1].astype(F32)
    ).astype(BF)
    step_copy(2).start()
    step_copy(3).start()
    hidden_ring.forward()
    both_ring.finish()
    load(0).start()
    keep_grad(dp)

    tile = 2 * HD
    whole, rest = units // tile, units % tile
    def unit_tiles(product, out, rows_first):
        def store(slot, span, size):
            if rows_first:
                return pltpu.make_async_copy(
                    tall_tiles.at[slot, pl.ds(0, size)], out.at[span], tile_sem.at[slot]
                )
            return pltpu.make_async_copy(
                wide_tiles.at[slot, :, pl.ds(0, size)], out.at[:, span], tile_sem.at[slot]
            )

        def put(slot, value, size):
            if rows_first:
                tall_tiles[slot, :size] = value.astype(BF)
            else:
                wide_tiles[slot, :, :size] = value.astype(BF)

        def pair(index, carry):
            for slot in range(2):
                span = pl.ds(pl.multiple_of((2 * index + slot) * tile, tile), tile)

                @pl.when(index > 0)
                def _(slot=slot, span=span):
                    store(slot, span, tile).wait()

                put(slot, product(span), tile)
                store(slot, span, tile).start()
            return carry

        lax.fori_loop(0, whole // 2, pair, 0)
        spans = [(0, pl.ds((whole - 2) * tile, tile), tile), (1, pl.ds((whole - 1) * tile, tile), tile)]
        for slot, span, size in spans:
            store(slot, span, size).wait()
        if whole % 2:
            span = pl.ds((whole - 1) * tile, tile)
            put(0, product(span), tile)
            store(0, span, tile).start()
        if rest:
            tail = pl.ds(whole * tile, rest)
            put(1, product(tail), rest)
            store(1, tail, rest).start()
            store(1, tail, rest).wait()
        if whole % 2:
            store(0, span, tile).wait()

    def wide_product(span):
        total = mm(features_turned[0], acts[0, :, span])
        for index in range(1, dps):
            total = total + mm(features_turned[index], acts[index, :, span])
        return total

    def tall_product(span):
        total = mm(acts[0, :, span], features[0], 0, 0)
        for index in range(1, dps):
            total = total + mm(acts[index, :, span], features[index], 0, 0)
        return total

    load(0).wait()
    unit_tiles(wide_product, gate_grad, False)
    load(1).start()

    wait_home(outgoing, owners)
    total = jnp.zeros((group, piece), F32)
    for side in range(2):
        for index in range(owners):
            total = total + landing[side, index].astype(F32)
    slices[share, 0] = total.astype(BF)
    slices[share, 1] = output_part[...]
    joining = share_start(slices, slice_send, slice_recv, own, share, shares)

    step_copy(2).wait()
    step_copy(3).wait()
    map_grads[dp] = (
        map_grads[dp].astype(F32) + late[0].astype(F32) + late[1].astype(F32)
    ).astype(BF)

    def home_rows(index):
        return pl.ds(pl.multiple_of(index * local_rows, local_rows), local_rows)

    def map_copy(step):
        to = lax.rem(own + step, owners)
        return remote(
            map_grads.at[dp, home_rows(to)],
            maps_in.at[own],
            map_send.at[step],
            map_recv.at[step],
            {"expert": to, "tensor": share},
        )

    each(owners, lambda step: map_copy(step).start())
    maps_in[own] = map_grads[dp, home_rows(own), :]

    load(1).wait()
    unit_tiles(wide_product, up_grad, False)

    each(shares, lambda step: joining(step).wait())
    inv = inv_one[...]
    mean = jnp.zeros_like(inv)
    for index in range(shares):
        span = slice(index * piece, (index + 1) * piece)
        grad, value = slices[index, 0].astype(F32), tokens[:, span].astype(F32)
        output[:, span] = slices[index, 1]
        mean = mean + jnp.sum(value * gains[0:1, span] * grad, 1, keepdims=True)
        gain_one = jnp.sum(grad * value * inv, 0, keepdims=True)
        for chunk in range(piece // HD):
            lanes = slice(chunk * HD, (chunk + 1) * HD)
            place = index * (piece // HD) + chunk
            gain_out[index, chunk, 0:1] = gain_one[:, lanes]
            gain_out[index, chunk, 1:2] = d_gain_two[:, place * HD : (place + 1) * HD]

    def gain_copy(step):
        to = lax.rem(own + step, owners)
        return remote(
            gain_out.at[:, lax.div(to, 2)],
            gain_in.at[own],
            gain_send.at[step],
            gain_recv.at[step],
            {"expert": to, "tensor": share},
        )

    def far_gain_copy(step):
        to = lax.rem(dp + step, dps)
        return remote(
            gain_mid.at[to],
            gain_last.at[dp],
            gain_send.at[owners + step],
            gain_recv.at[owners + step],
            {"dp": to},
        )

    each(owners, lambda step: gain_copy(step).start())
    gain_in[own] = gain_out[:, lax.div(own, 2)]
    mean = mean * (inv * inv * inv / width)
    for index in range(shares):
        span = slice(index * piece, (index + 1) * piece)
        grad = gains[0:1, span] * slices[index, 0].astype(F32)
        value = tokens[:, span].astype(F32)
        input_grad[:, span] = input_grad[:, span] + inv * grad - value * mean
    hidden_ring.finish()
    load(2).start()
    each(owners, lambda step: gain_copy(step).wait())
    total = gain_in[0]
    for index in range(1, owners):
        total = total + gain_in[index]
    gain_mid[...] = total
    each(dps, lambda step: far_gain_copy(step).start())
    gain_last[dp] = gain_mid[dp]
    load(2).wait()
    unit_tiles(tall_product, down_grad, True)
    each(dps, lambda step: far_gain_copy(step).wait())
    total = gain_last[0, 0:2]
    for index in range(1, dps):
        total = total + gain_last[index, 0:2]
    gain_grads[...] = total
    each(owners, lambda step: map_copy(step).wait())
    both_ring.drain(d_both)
    hidden_ring.drain(hidden)


def call_kernel(kernel, collective_id, outs, scratch, semaphores, args, far_args=(), far_outs=()):
    def specs(count, far):
        spaces = [pl.ANY if index in far else pltpu.VMEM for index in range(count)]
        return [pl.BlockSpec(memory_space=space) for space in spaces]

    return pl.pallas_call(
        kernel,
        out_shape=[jax.ShapeDtypeStruct(shape, dtype) for shape, dtype in outs],
        in_specs=specs(len(args), far_args),
        out_specs=specs(len(outs), far_outs),
        scratch_shapes=[pltpu.VMEM(shape, dtype) for shape, dtype in scratch]
        + [pltpu.SemaphoreType.DMA((count,)) for count in semaphores],
        compiler_params=pltpu.CompilerParams(
            collective_id=collective_id, has_side_effects=True, vmem_limit_bytes=60 * 2**20
        ),
    )(*args)


def per_device(
    tokens,
    cotangent,
    doc_lengths,
    att_routes,
    att_gates,
    ffn_routes,
    ffn_gates,
    kv_weight,
    query_weight,
    out_weight,
    attn_gain,
    ffn_gain,
    gate_weight,
    up_weight,
    down_weight,
):
    _, group, width = tokens.shape
    owners = lax.axis_size("expert")
    shares = lax.axis_size("tensor")
    dps = lax.axis_size("dp")
    own = lax.axis_index("expert")
    share = lax.axis_index("tensor")
    columns = owners // 2
    column_half = own % 2
    att_cap = -(-min(group, group * TOPK * 5 // (4 * ATT_EXP)) // 16) * 16
    ffn_cap = -(-min(group, group * TOPK * 5 // (4 * owners)) // 16) * 16
    rows = owners * att_cap
    seq_len = owners * group
    piece = width // shares
    local = kv_weight.shape[0]
    head_width = kv_weight.shape[2]

    kv_parts = jnp.transpose(kv_weight.reshape(local, 2, columns, HD), (2, 1, 0, 3))
    pack_one = kv_parts.reshape(owners, local, HD)
    own_gains = jnp.stack([attn_gain, ffn_gain]).astype(F32)
    own_gains = jnp.pad(own_gains, ((0, 8 - 2), (0, HD - local)))
    pack_two = jnp.swapaxes(out_weight, 1, 2)
    marks = jnp.concatenate(
        [
            att_routes[0].T.astype(F32),
            ffn_routes[0].T.astype(F32),
            att_gates[0].T,
            ffn_gates[0].T,
        ],
        0,
    )
    lengths = jnp.broadcast_to(doc_lengths[0].astype(F32)[:, None], (doc_lengths.shape[1], HD))
    angles = np.arange(seq_len)[:, None] * 10000.0 ** (-np.arange(HD // 2) * 2.0 / HD)
    cos_key = jnp.asarray(np.concatenate([np.cos(angles)] * 2, 1), F32)
    sin_key = jnp.asarray(np.concatenate([-np.sin(angles), np.sin(angles)], 1), F32)
    used = min(group, group * TOPK * 5 // (4 * owners))
    units = gate_weight.shape[2]
    slots = att_cap
    head_rows = columns * slots
    block = (2, owners, slots, piece)
    (
        first_full,
        out_full,
        normed,
        gains,
        inv_one,
        queries,
        pairs,
        row_info,
        cos_slot,
        sin_slot,
        place,
        mixed,
        state,
        inv_two,
        features_all,
        hidden,
        d_both,
        d_parts,
        output_part,
        sel_ffn,
        sel_att,
        gate_columns,
    ) = call_kernel(
        first_kernel,
        3,
        [
            ((dps, owners * local, HD + head_width), BF),
            ((dps, owners * local, head_width), BF),
            ((2, owners, group, width // 2), BF),
            ((2, width), F32),
            ((group, 1), F32),
            ((owners, head_rows, HD), BF),
            ((2, seq_len, HD), BF),
            ((owners * head_rows, HD), F32),
            ((rows, HD), F32),
            ((rows, HD), F32),
            ((owners, slots, group), BF),
            ((rows, head_width), BF),
            ((group, width), F32),
            ((group, 1), F32),
            ((2, dps, owners * used, piece), BF),
            ((owners * used, units), BF),
            ((2, owners * used, units), BF),
            (block, BF),
            ((group, piece), BF),
            ((rows, group), BF),
            ((rows, TOPK * group), BF),
            ((group, 8), F32),
        ],
        [
            ((dps, owners * local, HD + head_width), BF),
            ((dps, owners * local, head_width), BF),
            ((2, owners, group, width // 2), BF),
            ((rows, TOPK * group), BF),
            ((2, dps, owners * used, piece), BF),
            ((2, owners, slots, width // 2), BF),
            ((2, owners, slots, width // 2), BF),
            ((owners, 8, group), F32),
            ((dps, owners, 8, HD), F32),
            ((owners, owners, group), F32),
            ((owners, group, 1), F32),
            ((owners, head_rows, HD), BF),
            ((owners, head_rows, HD), BF),
            ((owners, head_rows, HD), BF),
        ]
        + [(block, BF)] * 6
        + [
            ((shares, group, piece), BF),
            ((owners, slots, width // 2), BF),
            ((owners, slots, width // 2), BF),
            ((2, dps, width // dps, units), BF),
            ((dps, units, piece), BF),
            ((2, owners * used, units), F32),
        ],
        [24, 24, 9, 3 * owners, 3 * owners]
        + [owners] * 4
        + [13, 13]
        + [owners] * 4
        + [2 * owners] * 4
        + [shares, shares]
        + [owners] * 4
        + [dps, dps]
        + [owners + dps] * 2,
        [
            tokens[0],
            marks,
            own_gains,
            pack_one,
            query_weight,
            pack_two,
            gate_weight[0],
            up_weight[0],
            down_weight[0],
            cotangent[0],
            lengths,
            cos_key,
            sin_key,
        ],
        far_args=(3, 4, 5, 6, 7, 8),
        far_outs=(0, 1, 2, 14),
    )

    grad_width = head_width + HD + head_width
    (
        output,
        input_grad,
        gain_grads,
        map_grads,
        gate_grad,
        up_grad,
        down_grad,
        *_,
    ) = call_kernel(
        back_kernel,
        1,
        [
            ((group, width), BF),
            ((group, width), F32),
            ((2, HD), F32),
            ((owners, local, grad_width), BF),
            ((piece, units), BF),
            ((piece, units), BF),
            ((units, piece), BF),
            ((dps, 2 * owners * used, units), BF),
            ((dps, owners * used, units), BF),
        ],
        [
            ((1, width), F32),
            ((2, owners, slots, width // 2), BF),
            ((seq_len, head_width + HD), BF),
            (block, BF),
            ((shares, group, piece), BF),
            ((owners, slots, width // 2), BF),
            ((owners, head_rows, HD), BF),
            ((owners, head_rows, HD), BF),
            ((owners, head_rows, HD), BF),
            ((owners, head_rows, HD), BF),
            ((seq_len, HD), BF),
            ((seq_len, HD), BF),
            ((seq_len, HD), F32),
            ((seq_len, HD), F32),
            ((2, owners, group, piece), BF),
            ((2, owners, group, piece), BF),
            ((2, owners, group, piece), BF),
            ((2, owners, group, piece), BF),
            ((shares, 2, group, piece), BF),
            ((dps, piece, grad_width), BF),
            ((2, piece // 2, grad_width), BF),
            ((2, piece, grad_width), BF),
            ((dps, owners // 2, 8, HD), F32),
            ((owners, dps, 8, HD), F32),
            ((dps, 8, HD), F32),
            ((dps, 8, HD), F32),
            ((dps, owners * local, HD + head_width), BF),
            ((2, owners, group, width // 2), BF),
            ((dps, owners * used, piece), BF),
            ((dps, owners * used, units), BF),
            ((dps, piece, owners * used), BF),
            ((2, piece, 2 * HD), BF),
            ((2, 2 * HD, piece), BF),
        ],
        [
            3,
            3,
            2 * owners,
            2 * owners,
            shares,
            shares,
            owners,
            owners,
            owners,
            owners,
            owners,
            owners,
            8,
            8,
            12,
            2,
            2,
            2 * owners,
            2 * owners,
            shares,
            shares,
            4,
            4,
            owners,
            owners,
            owners + dps,
            owners + dps,
            2,
        ],
        [
            d_parts,
            sel_ffn,
            state,
            inv_two,
            cotangent[0],
            gains,
            sel_att,
            gate_columns,
            out_full,
            queries,
            pairs,
            row_info,
            cos_slot,
            sin_slot,
            cos_key,
            -sin_key,
            place,
            d_both.reshape(2 * owners * used, units),
            hidden,
            output_part,
            tokens[0],
            inv_one,
            mixed,
            first_full,
            normed,
            features_all,
        ],
        far_args=(17, 18, 23, 24, 25),
        far_outs=(4, 5, 6, 7, 8),
    )
    chunk = HD // local
    place = lax.rem(own, chunk) * local
    gain_grads = lax.dynamic_slice_in_dim(gain_grads, place, local, 1)
    query_grad = map_grads[:, :, :head_width].astype(F32)
    out_grad = jnp.swapaxes(map_grads[:, :, head_width + HD :].astype(F32), 1, 2)
    kv_grad = map_grads[:, :, head_width : head_width + HD].reshape(columns, 2, local, HD)
    kv_grad = jnp.transpose(kv_grad, (2, 1, 0, 3)).reshape(local, 2, head_width).astype(F32)
    return (
        output[None],
        input_grad[None],
        kv_grad,
        query_grad,
        out_grad,
        gain_grads[0],
        gain_grads[1],
        gate_grad[None].astype(F32),
        up_grad[None].astype(F32),
        down_grad[None].astype(F32),
    )


def solution(mesh):
    in_specs = (
        P("dp", "expert", None),
        P("dp", "expert", None),
        P("dp", None),
        P("dp", "expert", None),
        P("dp", "expert", None),
        P("dp", "expert", None),
        P("dp", "expert", None),
        P(("dp", "expert"), None, "tensor"),
        P(None, ("dp", "expert"), "tensor"),
        P(None, "tensor", ("dp", "expert")),
        P(("dp", "expert")),
        P(("dp", "expert")),
        P("expert", "dp", "tensor"),
        P("expert", "dp", "tensor"),
        P("expert", "tensor", "dp"),
    )
    out_specs = (
        P("dp", "expert", None),
        P("dp", "expert", None),
        P(("dp", "expert"), None, "tensor"),
        P(None, ("dp", "expert"), "tensor"),
        P(None, "tensor", ("dp", "expert")),
        P(("dp", "expert")),
        P(("dp", "expert")),
        P("expert", "dp", "tensor"),
        P("expert", "dp", "tensor"),
        P("expert", "tensor", "dp"),
    )
    return jax.shard_map(
        per_device, mesh=mesh, in_specs=in_specs, out_specs=out_specs, check_vma=False
    )
```
